32 devices in a mesh: dp: 16 (over z, y, x), tensor: 2 (over core).
Axes of the slice: x: 2, y: 2, z: 4, core: 2. Of those that a mesh axis runs over, the one named last changes fastest.
Arguments:
- states: bfloat16 [71680, 512], P(('dp', 'tensor')), may hold values from -6 to 6
- cotangent: bfloat16 [71680, 512], P(('dp', 'tensor')), may hold values from -6 to 6
- lengths: int32 [448], P('dp'), may hold values from 100 to 160, as said below
- span_starts: int32 [448], P('dp'), may hold values from 0 to 80, as said below
- span_ends: int32 [448], P('dp'), may hold values from 1 to 160, as said below
- query_weight: bfloat16 [512, 512], P(None, 'tensor'), may hold values from -0.375 to 0.375
- query_bias: bfloat16 [512], P('tensor'), may hold values from -3 to 3
- key_weight: bfloat16 [512, 512], P(None, 'tensor'), may hold values from -0.375 to 0.375
- value_weight: bfloat16 [512, 512], P(None, 'tensor'), may hold values from -0.25 to 0.25
- value_bias: bfloat16 [512], P('tensor'), may hold values from -3 to 3
- output_weight: bfloat16 [512, 512], P('tensor'), may hold values from -1 to 1
- output_bias: bfloat16 [512], replicated, may hold values from -3 to 3
- first_gain: bfloat16 [512], replicated, may hold values from 0.25 to 1.75
- first_shift: bfloat16 [512], replicated, may hold values from -3 to 3
- inner_weight: bfloat16 [512, 2048], P(None, 'tensor'), may hold values from -0.25 to 0.25
- inner_bias: bfloat16 [2048], P('tensor'), may hold values from -3 to 3
- down_weight: bfloat16 [2048, 512], P('tensor'), may hold values from -0.125 to 0.125
- down_bias: bfloat16 [512], replicated, may hold values from -3 to 3
- second_gain: bfloat16 [512], replicated, may hold values from 0.25 to 1.75
- second_shift: bfloat16 [512], replicated, may hold values from -3 to 3
Outputs:
- layer_out: bfloat16 [71680, 512], P(('dp', 'tensor'))
- input_grad: float32 [71680, 512], P(('dp', 'tensor'))
- query_weight_grad: float32 [512, 512], P(None, 'tensor')
- query_bias_grad: float32 [512], P('tensor')
- key_weight_grad: float32 [512, 512], P(None, 'tensor')
- value_weight_grad: float32 [512, 512], P(None, 'tensor')
- value_bias_grad: float32 [512], P('tensor')
- output_weight_grad: float32 [512, 512], P('tensor')
- output_bias_grad: float32 [512], replicated
- first_gain_grad: float32 [512], replicated
- first_shift_grad: float32 [512], replicated
- inner_weight_grad: float32 [512, 2048], P(None, 'tensor')
- inner_bias_grad: float32 [2048], P('tensor')
- down_weight_grad: float32 [2048, 512], P('tensor')
- down_bias_grad: float32 [512], replicated
- second_gain_grad: float32 [512], replicated
- second_shift_grad: float32 [512], replicated
The draws below stay inside these ranges and needn't reach their ends.
Inputs may be any that keep to these rules, and one draw needn't show every extreme that they name: `lengths`: in every aligned block of 28 chains one chain has all 160 positions. `span_starts`: at most half of the chain's length; 0 for the full chain of each block. `span_ends`: after the span's start and within the chain's length; the full chain of each block is masked whole.
All inputs are finite; a program needn't handle non-finite values.
Results may differ from the reference program's by a relative error of at most 0.02.
Values may be sent and summed in bfloat16 or wider, within the bound.
A program may use at most 256 MiB of HBM per device.

```python
import jax
import jax.numpy as jnp
from jax import lax

D = 512
HEADS = 8
HEAD_DIM = 64
FF = 2048
SEQ = 160
CH_DEV = 28
CHAINS = 448
TOKENS = 71680
N_DP = 16


def chain_spans(key):
    first, second, third, fourth = jax.random.split(key, 4)
    chain_lengths = jax.random.randint(first, (CHAINS,), SEQ * 5 // 8, SEQ + 1)
    chosen = jax.random.randint(second, (CHAINS // CH_DEV,), 0, CH_DEV)
    index = jnp.arange(CHAINS, dtype=jnp.int32)
    forced = index % CH_DEV == jnp.repeat(chosen, CH_DEV)
    chain_lengths = jnp.where(forced, SEQ, chain_lengths)
    starts = jax.random.randint(third, (CHAINS,), 0, chain_lengths // 2 + 1)
    power = jax.random.randint(fourth, (CHAINS,), 0, 7)
    width = jnp.maximum(1, SEQ * jnp.left_shift(jnp.ones_like(power), power) // 128)
    ends = jnp.minimum(starts + width, chain_lengths)
    starts = jnp.where(forced, 0, starts)
    ends = jnp.where(forced, SEQ, ends)
    return (chain_lengths.astype(jnp.int32), starts.astype(jnp.int32), ends.astype(jnp.int32))


def draw_lengths(key, part):
    chain_lengths, starts, ends = chain_spans(key)
    return chain_lengths


def draw_span_starts(key, part):
    chain_lengths, starts, ends = chain_spans(key)
    return starts


def draw_span_ends(key, part):
    chain_lengths, starts, ends = chain_spans(key)
    return ends


def block_levels(key, extent, shards, least, high):
    factor_of, own = 1.0, jax.random.fold_in(key, 6)
    for dim, blocks in shards:
        heights = jnp.exp(jax.random.uniform(jax.random.fold_in(own, dim), (blocks,), jnp.float32, least / len(shards), high / len(shards)))
        factor_of = factor_of * jnp.repeat(heights, extent[dim] // blocks).reshape([-1 if axis == dim else 1 for axis in range(len(extent))])
    return factor_of


def gaussian(rng, dims, scale, bound, shards=(), kind=jnp.bfloat16):
    drawn = scale * jax.random.normal(rng, dims, jnp.float32)
    if shards:
        drawn = drawn * block_levels(rng, dims, shards, -0.22, 0.18)
    return jnp.clip(drawn, -bound, bound).astype(kind)


def setup_inputs(seed: int = 0) -> dict:
    arg_keys = jax.random.split(jax.random.key(seed), 21)
    return {
        "states": gaussian(arg_keys[0], (TOKENS, D), 1.0, 6.0, ((0, 32),)),
        "cotangent": gaussian(arg_keys[1], (TOKENS, D), 1.0, 6.0, ((0, 32),)),
        "lengths": draw_lengths(jax.random.fold_in(arg_keys[20], 71), 0),
        "span_starts": draw_span_starts(jax.random.fold_in(arg_keys[20], 71), 0),
        "span_ends": draw_span_ends(jax.random.fold_in(arg_keys[20], 71), 0),
        "query_weight": gaussian(arg_keys[5], (D, D), (D // 2) ** -0.5, 0.375, ((1, 2),)),
        "query_bias": gaussian(arg_keys[6], (D,), 0.3, 3.0, ((0, 2),)),
        "key_weight": gaussian(arg_keys[7], (D, D), (D // 2) ** -0.5, 0.375, ((1, 2),)),
        "value_weight": gaussian(arg_keys[8], (D, D), D ** -0.5, 0.25, ((1, 2),)),
        "value_bias": gaussian(arg_keys[9], (D,), 0.3, 3.0, ((0, 2),)),
        "output_weight": gaussian(arg_keys[10], (D, D), (D // 16) ** -0.5, 1.0, ((0, 2),)),
        "output_bias": gaussian(arg_keys[11], (D,), 0.3, 3.0),
        "first_gain": jnp.clip(1.0 + 0.15 * jax.random.normal(arg_keys[12], (D,), jnp.float32), 0.25, 1.75).astype(jnp.bfloat16),
        "first_shift": gaussian(arg_keys[13], (D,), 0.3, 3.0),
        "inner_weight": gaussian(arg_keys[14], (D, FF), D ** -0.5, 0.25, ((1, 2),)),
        "inner_bias": gaussian(arg_keys[15], (FF,), 0.3, 3.0, ((0, 2),)),
        "down_weight": gaussian(arg_keys[16], (FF, D), FF ** -0.5, 0.125, ((0, 2),)),
        "down_bias": gaussian(arg_keys[17], (D,), 0.3, 3.0),
        "second_gain": jnp.clip(1.0 + 0.15 * jax.random.normal(arg_keys[18], (D,), jnp.float32), 0.25, 1.75).astype(jnp.bfloat16),
        "second_shift": gaussian(arg_keys[19], (D,), 0.3, 3.0),
    }


@jax.custom_vjp
def low(v):
    return lax.optimization_barrier(v.astype(jnp.bfloat16)).astype(jnp.float32)

@jax.custom_vjp
def low_back(v):
    return v

def low_keep(v):
    return (low(v), None)

def low_pass(kept, grad):
    return (grad,)

def back_keep(v):
    return (v, None)

def back_low(kept, grad):
    return (low(grad),)
low.defvjp(low_keep, low_pass)
low_back.defvjp(back_keep, back_low)
EPSILON = 1e-12

def highest(left, right):
    return jnp.dot(left, right, precision=lax.Precision.HIGHEST, preferred_element_type=jnp.float32)

def layer_norm(values, gain, shift):
    center = values - lax.optimization_barrier(jnp.mean(values, axis=-1, keepdims=True))
    spread = lax.optimization_barrier(jnp.mean(center * center, axis=-1, keepdims=True))
    return center * lax.rsqrt(spread + EPSILON) * gain + shift

def forward(inputs, params, key_live):
    query_weight, query_bias, key_weight, value_weight, value_bias, output_weight, output_bias, first_gain, first_shift, inner_weight, inner_bias, down_weight, down_bias, second_gain, second_shift = params
    layout = (CH_DEV, SEQ, HEADS, HEAD_DIM)
    queries = low(low_back(highest(inputs, query_weight) + query_bias)).reshape(layout)
    keys = low(low_back(highest(inputs, key_weight))).reshape(layout)
    values = low(low_back(highest(inputs, value_weight) + value_bias)).reshape(layout)
    scores = jnp.einsum('cqhd,ckhd->chqk', queries, keys, precision=lax.Precision.HIGHEST) * HEAD_DIM ** (-0.5)
    scores = low_back(scores)
    scores = jnp.where(key_live[:, None, None, :], scores, -1000000000.0)
    probs = jax.nn.softmax(scores, axis=-1)
    context = jnp.einsum('chqk,ckhd->cqhd', low(probs), values, precision=lax.Precision.HIGHEST)
    context = low(low_back(context.reshape(CH_DEV * SEQ, D)))
    attended = low_back(highest(context, output_weight) + output_bias)
    normed = layer_norm(inputs + attended, first_gain, first_shift)
    hidden = low_back(highest(low(normed), inner_weight) + inner_bias)
    branch = low_back(highest(low(jax.nn.gelu(hidden, approximate=False)), down_weight) + down_bias)
    return layer_norm(normed + branch, second_gain, second_shift)

def reference(states, cotangent, lengths, span_starts, span_ends, query_weight, query_bias, key_weight, value_weight, value_bias, output_weight, output_bias, first_gain, first_shift, inner_weight, inner_bias, down_weight, down_bias, second_gain, second_shift):
    params = tuple((item.astype(jnp.float32) for item in (query_weight, query_bias, key_weight, value_weight, value_bias, output_weight, output_bias, first_gain, first_shift, inner_weight, inner_bias, down_weight, down_bias, second_gain, second_shift)))
    group_rows = CH_DEV * SEQ
    inputs = states.astype(jnp.float32).reshape(N_DP, group_rows, D)
    cotangents = cotangent.astype(jnp.float32).reshape(N_DP, group_rows, D)
    chain_lengths = lengths.reshape(N_DP, CH_DEV)
    chain_starts = span_starts.reshape(N_DP, CH_DEV)
    chain_ends = span_ends.reshape(N_DP, CH_DEV)

    def group(totals, item):
        rows, upstream, length_row, start_row, end_row = item
        position = jnp.arange(SEQ, dtype=jnp.int32)[None, :]
        key_live = position < length_row[:, None]
        live = (position >= start_row[:, None]) & (position < end_row[:, None]) & key_live
        upstream = upstream * live.reshape(group_rows, 1).astype(jnp.float32)
        output, pullback = jax.vjp(lambda left, right: forward(left, right, key_live), rows, params)
        rows_grad, param_grads = pullback(upstream)
        totals = tuple((total + grad for total, grad in zip(totals, param_grads)))
        return (totals, (output.astype(jnp.bfloat16), rows_grad))
    zeros = tuple((jnp.zeros_like(item) for item in params))
    sums, (outputs, grads) = lax.scan(group, zeros, (inputs, cotangents, chain_lengths, chain_starts, chain_ends))
    return (outputs.reshape(TOKENS, D), grads.reshape(TOKENS, D), sums[0], sums[1], sums[2], sums[3], sums[4], sums[5], sums[6], sums[7], sums[8], sums[9], sums[10], sums[11], sums[12], sums[13], sums[14])
```

```python
import functools

import jax
import jax.numpy as jnp
from jax import lax
from jax.experimental import pallas as pl
from jax.experimental.pallas import tpu as pltpu
from jax.sharding import PartitionSpec as P

MESH = pl.DeviceIdType.MESH
f32, bf16 = jnp.float32, jnp.bfloat16
HEAD_DIM = 64
SEQ = 160
ROWS = 3072
EPSILON = 1e-12


def product(left, right):
    return jnp.dot(left, right, preferred_element_type=jnp.float32)


def product_left(left, right):
    return lax.dot_general(
        left, right, (((0,), (0,)), ((), ())), preferred_element_type=jnp.float32
    )


def product_right(left, right):
    return lax.dot_general(
        left, right, (((1,), (1,)), ((), ())), preferred_element_type=jnp.float32
    )


def layer_norm(values, gain, shift):
    center = values - jnp.mean(values, axis=-1, keepdims=True)
    spread = jnp.mean(center * center, axis=-1, keepdims=True)
    return center * lax.rsqrt(spread + EPSILON) * gain + shift


def exact_gelu(values):
    return jax.nn.gelu(values, approximate=False)


def attention_scores(queries, keys, key_live):
    scores = jnp.einsum(
        "cqhd,ckhd->chqk", queries, keys, preferred_element_type=jnp.float32
    ) * HEAD_DIM ** (-0.5)
    return jnp.where(key_live[:, None, None, :], scores, -1000000000.0)


def per_row(table, picker):
    return jnp.sum(jnp.where(picker, table[None, :], 0), axis=1)


def column_sum(values):
    return jnp.sum(values.astype(jnp.float32), axis=0)


def general(
    states,
    cotangent,
    lengths,
    span_starts,
    span_ends,
    query_weight,
    query_bias,
    key_weight,
    value_weight,
    value_bias,
    output_weight,
    output_bias,
    first_gain,
    first_shift,
    inner_weight,
    inner_bias,
    down_weight,
    down_bias,
    second_gain,
    second_shift,
):
    slice_rows = states.shape[0]
    chains = lengths.shape[0]
    group_rows = chains * SEQ
    heads_local = query_weight.shape[1] // HEAD_DIM
    layout = (chains, SEQ, heads_local, HEAD_DIM)
    whole = lax.all_gather(states, "tensor", axis=0, tiled=True)
    queries = (product(whole, query_weight) + query_bias).astype(jnp.bfloat16).reshape(layout)
    keys_low = product(whole, key_weight).astype(jnp.bfloat16).reshape(layout)
    values_low = (product(whole, value_weight) + value_bias).astype(jnp.bfloat16).reshape(layout)
    key_live = jnp.arange(SEQ, dtype=jnp.int32)[None, :] < lengths[:, None]
    scores = attention_scores(queries, keys_low, key_live)
    highest = jnp.max(scores, axis=-1, keepdims=True)
    logsum = highest + jnp.log(jnp.sum(jnp.exp(scores - highest), axis=-1, keepdims=True))
    probs_low = jnp.exp(scores - logsum).astype(jnp.bfloat16)
    context = jnp.einsum(
        "chqk,ckhd->cqhd", probs_low, values_low, preferred_element_type=jnp.float32
    )
    context = context.reshape(group_rows, heads_local * HEAD_DIM).astype(jnp.bfloat16)
    attended = lax.psum_scatter(
        product(context, output_weight), "tensor", scatter_dimension=0, tiled=True
    ) + output_bias.astype(jnp.float32)
    first_sum = states.astype(jnp.float32) + attended
    normed, first_pull = jax.vjp(
        layer_norm, first_sum, first_gain.astype(jnp.float32), first_shift.astype(jnp.float32)
    )
    normed_low = normed.astype(jnp.bfloat16)
    normed_all = lax.all_gather(normed_low, "tensor", axis=0, tiled=True)
    hidden = product(normed_all, inner_weight) + inner_bias.astype(jnp.float32)
    activation, gelu_pull = jax.vjp(exact_gelu, hidden)
    activation_low = activation.astype(jnp.bfloat16)
    branch = lax.psum_scatter(
        product(activation_low, down_weight), "tensor", scatter_dimension=0, tiled=True
    )
    second_sum = normed + (branch + down_bias.astype(jnp.float32))
    output, second_pull = jax.vjp(
        layer_norm, second_sum, second_gain.astype(jnp.float32), second_shift.astype(jnp.float32)
    )
    row_ids = lax.axis_index("tensor") * slice_rows + jnp.arange(slice_rows, dtype=jnp.int32)
    chain_ids = row_ids // SEQ
    position = row_ids % SEQ
    picker = chain_ids[:, None] == jnp.arange(chains, dtype=jnp.int32)[None, :]
    live = (
        (position >= per_row(span_starts, picker))
        & (position < per_row(span_ends, picker))
        & (position < per_row(lengths, picker))
    )
    grad_out = jnp.where(live[:, None], cotangent.astype(jnp.float32), 0.0)
    grad_second, second_gain_part, second_shift_part = second_pull(grad_out)
    grad_branch = grad_second.astype(jnp.bfloat16)
    down_bias_part = column_sum(grad_branch)
    grad_branch_all = lax.all_gather(grad_branch, "tensor", axis=0, tiled=True)
    down_weight_part = product_left(activation_low, grad_branch_all)
    grad_activation = product_right(grad_branch_all, down_weight)
    (grad_hidden,) = gelu_pull(grad_activation)
    grad_hidden_low = grad_hidden.astype(jnp.bfloat16)
    inner_weight_part = product_left(normed_all, grad_hidden_low)
    inner_bias_part = column_sum(grad_hidden_low)
    grad_normed = lax.psum_scatter(
        product_right(grad_hidden_low, inner_weight), "tensor", scatter_dimension=0, tiled=True
    )
    grad_first, first_gain_part, first_shift_part = first_pull(grad_second + grad_normed)
    grad_attended = grad_first.astype(jnp.bfloat16)
    output_bias_part = column_sum(grad_attended)
    grad_attended_all = lax.all_gather(grad_attended, "tensor", axis=0, tiled=True)
    output_weight_part = product_left(context, grad_attended_all)
    grad_context = (
        product_right(grad_attended_all, output_weight).astype(jnp.bfloat16).reshape(layout)
    )
    probs = jnp.exp(attention_scores(queries, keys_low, key_live) - logsum)
    grad_probs = jnp.einsum(
        "cqhd,ckhd->chqk", grad_context, values_low, preferred_element_type=jnp.float32
    )
    grad_scores = probs * (grad_probs - jnp.sum(probs * grad_probs, axis=-1, keepdims=True))
    grad_scores_low = grad_scores.astype(jnp.bfloat16)
    scale = HEAD_DIM ** (-0.5)
    grad_queries = (
        jnp.einsum("chqk,ckhd->cqhd", grad_scores_low, keys_low, preferred_element_type=jnp.float32)
        * scale
    )
    grad_keys = (
        jnp.einsum("chqk,cqhd->ckhd", grad_scores_low, queries, preferred_element_type=jnp.float32)
        * scale
    )
    grad_values = jnp.einsum(
        "chqk,cqhd->ckhd", probs_low, grad_context, preferred_element_type=jnp.float32
    )
    flat = (group_rows, heads_local * HEAD_DIM)
    grad_queries = grad_queries.reshape(flat).astype(jnp.bfloat16)
    grad_keys = grad_keys.reshape(flat).astype(jnp.bfloat16)
    grad_values = grad_values.reshape(flat).astype(jnp.bfloat16)
    query_weight_part = product_left(whole, grad_queries)
    key_weight_part = product_left(whole, grad_keys)
    value_weight_part = product_left(whole, grad_values)
    query_bias_part = column_sum(grad_queries)
    value_bias_part = column_sum(grad_values)
    grad_whole = (
        product_right(grad_queries, query_weight)
        + product_right(grad_keys, key_weight)
        + product_right(grad_values, value_weight)
    )
    input_grad = (
        lax.psum_scatter(
            grad_whole.astype(jnp.bfloat16), "tensor", scatter_dimension=0, tiled=True
        ).astype(jnp.float32)
        + grad_first
    )
    (
        query_weight_grad,
        query_bias_grad,
        key_weight_grad,
        value_weight_grad,
        value_bias_grad,
        output_weight_grad,
        inner_weight_grad,
        inner_bias_grad,
        down_weight_grad,
    ) = (
        lax.psum(query_weight_part.astype(jnp.bfloat16), "dp").astype(jnp.float32),
        lax.psum(query_bias_part.astype(jnp.bfloat16), "dp").astype(jnp.float32),
        lax.psum(key_weight_part.astype(jnp.bfloat16), "dp").astype(jnp.float32),
        lax.psum(value_weight_part.astype(jnp.bfloat16), "dp").astype(jnp.float32),
        lax.psum(value_bias_part.astype(jnp.bfloat16), "dp").astype(jnp.float32),
        lax.psum(output_weight_part.astype(jnp.bfloat16), "dp").astype(jnp.float32),
        lax.psum(inner_weight_part.astype(jnp.bfloat16), "dp").astype(jnp.float32),
        lax.psum(inner_bias_part.astype(jnp.bfloat16), "dp").astype(jnp.float32),
        lax.psum(down_weight_part.astype(jnp.bfloat16), "dp").astype(jnp.float32),
    )
    (
        output_bias_grad,
        first_gain_grad,
        first_shift_grad,
        down_bias_grad,
        second_gain_grad,
        second_shift_grad,
    ) = lax.psum(
        (
            output_bias_part,
            first_gain_part,
            first_shift_part,
            down_bias_part,
            second_gain_part,
            second_shift_part,
        ),
        ("dp", "tensor"),
    )
    return (
        output.astype(jnp.bfloat16),
        input_grad,
        query_weight_grad,
        query_bias_grad,
        key_weight_grad,
        value_weight_grad,
        value_bias_grad,
        output_weight_grad,
        output_bias_grad,
        first_gain_grad,
        first_shift_grad,
        inner_weight_grad,
        inner_bias_grad,
        down_weight_grad,
        down_bias_grad,
        second_gain_grad,
        second_shift_grad,
    )


class Comm:
    NSTAGE = 10
    def __init__(self, K, g, small, out, sout, bufs, stride=1):
        self.stride = stride
        self.K = K; self.CH = ROWS // K; self.SB = self.CH // 3
        self.g, self.small, self.out, self.sout = g, small, out, sout
        (self.core_buf, self.acc, self.r1, self.r2, self.r3, self.r4, self.sm, self.csem, self.rsem, self.asem, self.smsem) = bufs
        dp = lax.axis_index("dp"); t = lax.axis_index("tensor")
        self.t = t
        x = lax.rem(dp, 2); y = lax.rem(dp // 2, 2); p = lax.rem(dp // 4, 2); q = dp // 8
        self.bits = (x, y, p, q)
        self.parts = tuple(dp + w * (1 - 2 * b) for w, b in ((1, x), (2, y), (4, p), (8, q)))
        self.dp = dp
    def barrier(self):
        b = pltpu.get_barrier_semaphore()
        pl.semaphore_signal(b, inc=1, device_id=(self.dp, 1 - self.t), device_id_type=MESH)
        for n in self.parts:
            pl.semaphore_signal(b, inc=1, device_id=(n, self.t), device_id_type=MESH)
        pl.semaphore_wait(b, 5)
    def rc(self, src, dst, s, r, n):
        return pltpu.make_async_remote_copy(src_ref=src, dst_ref=dst, send_sem=s, recv_sem=r, device_id=(n, self.t), device_id_type=MESH)
    def core_copy(self, k):
        return pltpu.make_async_remote_copy(src_ref=self.g.at[1 - self.t, pl.ds(k * self.CH, self.CH)], dst_ref=self.core_buf.at[k],
            send_sem=self.csem.at[0, k], recv_sem=self.csem.at[1, k], device_id=(self.dp, 1 - self.t), device_id_type=MESH)
    def order(self, k, r):
        B, N = self.bits, self.parts
        X, Y, Pp, Qq = ((B[i], N[i]) for i in range(4))
        if r == 0: return X, Y, Pp, Qq
        if r == 1: return Y, X, Pp, Qq
        even = lax.rem(k, 2) == 0
        U = (jnp.where(even, B[0], B[1]), jnp.where(even, N[0], N[1]))
        V = (jnp.where(even, B[1], B[0]), jnp.where(even, N[1], N[0]))
        return Pp, U, V, Qq
    def region(self, k, r, depth, keep):
        o = self.order(k, r)
        rows, cols = self.SB, 512
        r0, c0 = k * self.CH + r * self.SB, 0
        for i in range(depth):
            b = o[i][0]
            if i == depth - 1 and not keep: b = 1 - b
            if i < 2:
                rows //= 2; r0 = r0 + b * rows
            else:
                cols //= 2; c0 = c0 + b * cols
        if depth > 2: c0 = pl.multiple_of(c0, 128)
        return pl.ds(pl.multiple_of(r0, 16), rows), pl.ds(c0, cols)
    def rs(self, k, r, i):
        n = self.order(k, r)[i][1]
        buf = (self.r1, self.r2, self.r3, self.r4)[i]
        return self.rc(self.acc.at[self.region(k, r, i + 1, False)], buf.at[k, r], self.rsem.at[0, i, k, r], self.rsem.at[1, i, k, r], n)
    def ag(self, k, r, i):
        n = self.order(k, r)[i][1]
        sl = self.region(k, r, i + 1, True)
        return self.rc(self.out.at[sl], self.out.at[sl], self.asem.at[0, i, k, r], self.asem.at[1, i, k, r], n)
    def small_copy(self, i):
        dev = (self.dp, 1 - self.t) if i == 0 else (self.parts[i - 1], self.t)
        src = self.small if i == 0 else self.sm.at[1, i - 1]
        return pltpu.make_async_remote_copy(src_ref=src, dst_ref=self.sm.at[0, i], send_sem=self.smsem.at[0, i], recv_sem=self.smsem.at[1, i], device_id=dev, device_id_type=MESH)
    def stage(self, s, k):
        if s == 0:
            self.core_copy(k).start()
        elif s == 1:
            self.core_copy(k).wait_recv()
            sl = pl.ds(pl.multiple_of(k * self.CH, 16), self.CH)
            self.acc[sl] = (self.g[self.t, sl].astype(f32) + self.core_buf[k].astype(f32)).astype(bf16)
            for r in range(3): self.rs(k, r, 0).start()
        elif s <= 5:
            i = s - 2
            buf = (self.r1, self.r2, self.r3, self.r4)[i]
            for r in range(3):
                self.rs(k, r, i).wait_recv()
                sl = self.region(k, r, i + 1, True)
                v = (self.acc[sl].astype(f32) + buf[k, r].astype(f32)).astype(bf16)
                if i < 3:
                    self.acc[sl] = v
                    self.rs(k, r, i + 1).start()
                else:
                    self.out[sl] = v
                    self.ag(k, r, 3).start()
        else:
            i = 9 - s
            for r in range(3):
                self.ag(k, r, i).wait_recv()
                if i > 0: self.ag(k, r, i - 1).start()
    def small_stage(self, i):
        if i > 0:
            self.small_copy(i - 1).wait_recv()
            own = self.small[...] if i == 1 else self.sm[1, i - 2]
            v = own + self.sm[0, i - 1]
            if i < 5: self.sm[1, i - 1] = v
            else: self.sout[...] = v
        if i < 5: self.small_copy(i).start()
    def iteration(self, it):
        for s in reversed(range(self.NSTAGE)):
            k = it - s * self.stride
            @pl.when((k >= 0) & (k < self.K))
            def _(s=s, k=k):
                self.stage(s, k)
        for i in range(6):
            @pl.when(it == i * self.stride + 1)
            def _(i=i): self.small_stage(i)
    @property
    def iterations(self): return self.K + (self.NSTAGE - 1) * self.stride
    def finish(self):
        def body(k, c):
            self.core_copy(k).wait_send()
            for r in range(3):
                for i in range(4):
                    self.rs(k, r, i).wait_send(); self.ag(k, r, i).wait_send()
            return c
        lax.fori_loop(0, self.K, body, 0)
        for i in range(5): self.small_copy(i).wait_send()
    @staticmethod
    def scratch(K, S):
        SB = ROWS // K // 3
        D = pltpu.SemaphoreType.DMA
        return [pltpu.VMEM((K, 3 * SB, 512), bf16), pltpu.VMEM((ROWS, 512), bf16),
            pltpu.VMEM((K, 3, SB // 2, 512), bf16), pltpu.VMEM((K, 3, SB // 4, 512), bf16),
            pltpu.VMEM((K, 3, SB // 4, 256), bf16), pltpu.VMEM((K, 3, SB // 4, 128), bf16),
            pltpu.VMEM((2, 5, S, 512), f32),
            D((2, K)), D((2, 4, K, 3)), D((2, 4, K, 3)), D((2, 5))]

def kern(K, stride, g, small, out, sout, *bufs):
    c = Comm(K, g, small, out, sout, bufs, stride)
    c.barrier()
    def body(it, _):
        c.iteration(it); return _
    lax.fori_loop(0, c.iterations, body, 0)
    c.finish()

def comm(g, small, K=8, stride=1):
    S = small.shape[0]
    V = pl.BlockSpec(memory_space=pltpu.VMEM)
    return pl.pallas_call(functools.partial(kern, K, stride),
        out_shape=(jax.ShapeDtypeStruct((ROWS, 512), bf16), jax.ShapeDtypeStruct((S, 512), f32)),
        in_specs=[V, V], out_specs=(V, V), scratch_shapes=Comm.scratch(K, S),
        compiler_params=pltpu.CompilerParams(collective_id=0, has_side_effects=True, vmem_limit_bytes=50 << 20), name="comm")(g, small)


def pack_half(dq, dk, dv, do, di, dd):
    vo = jnp.concatenate([dv, jnp.concatenate([do[:, :256], do[:, 256:]], axis=0)], axis=1)
    return jnp.concatenate([dd, di[:, :512], di[:, 512:], jnp.concatenate([dq, dk], axis=1), vo], axis=0)


def unpack_half(w):
    do = w[2560:3072, 256:]
    return dict(
        down=w[:1024], inner=jnp.concatenate([w[1024:1536], w[1536:2048]], axis=1),
        query=w[2048:2560, :256], key=w[2048:2560, 256:], value=w[2560:3072, :256],
        output=jnp.concatenate([do[:256], do[256:]], axis=1),
    )


def whole_chains(
    states, cotangent, lengths, span_starts, span_ends, query_weight, query_bias, key_weight, value_weight, value_bias,
    output_weight, output_bias, first_gain, first_shift, inner_weight, inner_bias, down_weight, down_bias, second_gain, second_shift,
):
    t = lax.axis_index("tensor")
    gather = lambda a, axis: lax.all_gather(a, "tensor", axis=axis, tiled=True)
    wq, wk, wv = gather(query_weight, 1), gather(key_weight, 1), gather(value_weight, 1)
    wo, wi, wd = gather(output_weight, 0), gather(inner_weight, 1), gather(down_weight, 0)
    bq, bv, bi = gather(query_bias, 0), gather(value_bias, 0), gather(inner_bias, 0)
    rows = states.shape[0]
    chains = rows // SEQ
    heads = wq.shape[1] // HEAD_DIM
    mine = lambda a: lax.dynamic_slice_in_dim(a, t * chains, chains)
    lengths, span_starts, span_ends = mine(lengths), mine(span_starts), mine(span_ends)
    layout = (chains, SEQ, heads, HEAD_DIM)
    queries = (product(states, wq) + bq).astype(bf16).reshape(layout)
    keys = product(states, wk).astype(bf16).reshape(layout)
    values = (product(states, wv) + bv).astype(bf16).reshape(layout)
    key_live = jnp.arange(SEQ, dtype=jnp.int32)[None, :] < lengths[:, None]
    scores = attention_scores(queries, keys, key_live)
    highest = jnp.max(scores, axis=-1, keepdims=True)
    logsum = highest + jnp.log(jnp.sum(jnp.exp(scores - highest), axis=-1, keepdims=True))
    probs = jnp.exp(scores - logsum)
    probs_low = probs.astype(bf16)
    context = jnp.einsum("chqk,ckhd->cqhd", probs_low, values, preferred_element_type=f32)
    context = context.reshape(rows, heads * HEAD_DIM).astype(bf16)
    first_sum = states.astype(f32) + product(context, wo) + output_bias.astype(f32)
    normed, first_pull = jax.vjp(layer_norm, first_sum, first_gain.astype(f32), first_shift.astype(f32))
    normed_low = normed.astype(bf16)
    hidden = product(normed_low, wi) + bi.astype(f32)
    activation, gelu_pull = jax.vjp(exact_gelu, hidden)
    activation_low = activation.astype(bf16)
    second_sum = normed + product(activation_low, wd) + down_bias.astype(f32)
    output, second_pull = jax.vjp(layer_norm, second_sum, second_gain.astype(f32), second_shift.astype(f32))
    position = jnp.arange(SEQ, dtype=jnp.int32)[None, :]
    live = (position >= span_starts[:, None]) & (position < span_ends[:, None]) & key_live
    grad_out = jnp.where(live.reshape(rows, 1), cotangent.astype(f32), 0.0)
    grad_second, second_gain_part, second_shift_part = second_pull(grad_out)
    grad_branch = grad_second.astype(bf16)
    down_weight_part = product_left(activation_low, grad_branch)
    (grad_hidden,) = gelu_pull(product_right(grad_branch, wd))
    grad_hidden = grad_hidden.astype(bf16)
    inner_weight_part = product_left(normed_low, grad_hidden)
    grad_normed = product_right(grad_hidden, wi) + grad_second
    grad_first, first_gain_part, first_shift_part = first_pull(grad_normed)
    grad_attended = grad_first.astype(bf16)
    output_weight_part = product_left(context, grad_attended)
    grad_context = product_right(grad_attended, wo).astype(bf16).reshape(layout)
    grad_probs = jnp.einsum("cqhd,ckhd->chqk", grad_context, values, preferred_element_type=f32)
    grad_scores = (probs * (grad_probs - jnp.sum(probs * grad_probs, axis=-1, keepdims=True))).astype(bf16)
    scale = HEAD_DIM ** (-0.5)
    flat = (rows, heads * HEAD_DIM)
    grad_queries = (jnp.einsum("chqk,ckhd->cqhd", grad_scores, keys, preferred_element_type=f32) * scale).reshape(flat).astype(bf16)
    grad_keys = (jnp.einsum("chqk,cqhd->ckhd", grad_scores, queries, preferred_element_type=f32) * scale).reshape(flat).astype(bf16)
    grad_values = jnp.einsum("chqk,cqhd->ckhd", probs_low, grad_context, preferred_element_type=f32).reshape(flat).astype(bf16)
    query_weight_part = product_left(states, grad_queries)
    key_weight_part = product_left(states, grad_keys)
    value_weight_part = product_left(states, grad_values)
    input_grad = product_right(grad_queries, wq) + product_right(grad_keys, wk) + product_right(grad_values, wv) + grad_first
    halves = jnp.stack([
        pack_half(query_weight_part[:, a * 256:a * 256 + 256], key_weight_part[:, a * 256:a * 256 + 256],
                  value_weight_part[:, a * 256:a * 256 + 256], output_weight_part[a * 256:a * 256 + 256],
                  inner_weight_part[:, a * 1024:a * 1024 + 1024], down_weight_part[a * 1024:a * 1024 + 1024])
        for a in (0, 1)]).astype(bf16)
    small = jnp.stack([
        column_sum(grad_attended), first_gain_part, first_shift_part, column_sum(grad_branch), second_gain_part, second_shift_part,
        column_sum(grad_queries), column_sum(grad_values), *column_sum(grad_hidden).reshape(4, 512)] + [jnp.zeros((512,), f32)] * 4)
    summed, small = comm(halves, small, 4, 2)
    w = {k: v.astype(f32) for k, v in unpack_half(summed).items()}
    half = lambda row: lax.dynamic_slice_in_dim(row, t * 256, 256)
    return (
        output.astype(bf16), input_grad, w["query"], half(small[6]), w["key"], w["value"], half(small[7]), w["output"],
        small[0], small[1], small[2], w["inner"], lax.dynamic_slice_in_dim(small[8:12].reshape(2048), t * 1024, 1024),
        w["down"], small[3], small[4], small[5],
    )


def local(*arguments):
    rows, hidden = arguments[0].shape[0], arguments[14].shape[1]
    if rows % SEQ == 0 and lax.axis_size("dp") == 16 and lax.axis_size("tensor") == 2:
        return whole_chains(*arguments)
    return general(*arguments)


def solution(mesh):
    placed = (
        P(("dp", "tensor"), None),
        P(("dp", "tensor"), None),
        P("dp"),
        P("dp"),
        P("dp"),
        P(None, "tensor"),
        P("tensor"),
        P(None, "tensor"),
        P(None, "tensor"),
        P("tensor"),
        P("tensor", None),
        P(),
        P(),
        P(),
        P(None, "tensor"),
        P("tensor"),
        P("tensor", None),
        P(),
        P(),
        P(),
    )
    return jax.shard_map(
        local,
        mesh=mesh,
        in_specs=placed,
        out_specs=(
            P(("dp", "tensor"), None),
            P(("dp", "tensor"), None),
            P(None, "tensor"),
            P("tensor"),
            P(None, "tensor"),
            P(None, "tensor"),
            P("tensor"),
            P("tensor", None),
            P(),
            P(),
            P(),
            P(None, "tensor"),
            P("tensor"),
            P("tensor", None),
            P(),
            P(),
            P(),
        ),
        check_vma=False,
    )
```

```python
import functools

import jax
import jax.numpy as jnp
from jax import lax
from jax.experimental import pallas as pl
from jax.experimental.pallas import tpu as pltpu
from jax.sharding import PartitionSpec as P

MESH = pl.DeviceIdType.MESH
f32, bf16 = jnp.float32, jnp.bfloat16
HEAD_DIM = 64
SEQ = 160
ROWS = 3072
SCALE = HEAD_DIM ** (-0.5)
ATT_BLOCK = 32
FFN_BLOCK = 256
EPSILON = 1e-12


def product(left, right):
    return jnp.dot(left, right, preferred_element_type=jnp.float32)


def product_left(left, right):
    return lax.dot_general(
        left, right, (((0,), (0,)), ((), ())), preferred_element_type=jnp.float32
    )


def product_right(left, right):
    return lax.dot_general(
        left, right, (((1,), (1,)), ((), ())), preferred_element_type=jnp.float32
    )


def layer_norm(values, gain, shift):
    center = values - jnp.mean(values, axis=-1, keepdims=True)
    spread = jnp.mean(center * center, axis=-1, keepdims=True)
    return center * lax.rsqrt(spread + EPSILON) * gain + shift


def exact_gelu(values):
    return jax.nn.gelu(values, approximate=False)


def attention_scores(queries, keys, key_live):
    scores = jnp.einsum(
        "cqhd,ckhd->chqk", queries, keys, preferred_element_type=jnp.float32
    ) * HEAD_DIM ** (-0.5)
    return jnp.where(key_live[:, None, None, :], scores, -1000000000.0)


def per_row(table, picker):
    return jnp.sum(jnp.where(picker, table[None, :], 0), axis=1)


def column_sum(values):
    return jnp.sum(values.astype(jnp.float32), axis=0)


def general(
    states,
    cotangent,
    lengths,
    span_starts,
    span_ends,
    query_weight,
    query_bias,
    key_weight,
    value_weight,
    value_bias,
    output_weight,
    output_bias,
    first_gain,
    first_shift,
    inner_weight,
    inner_bias,
    down_weight,
    down_bias,
    second_gain,
    second_shift,
):
    slice_rows = states.shape[0]
    chains = lengths.shape[0]
    group_rows = chains * SEQ
    heads_local = query_weight.shape[1] // HEAD_DIM
    layout = (chains, SEQ, heads_local, HEAD_DIM)
    whole = lax.all_gather(states, "tensor", axis=0, tiled=True)
    queries = (product(whole, query_weight) + query_bias).astype(jnp.bfloat16).reshape(layout)
    keys_low = product(whole, key_weight).astype(jnp.bfloat16).reshape(layout)
    values_low = (product(whole, value_weight) + value_bias).astype(jnp.bfloat16).reshape(layout)
    key_live = jnp.arange(SEQ, dtype=jnp.int32)[None, :] < lengths[:, None]
    scores = attention_scores(queries, keys_low, key_live)
    highest = jnp.max(scores, axis=-1, keepdims=True)
    logsum = highest + jnp.log(jnp.sum(jnp.exp(scores - highest), axis=-1, keepdims=True))
    probs_low = jnp.exp(scores - logsum).astype(jnp.bfloat16)
    context = jnp.einsum(
        "chqk,ckhd->cqhd", probs_low, values_low, preferred_element_type=jnp.float32
    )
    context = context.reshape(group_rows, heads_local * HEAD_DIM).astype(jnp.bfloat16)
    attended = lax.psum_scatter(
        product(context, output_weight), "tensor", scatter_dimension=0, tiled=True
    ) + output_bias.astype(jnp.float32)
    first_sum = states.astype(jnp.float32) + attended
    normed, first_pull = jax.vjp(
        layer_norm, first_sum, first_gain.astype(jnp.float32), first_shift.astype(jnp.float32)
    )
    normed_low = normed.astype(jnp.bfloat16)
    normed_all = lax.all_gather(normed_low, "tensor", axis=0, tiled=True)
    hidden = product(normed_all, inner_weight) + inner_bias.astype(jnp.float32)
    activation, gelu_pull = jax.vjp(exact_gelu, hidden)
    activation_low = activation.astype(jnp.bfloat16)
    branch = lax.psum_scatter(
        product(activation_low, down_weight), "tensor", scatter_dimension=0, tiled=True
    )
    second_sum = normed + (branch + down_bias.astype(jnp.float32))
    output, second_pull = jax.vjp(
        layer_norm, second_sum, second_gain.astype(jnp.float32), second_shift.astype(jnp.float32)
    )
    row_ids = lax.axis_index("tensor") * slice_rows + jnp.arange(slice_rows, dtype=jnp.int32)
    chain_ids = row_ids // SEQ
    position = row_ids % SEQ
    picker = chain_ids[:, None] == jnp.arange(chains, dtype=jnp.int32)[None, :]
    live = (
        (position >= per_row(span_starts, picker))
        & (position < per_row(span_ends, picker))
        & (position < per_row(lengths, picker))
    )
    grad_out = jnp.where(live[:, None], cotangent.astype(jnp.float32), 0.0)
    grad_second, second_gain_part, second_shift_part = second_pull(grad_out)
    grad_branch = grad_second.astype(jnp.bfloat16)
    down_bias_part = column_sum(grad_branch)
    grad_branch_all = lax.all_gather(grad_branch, "tensor", axis=0, tiled=True)
    down_weight_part = product_left(activation_low, grad_branch_all)
    grad_activation = product_right(grad_branch_all, down_weight)
    (grad_hidden,) = gelu_pull(grad_activation)
    grad_hidden_low = grad_hidden.astype(jnp.bfloat16)
    inner_weight_part = product_left(normed_all, grad_hidden_low)
    inner_bias_part = column_sum(grad_hidden_low)
    grad_normed = lax.psum_scatter(
        product_right(grad_hidden_low, inner_weight), "tensor", scatter_dimension=0, tiled=True
    )
    grad_first, first_gain_part, first_shift_part = first_pull(grad_second + grad_normed)
    grad_attended = grad_first.astype(jnp.bfloat16)
    output_bias_part = column_sum(grad_attended)
    grad_attended_all = lax.all_gather(grad_attended, "tensor", axis=0, tiled=True)
    output_weight_part = product_left(context, grad_attended_all)
    grad_context = (
        product_right(grad_attended_all, output_weight).astype(jnp.bfloat16).reshape(layout)
    )
    probs = jnp.exp(attention_scores(queries, keys_low, key_live) - logsum)
    grad_probs = jnp.einsum(
        "cqhd,ckhd->chqk", grad_context, values_low, preferred_element_type=jnp.float32
    )
    grad_scores = probs * (grad_probs - jnp.sum(probs * grad_probs, axis=-1, keepdims=True))
    grad_scores_low = grad_scores.astype(jnp.bfloat16)
    scale = HEAD_DIM ** (-0.5)
    grad_queries = (
        jnp.einsum("chqk,ckhd->cqhd", grad_scores_low, keys_low, preferred_element_type=jnp.float32)
        * scale
    )
    grad_keys = (
        jnp.einsum("chqk,cqhd->ckhd", grad_scores_low, queries, preferred_element_type=jnp.float32)
        * scale
    )
    grad_values = jnp.einsum(
        "chqk,cqhd->ckhd", probs_low, grad_context, preferred_element_type=jnp.float32
    )
    flat = (group_rows, heads_local * HEAD_DIM)
    grad_queries = grad_queries.reshape(flat).astype(jnp.bfloat16)
    grad_keys = grad_keys.reshape(flat).astype(jnp.bfloat16)
    grad_values = grad_values.reshape(flat).astype(jnp.bfloat16)
    query_weight_part = product_left(whole, grad_queries)
    key_weight_part = product_left(whole, grad_keys)
    value_weight_part = product_left(whole, grad_values)
    query_bias_part = column_sum(grad_queries)
    value_bias_part = column_sum(grad_values)
    grad_whole = (
        product_right(grad_queries, query_weight)
        + product_right(grad_keys, key_weight)
        + product_right(grad_values, value_weight)
    )
    input_grad = (
        lax.psum_scatter(
            grad_whole.astype(jnp.bfloat16), "tensor", scatter_dimension=0, tiled=True
        ).astype(jnp.float32)
        + grad_first
    )
    (
        query_weight_grad,
        query_bias_grad,
        key_weight_grad,
        value_weight_grad,
        value_bias_grad,
        output_weight_grad,
        inner_weight_grad,
        inner_bias_grad,
        down_weight_grad,
    ) = (
        lax.psum(query_weight_part.astype(jnp.bfloat16), "dp").astype(jnp.float32),
        lax.psum(query_bias_part.astype(jnp.bfloat16), "dp").astype(jnp.float32),
        lax.psum(key_weight_part.astype(jnp.bfloat16), "dp").astype(jnp.float32),
        lax.psum(value_weight_part.astype(jnp.bfloat16), "dp").astype(jnp.float32),
        lax.psum(value_bias_part.astype(jnp.bfloat16), "dp").astype(jnp.float32),
        lax.psum(output_weight_part.astype(jnp.bfloat16), "dp").astype(jnp.float32),
        lax.psum(inner_weight_part.astype(jnp.bfloat16), "dp").astype(jnp.float32),
        lax.psum(inner_bias_part.astype(jnp.bfloat16), "dp").astype(jnp.float32),
        lax.psum(down_weight_part.astype(jnp.bfloat16), "dp").astype(jnp.float32),
    )
    (
        output_bias_grad,
        first_gain_grad,
        first_shift_grad,
        down_bias_grad,
        second_gain_grad,
        second_shift_grad,
    ) = lax.psum(
        (
            output_bias_part,
            first_gain_part,
            first_shift_part,
            down_bias_part,
            second_gain_part,
            second_shift_part,
        ),
        ("dp", "tensor"),
    )
    return (
        output.astype(jnp.bfloat16),
        input_grad,
        query_weight_grad,
        query_bias_grad,
        key_weight_grad,
        value_weight_grad,
        value_bias_grad,
        output_weight_grad,
        output_bias_grad,
        first_gain_grad,
        first_shift_grad,
        inner_weight_grad,
        inner_bias_grad,
        down_weight_grad,
        down_bias_grad,
        second_gain_grad,
        second_shift_grad,
    )


class Comm:
    NSTAGE = 10
    def __init__(self, K, g, small, out, sout, bufs, stride=1):
        self.stride = stride
        self.K = K; self.CH = ROWS // K; self.SB = self.CH // 3
        self.g, self.small, self.out_hbm, self.sout = g, small, out, sout
        (self.core_buf, self.acc, self.r1, self.r2, self.r3, self.r4, self.out, self.sm, self.csem, self.rsem, self.asem, self.smsem, self.fsem) = bufs
        dp = lax.axis_index("dp"); t = lax.axis_index("tensor")
        self.t = t
        x = lax.rem(dp, 2); y = lax.rem(dp // 2, 2); p = lax.rem(dp // 4, 2); q = dp // 8
        self.bits = (x, y, p, q)
        self.parts = tuple(dp + w * (1 - 2 * b) for w, b in ((1, x), (2, y), (4, p), (8, q)))
        self.dp = dp
    def barrier(self):
        b = pltpu.get_barrier_semaphore()
        pl.semaphore_signal(b, inc=1, device_id=(self.dp, 1 - self.t), device_id_type=MESH)
        for n in self.parts:
            pl.semaphore_signal(b, inc=1, device_id=(n, self.t), device_id_type=MESH)
        pl.semaphore_wait(b, 5)
    def rc(self, src, dst, s, r, n):
        return pltpu.make_async_remote_copy(src_ref=src, dst_ref=dst, send_sem=s, recv_sem=r, device_id=(n, self.t), device_id_type=MESH)
    def core_copy(self, k):
        return pltpu.make_async_remote_copy(src_ref=self.g.at[1 - self.t, pl.ds(k * self.CH, self.CH)], dst_ref=self.core_buf.at[k],
            send_sem=self.csem.at[0, k], recv_sem=self.csem.at[1, k], device_id=(self.dp, 1 - self.t), device_id_type=MESH)
    def order(self, k, r):
        B, N = self.bits, self.parts
        X, Y, Pp, Qq = ((B[i], N[i]) for i in range(4))
        if r == 0: return X, Y, Pp, Qq
        if r == 1: return Y, X, Pp, Qq
        even = lax.rem(k, 2) == 0
        U = (jnp.where(even, B[0], B[1]), jnp.where(even, N[0], N[1]))
        V = (jnp.where(even, B[1], B[0]), jnp.where(even, N[1], N[0]))
        return Pp, U, V, Qq
    def region(self, k, r, depth, keep):
        o = self.order(k, r)
        rows, cols = self.SB, 512
        r0, c0 = k * self.CH + r * self.SB, 0
        for i in range(depth):
            b = o[i][0]
            if i == depth - 1 and not keep: b = 1 - b
            if i < 2:
                rows //= 2; r0 = r0 + b * rows
            else:
                cols //= 2; c0 = c0 + b * cols
        if depth > 2: c0 = pl.multiple_of(c0, 128)
        return pl.ds(pl.multiple_of(r0, 16), rows), pl.ds(c0, cols)
    def rs(self, k, r, i):
        n = self.order(k, r)[i][1]
        buf = (self.r1, self.r2, self.r3, self.r4)[i]
        return self.rc(self.acc.at[self.region(k, r, i + 1, False)], buf.at[k, r], self.rsem.at[0, i, k, r], self.rsem.at[1, i, k, r], n)
    def ag(self, k, r, i):
        n = self.order(k, r)[i][1]
        sl = self.region(k, r, i + 1, True)
        return self.rc(self.out.at[sl], self.out.at[sl], self.asem.at[0, i, k, r], self.asem.at[1, i, k, r], n)
    def small_copy(self, i):
        dev = (self.dp, 1 - self.t) if i == 0 else (self.parts[i - 1], self.t)
        src = self.small if i == 0 else self.sm.at[1, i - 1]
        return pltpu.make_async_remote_copy(src_ref=src, dst_ref=self.sm.at[0, i], send_sem=self.smsem.at[0, i], recv_sem=self.smsem.at[1, i], device_id=dev, device_id_type=MESH)
    def stage(self, s, k):
        if s == 0:
            self.core_copy(k).start()
        elif s == 1:
            self.core_copy(k).wait_recv()
            sl = pl.ds(pl.multiple_of(k * self.CH, 16), self.CH)
            self.acc[sl] = (self.g[self.t, sl].astype(f32) + self.core_buf[k].astype(f32)).astype(bf16)
            for r in range(3): self.rs(k, r, 0).start()
        elif s <= 5:
            i = s - 2
            buf = (self.r1, self.r2, self.r3, self.r4)[i]
            for r in range(3):
                self.rs(k, r, i).wait_recv()
                sl = self.region(k, r, i + 1, True)
                v = (self.acc[sl].astype(f32) + buf[k, r].astype(f32)).astype(bf16)
                if i < 3:
                    self.acc[sl] = v
                    self.rs(k, r, i + 1).start()
                else:
                    self.out[sl] = v
                    self.ag(k, r, 3).start()
        else:
            i = 9 - s
            for r in range(3):
                self.ag(k, r, i).wait_recv()
                if i > 0: self.ag(k, r, i - 1).start()
            if i == 0: self.final_copy(k).start()
    def final_copy(self, k):
        sl = pl.ds(k * self.CH, self.CH)
        return pltpu.make_async_copy(self.out.at[sl], self.out_hbm.at[sl], self.fsem.at[k])
    def small_stage(self, i):
        if i > 0:
            self.small_copy(i - 1).wait_recv()
            own = self.small[...] if i == 1 else self.sm[1, i - 2]
            v = own + self.sm[0, i - 1]
            if i < 5: self.sm[1, i - 1] = v
            else: self.sout[...] = v
        if i < 5: self.small_copy(i).start()
    def iteration(self, it):
        for s in reversed(range(self.NSTAGE)):
            k = it - s * self.stride
            @pl.when((k >= 0) & (k < self.K))
            def _(s=s, k=k):
                self.stage(s, k)
        for i in range(6):
            @pl.when(it == i * self.stride + 1)
            def _(i=i): self.small_stage(i)
    @property
    def iterations(self): return self.K + (self.NSTAGE - 1) * self.stride
    def finish(self):
        def body(k, c):
            self.core_copy(k).wait_send(); self.final_copy(k).wait()
            for r in range(3):
                for i in range(4):
                    self.rs(k, r, i).wait_send(); self.ag(k, r, i).wait_send()
            return c
        lax.fori_loop(0, self.K, body, 0)
        for i in range(5): self.small_copy(i).wait_send()
    @staticmethod
    def scratch(K, S):
        SB = ROWS // K // 3
        D = pltpu.SemaphoreType.DMA
        return [pltpu.VMEM((K, 3 * SB, 512), bf16), pltpu.VMEM((ROWS, 512), bf16),
            pltpu.VMEM((K, 3, SB // 2, 512), bf16), pltpu.VMEM((K, 3, SB // 4, 512), bf16),
            pltpu.VMEM((K, 3, SB // 4, 256), bf16), pltpu.VMEM((K, 3, SB // 4, 128), bf16),
            pltpu.VMEM((ROWS, 512), bf16), pltpu.VMEM((2, 5, S, 512), f32),
            D((2, K)), D((2, 4, K, 3)), D((2, 4, K, 3)), D((2, 5)), D((K,))]


def gather_kernel(
    x_ref, wq_ref, wk_ref, wv_ref, bq_ref, bv_ref, bi_ref, wo_ref, wi_ref, wd_ref,
    q_ref, k_ref, v_ref, wqkv_out, wo_out, wi_out, wd_out, bias_out,
    wqkv, bias, near, sent, came,
):
    step = pl.program_id(0)
    dp, t = lax.axis_index("dp"), lax.axis_index("tensor")

    def pair(i, src, dst):
        return pltpu.make_async_remote_copy(
            src_ref=src, dst_ref=dst, send_sem=sent.at[i], recv_sem=came.at[i],
            device_id=(dp, 1 - t), device_id_type=MESH,
        )

    first = [
        pair(0, wq_ref, wqkv.at[t, 0]), pair(1, wk_ref, wqkv.at[t, 1]), pair(2, wv_ref, wqkv.at[t, 2]),
        pair(3, bias.at[t], bias.at[t]),
    ]
    later = [pair(4, wo_ref, wo_out.at[t]), pair(5, wi_ref, wi_out.at[t]), pair(6, wd_ref, wd_out.at[t])]
    own = [
        pltpu.make_async_copy(wo_ref, wo_out.at[t], near.at[0]),
        pltpu.make_async_copy(wi_ref, wi_out.at[t], near.at[1]),
        pltpu.make_async_copy(wd_ref, wd_out.at[t], near.at[2]),
    ]
    keep = [pltpu.make_async_copy(wqkv, wqkv_out, near.at[3]), pltpu.make_async_copy(bias, bias_out, near.at[4])]

    @pl.when(step == 0)
    def _():
        barrier = pltpu.get_barrier_semaphore()
        pl.semaphore_signal(barrier, inc=1, device_id=(dp, 1 - t), device_id_type=MESH)
        bias[t, 0:1] = bq_ref[...].astype(f32)
        bias[t, 1:2] = bv_ref[...].astype(f32)
        for i in range(4):
            bias[t, 2 + i : 3 + i] = bi_ref[:, 256 * i : 256 * i + 256].astype(f32)
        bias[t, 6:8] = jnp.zeros((2, 256), f32)
        pl.semaphore_wait(barrier, 1)
        for copy in first + later:
            copy.start()
        for copy in own:
            copy.start()
        for j, ref in enumerate((wq_ref, wk_ref, wv_ref)):
            wqkv[t, j] = ref[...]
        for copy in first:
            copy.wait_recv()
        for copy in keep:
            copy.start()

    x = x_ref[...]
    for h in range(2):
        cols = slice(256 * h, 256 * h + 256)
        q_ref[:, cols] = ((product(x, wqkv[h, 0]) + bias[h, 0:1]).astype(bf16).astype(f32) * SCALE).astype(bf16)
        k_ref[:, cols] = product(x, wqkv[h, 1]).astype(bf16)
        v_ref[:, cols] = (product(x, wqkv[h, 2]) + bias[h, 1:2]).astype(bf16)

    @pl.when(step == pl.num_programs(0) - 1)
    def _():
        for copy in first:
            copy.wait_send()
        for copy in later:
            copy.wait()
        for copy in own + keep:
            copy.wait()


def gather(states, wq, wk, wv, bq, bv, bi, wo, wi, wd):
    rows = states.shape[0]
    block = 2 * SEQ
    whole = lambda a: pl.BlockSpec(a.shape, lambda i: (0,) * a.ndim)
    tile = pl.BlockSpec((block, 512), lambda i: (i, 0))
    hbm = pl.BlockSpec(memory_space=pl.ANY)
    D = pltpu.SemaphoreType.DMA
    S = jax.ShapeDtypeStruct
    return pl.pallas_call(
        gather_kernel,
        grid=(rows // block,),
        in_specs=[tile, whole(wq), whole(wk), whole(wv), whole(bq), whole(bv), whole(bi), hbm, hbm, hbm],
        out_specs=[tile, tile, tile, hbm, hbm, hbm, hbm, hbm],
        out_shape=[S((rows, 512), bf16)] * 3 + [
            S((2, 3, 512, 256), bf16), S((2, 256, 512), bf16), S((2, 512, 1024), bf16), S((2, 1024, 512), bf16), S((2, 8, 256), f32),
        ],
        scratch_shapes=[pltpu.VMEM((2, 3, 512, 256), bf16), pltpu.VMEM((2, 8, 256), f32), D((5,)), D((7,)), D((7,))],
        compiler_params=pltpu.CompilerParams(collective_id=1, has_side_effects=True, vmem_limit_bytes=60 << 20),
        name="gather",
    )(states, wq, wk, wv, bq, bv, bi, wo, wi, wd)


def select_heads(full, block, heads):
    out = full[3 * block :]
    for h in (2, 1, 0):
        out = jnp.where(heads[:block] == h, full[h * block : (h + 1) * block], out)
    return out


def spread_heads(rows, block, own):
    return jnp.where(own, jnp.concatenate([rows] * 4, axis=0), jnp.zeros((), rows.dtype))


def normal_parts(h):
    a = jnp.abs(h)
    u = 1.0 / (1.0 + (0.3275911 * 0.7071067811865476) * a)
    bell = jnp.exp(-0.5 * h * h)
    poly = u * (0.254829592 + u * (-0.284496736 + u * (1.421413741 + u * (-1.453152027 + u * 1.061405429))))
    tail = 0.5 * poly * bell
    return jnp.where(h < 0, tail, 1.0 - tail), bell * 0.3989422804014327


def row_mean(a):
    return jnp.sum(a, axis=-1, keepdims=True) * (1.0 / 512)


def chain_scalars(len_ref, start_ref, end_ref, c):
    length = len_ref[c]
    start = start_ref[c]
    end = jnp.minimum(end_ref[c], length)
    return length, start, end


def live_kernel(
    len_ref, start_ref, end_ref,
    x_ref, cot_ref, q_ref, k_ref, v_ref, wo_hbm, wi_hbm, wd_hbm, bias_ref, vec_ref,
    g_out, small_out, dq_ref, dk_ref, dv_ref, gf_ref,
    wo, wi, wd, context, inputs, upstream, first, x_all, dk_all, dv_all, acc_k, acc_v, acc_d, acc_i, acc_o, acc_s, gelu_grad, act, stage, off, sems,
):
    step = pl.program_id(0)
    chains = len_ref.shape[0] // 2
    t = lax.axis_index("tensor")
    B = ATT_BLOCK
    R = FFN_BLOCK
    PAD = 32
    loads = [pltpu.make_async_copy(a, b, sems.at[i]) for i, (a, b) in enumerate(((wo_hbm, wo), (wi_hbm, wi), (wd_hbm, wd)))]
    heads = lax.broadcasted_iota(jnp.int32, (4 * B, 256), 1) // HEAD_DIM
    own = heads == lax.broadcasted_iota(jnp.int32, (4 * B, 256), 0) // B

    @pl.when(step == 0)
    def _():
        for copy in loads:
            copy.start()
        off[0] = 0
        acc_d[...] = jnp.zeros_like(acc_d)
        acc_i[...] = jnp.zeros_like(acc_i)
        acc_o[...] = jnp.zeros_like(acc_o)
        acc_s[...] = jnp.zeros_like(acc_s)

    def blocks_of(c):
        length, start, end = chain_scalars(len_ref, start_ref, end_ref, t * chains + c)
        r16 = (start // 16) * 16
        b0 = start // B
        b1 = jnp.where(end > start, (end + B - 1) // B, b0)
        return length, start, end, r16, b0, b1

    def probabilities(q, k, length):
        qs = spread_heads(q, B, own)
        scores = product_right(qs, k)
        scores = jnp.where(lax.broadcasted_iota(jnp.int32, scores.shape, 1) < length, scores, -1e9)
        e = jnp.exp(scores - jnp.max(scores, axis=-1, keepdims=True))
        return qs, e * (1.0 / jnp.sum(e, axis=-1, keepdims=True))

    @pl.when(step < chains)
    def _forward():
        c = step
        length, start, end, r16, b0, b1 = blocks_of(c)
        base = off[c] + PAD - r16
        off[c + 1] = off[c] + jnp.where(end > start, ((end + 15) // 16) * 16 - r16, 0)
        x_all[pl.ds(c * SEQ, SEQ)] = x_ref[...]

        def block(b, carry):
            p0 = pl.multiple_of(b * B, B)
            out = []
            for g in range(2):
                cols = slice(256 * g, 256 * g + 256)
                _, p = probabilities(q_ref[pl.ds(p0, B), cols], k_ref[:, cols], length)
                out.append(select_heads(product(p.astype(bf16), v_ref[:, cols]), B, heads))
            ctx = jnp.concatenate(out, axis=1).astype(bf16)
            pos = p0 + lax.broadcasted_iota(jnp.int32, (B, 512), 0)
            live = (pos >= start) & (pos < end)
            cot = jnp.where(live, cot_ref[pl.ds(p0, B)].astype(f32), 0.0).astype(bf16)
            x = x_ref[pl.ds(p0, B)]
            for i in range(B // 16):
                @pl.when(p0 + 16 * i >= r16)
                def _(i=i):
                    dst = pl.ds(pl.multiple_of(base + p0 + 16 * i, 16), 16)
                    rows = slice(16 * i, 16 * i + 16)
                    context[dst] = ctx[rows]
                    inputs[dst] = x[rows]
                    upstream[dst] = cot[rows]
            return carry

        lax.fori_loop(b0, b1, block, 0)

    @pl.when(step == chains)
    def _feed_forward():
        n = off[chains]
        tail = pl.ds(pl.multiple_of(PAD + n, 16), R)
        for ref in (context, inputs, upstream):
            ref[tail] = jnp.zeros((R, 512), bf16)
        for copy in loads:
            copy.wait()
        vec = vec_ref[...].astype(f32)
        bo, g1, s1, bd, g2, s2 = (vec[i : i + 1] for i in range(6))

        def block(b, carry):
            rows = pl.ds(pl.multiple_of(PAD + b * R, 16), R)
            ctx = context[rows]
            attended = product(ctx[:, :256], wo[0]) + product(ctx[:, 256:], wo[1]) + bo
            s = inputs[rows].astype(f32) + attended
            center = s - row_mean(s)
            rstd1 = lax.rsqrt(row_mean(center * center) + EPSILON)
            hat1 = center * rstd1
            normed = hat1 * g1 + s1
            low = normed.astype(bf16)
            branch = jnp.zeros((R, 512), f32) + bd
            for j in range(4):
                h, o = j // 2, 512 * (j % 2)
                bi = jnp.concatenate([bias_ref[h, 2 + o // 256 : 3 + o // 256], bias_ref[h, 3 + o // 256 : 4 + o // 256]], axis=1)
                hid = product(low, wi[h, :, o : o + 512]) + bi
                cdf, pdf = normal_parts(hid)
                a = (hid * cdf).astype(bf16)
                gelu_grad[j] = cdf + hid * pdf
                act[j] = a
                branch = branch + product(a, wd[h, o : o + 512])
            s = normed + branch
            center = s - row_mean(s)
            rstd2 = lax.rsqrt(row_mean(center * center) + EPSILON)
            hat2 = center * rstd2
            up = upstream[rows].astype(f32)
            gy = up * g2
            grad = rstd2 * (gy - row_mean(gy) - hat2 * row_mean(gy * hat2))
            gb = grad.astype(bf16)
            gn = grad
            for j in range(4):
                h, o = j // 2, 512 * (j % 2)
                gh = (product_right(gb, wd[h, o : o + 512]) * gelu_grad[j]).astype(bf16)
                acc_d[h, o : o + 512] += product_left(act[j], gb)
                acc_i[j] += product_left(low, gh)
                acc_s[8 + j : 9 + j] += jnp.sum(gh.astype(f32), axis=0, keepdims=True)
                gn = gn + product_right(gh, wi[h, :, o : o + 512])
            acc_s[1:2] += jnp.sum(gn * hat1, axis=0, keepdims=True)
            acc_s[2:3] += jnp.sum(gn, axis=0, keepdims=True)
            acc_s[3:4] += jnp.sum(gb.astype(f32), axis=0, keepdims=True)
            acc_s[4:5] += jnp.sum(up * hat2, axis=0, keepdims=True)
            acc_s[5:6] += jnp.sum(up, axis=0, keepdims=True)
            gy = gn * g1
            grad = rstd1 * (gy - row_mean(gy) - hat1 * row_mean(gy * hat1))
            first[rows] = grad
            ga = grad.astype(bf16)
            acc_s[0:1] += jnp.sum(ga.astype(f32), axis=0, keepdims=True)
            acc_o[...] += product_left(ctx, ga)
            upstream[rows] = jnp.concatenate([product_right(ga, wo[0]), product_right(ga, wo[1])], axis=1).astype(bf16)
            return carry

        lax.fori_loop(0, (n + R - 1) // R, block, 0)
        for h in range(2):
            stage[h, 0:1024] = acc_d[h].astype(bf16)
            stage[h, 1024:1536] = acc_i[2 * h].astype(bf16)
            stage[h, 1536:2048] = acc_i[2 * h + 1].astype(bf16)
            pltpu.make_async_copy(stage.at[h, pl.ds(0, 2048)], g_out.at[h, pl.ds(0, 2048)], sems.at[3 + h]).start()
            stage[h, 2560:2816, 256:512] = acc_o[256 * h : 256 * h + 256, 0:256].astype(bf16)
            stage[h, 2816:3072, 256:512] = acc_o[256 * h : 256 * h + 256, 256:512].astype(bf16)

    @pl.when(step > chains)
    def _backward():
        c = step - chains - 1
        length, start, end, r16, b0, b1 = blocks_of(c)
        base = off[c] + PAD - r16
        acc_k[...] = jnp.zeros_like(acc_k)
        acc_v[...] = jnp.zeros_like(acc_v)
        dq_ref[...] = jnp.zeros_like(dq_ref)
        gf_ref[...] = jnp.zeros_like(gf_ref)

        def block(b, carry):
            p0 = pl.multiple_of(b * B, B)
            src = pl.ds(pl.multiple_of(base + p0, 16), B)
            pos = p0 + lax.broadcasted_iota(jnp.int32, (B, 512), 0)
            live = (pos >= start) & (pos < end)
            gc = jnp.where(live, upstream[src].astype(f32), 0.0).astype(bf16)
            out = []
            for g in range(2):
                cols = slice(256 * g, 256 * g + 256)
                qs, p = probabilities(q_ref[pl.ds(p0, B), cols], k_ref[:, cols], length)
                gs = spread_heads(gc[:, cols], B, own)
                gp = product_right(gs, v_ref[:, cols])
                ds = (p * (gp - jnp.sum(p * gp, axis=-1, keepdims=True))).astype(bf16)
                out.append(select_heads(product(ds, k_ref[:, cols]), B, heads) * SCALE)
                acc_k[:, cols] += product_left(ds, qs)
                acc_v[:, cols] += product_left(p.astype(bf16), gs)
            dq = jnp.concatenate(out, axis=1).astype(bf16)
            dq_ref[pl.ds(p0, B)] = dq
            gf_ref[pl.ds(p0, B)] = jnp.where(live, first[src], 0.0)
            for i in range(B // 16):
                @pl.when(p0 + 16 * i >= r16)
                def _(i=i):
                    dst = pl.ds(pl.multiple_of(base + p0 + 16 * i, 16), 16)
                    context[dst] = dq[16 * i : 16 * i + 16]
            return carry

        lax.fori_loop(b0, b1, block, 0)
        dk_ref[...] = acc_k[...].astype(bf16)
        dv_ref[...] = acc_v[...].astype(bf16)
        rows = pl.ds(c * SEQ, SEQ)
        dk_all[rows] = dk_ref[...]
        dv_all[rows] = dv_ref[...]

    @pl.when(step == 2 * chains)
    def _weights():
        n = off[chains]
        context[pl.ds(pl.multiple_of(PAD + n, 16), R)] = jnp.zeros((R, 512), bf16)
        acc_o[...] = jnp.zeros_like(acc_o)

        def block(b, carry):
            rows = pl.ds(pl.multiple_of(PAD + b * R, 16), R)
            dq = context[rows]
            acc_o[...] += product_left(inputs[rows], dq)
            acc_s[6:7] += jnp.sum(dq.astype(f32), axis=0, keepdims=True)
            return carry

        lax.fori_loop(0, (n + R - 1) // R, block, 0)
        acc_s[7:8] = jnp.sum(dv_all[...].astype(f32), axis=0, keepdims=True)
        dk = product_left(x_all[...], dk_all[...])
        dv = product_left(x_all[...], dv_all[...])
        for h in range(2):
            cols = slice(256 * h, 256 * h + 256)
            stage[h, 2048:2560, 0:256] = acc_o[:, cols].astype(bf16)
            stage[h, 2048:2560, 256:512] = dk[:, cols].astype(bf16)
            stage[h, 2560:3072, 0:256] = dv[:, cols].astype(bf16)
            pltpu.make_async_copy(stage.at[h, pl.ds(2048, 1024)], g_out.at[h, pl.ds(2048, 1024)], sems.at[5 + h]).start()
        small_out[...] = acc_s[...]
        for h in range(2):
            pltpu.make_async_copy(stage.at[h, pl.ds(0, 2048)], g_out.at[h, pl.ds(0, 2048)], sems.at[3 + h]).wait()
            pltpu.make_async_copy(stage.at[h, pl.ds(2048, 1024)], g_out.at[h, pl.ds(2048, 1024)], sems.at[5 + h]).wait()


def live_rows(lengths, starts, ends, states, cotangent, q, k, v, wo, wi, wd, bias, vec):
    rows = states.shape[0]
    chains = rows // SEQ
    R = FFN_BLOCK
    C = rows + 32 + R
    twice = lambda i, *_: (jnp.where(i < chains, i, jnp.maximum(i - chains - 1, 0)), 0)
    ahead = lambda i, *_: (jnp.minimum(i, chains - 1), 0)
    after = lambda i, *_: (jnp.maximum(i - chains - 1, 0), 0)
    tile = lambda f: pl.BlockSpec((SEQ, 512), f)
    whole = lambda a: pl.BlockSpec(a.shape, lambda i, *_: (0,) * a.ndim)
    hbm = pl.BlockSpec(memory_space=pl.ANY)
    S, V = jax.ShapeDtypeStruct, pltpu.VMEM
    return pl.pallas_call(
        live_kernel,
        grid_spec=pltpu.PrefetchScalarGridSpec(
            num_scalar_prefetch=3,
            grid=(2 * chains + 1,),
            in_specs=[tile(ahead), tile(ahead), tile(twice), tile(twice), tile(twice), hbm, hbm, hbm, whole(bias), whole(vec)],
            out_specs=[hbm, pl.BlockSpec((16, 512), lambda i, *_: (0, 0)), tile(after), tile(after), tile(after), tile(after)],
            scratch_shapes=[
                V((2, 256, 512), bf16), V((2, 512, 1024), bf16), V((2, 1024, 512), bf16),
                V((C, 512), bf16), V((C, 512), bf16), V((C, 512), bf16), V((C, 512), f32),
                V((rows, 512), bf16), V((rows, 512), bf16), V((rows, 512), bf16),
                V((SEQ, 512), f32), V((SEQ, 512), f32),
                V((2, 1024, 512), f32), V((4, 512, 512), f32), V((512, 512), f32), V((16, 512), f32),
                V((4, R, 512), f32), V((4, R, 512), bf16), V((2, 3072, 512), bf16),
                pltpu.SMEM((chains + 1,), jnp.int32), pltpu.SemaphoreType.DMA((7,)),
            ],
        ),
        out_shape=[S((2, 3072, 512), bf16), S((16, 512), f32)] + [S((rows, 512), bf16)] * 3 + [S((rows, 512), f32)],
        compiler_params=pltpu.CompilerParams(vmem_limit_bytes=62 << 20),
        name="live_rows",
    )(lengths, starts, ends, states, cotangent, q, k, v, wo, wi, wd, bias, vec)


def rest_kernel(
    SLOTS, K, STRIDE,
    g, small, x_ref, q_ref, k_ref, v_ref, len_ref, dq_ref, dk_ref, dv_ref, gf_ref, wqkv, wo, wi, wd, bias_ref, vec_ref,
    out, sout, y_ref, dx_ref, *bufs,
):
    step = pl.program_id(0)
    comm = Comm(K, g, small, out, sout, bufs, STRIDE)
    slots = SLOTS
    done = 0

    def slot(i):
        it = step * slots + i

        @pl.when(it < comm.iterations)
        def _():
            comm.iteration(it)

    @pl.when(step == 0)
    def _():
        comm.barrier()

    vec = vec_ref[...].astype(f32)
    bo, g1, s1, bd, g2, s2 = (vec[i : i + 1] for i in range(6))
    heads = lax.broadcasted_iota(jnp.int32, (4 * SEQ, 256), 1) // HEAD_DIM
    ctx = []
    for c in range(2):
        rows = slice(c * SEQ, c * SEQ + SEQ)
        length = len_ref[rows, 0:1]
        slot(c)
        parts = []
        for g_ in range(8):
            cols = slice(64 * g_, 64 * g_ + 64)
            scores = product_right(q_ref[rows, cols], k_ref[rows, cols])
            scores = jnp.where(lax.broadcasted_iota(jnp.int32, scores.shape, 1) < length, scores, -1e9)
            e = jnp.exp(scores - jnp.max(scores, axis=-1, keepdims=True))
            p = e * (1.0 / jnp.sum(e, axis=-1, keepdims=True))
            parts.append(product(p.astype(bf16), v_ref[rows, cols]))
        ctx.append(jnp.concatenate(parts, axis=1).astype(bf16))
    ctx = jnp.concatenate(ctx, axis=0)
    slot(2)
    s = x_ref[...].astype(f32) + (product(ctx[:, :256], wo[0]) + product(ctx[:, 256:], wo[1]) + bo)
    center = s - row_mean(s)
    normed = center * lax.rsqrt(row_mean(center * center) + EPSILON) * g1 + s1
    low = normed.astype(bf16)
    branch = bd
    for j in range(4):
        h, o = j // 2, 512 * (j % 2)
        bi = jnp.concatenate([bias_ref[h, 2 + o // 256 : 3 + o // 256], bias_ref[h, 3 + o // 256 : 4 + o // 256]], axis=1)
        hid = product(low, wi[h, :, o : o + 512]) + bi
        cdf, _ = normal_parts(hid)
        branch = branch + product((hid * cdf).astype(bf16), wd[h, o : o + 512])
        if j == 1:
            slot(3)
    s = normed + branch
    center = s - row_mean(s)
    y_ref[...] = (center * lax.rsqrt(row_mean(center * center) + EPSILON) * g2 + s2).astype(bf16)
    slot(4)
    dx = gf_ref[...]
    for h in range(2):
        cols = slice(256 * h, 256 * h + 256)
        for j, ref in enumerate((dq_ref, dk_ref, dv_ref)):
            dx = dx + product_right(ref[:, cols], wqkv[h, j])
    dx_ref[...] = dx

    @pl.when(step == pl.num_programs(0) - 1)
    def _():
        def body(it, carry):
            comm.iteration(it)
            return carry

        lax.fori_loop(slots * pl.num_programs(0), comm.iterations, body, 0)
        comm.finish()


def rest(g, small, states, q, k, v, lens, dq, dk, dv, gf, wqkv, wo, wi, wd, bias, vec):
    rows = states.shape[0]
    block = 2 * SEQ
    K, STRIDE, SLOTS = 8, 2, 5
    tile = pl.BlockSpec((block, 512), lambda i: (i, 0))
    whole = lambda a: pl.BlockSpec(a.shape, lambda i: (0,) * a.ndim)
    vm = pl.BlockSpec(memory_space=pltpu.VMEM)
    S = jax.ShapeDtypeStruct
    return pl.pallas_call(
        functools.partial(rest_kernel, SLOTS, K, STRIDE),
        grid=(rows // block,),
        in_specs=[vm, vm, tile, tile, tile, tile, pl.BlockSpec((block, 128), lambda i: (i, 0)), tile, tile, tile, tile,
                  whole(wqkv), whole(wo), whole(wi), whole(wd), whole(bias), whole(vec)],
        out_specs=[pl.BlockSpec(memory_space=pl.ANY), vm, tile, tile],
        out_shape=[S((ROWS, 512), bf16), S(small.shape, f32), S((rows, 512), bf16), S((rows, 512), f32)],
        scratch_shapes=Comm.scratch(K, small.shape[0]),
        compiler_params=pltpu.CompilerParams(collective_id=0, has_side_effects=True, vmem_limit_bytes=61 << 20),
        name="rest",
    )(g, small, states, q, k, v, lens, dq, dk, dv, gf, wqkv, wo, wi, wd, bias, vec)


def unpack_half(w):
    do = w[2560:3072, 256:]
    return dict(
        down=w[:1024], inner=jnp.concatenate([w[1024:1536], w[1536:2048]], axis=1),
        query=w[2048:2560, :256], key=w[2048:2560, 256:], value=w[2560:3072, :256],
        output=jnp.concatenate([do[:256], do[256:]], axis=1),
    )


def whole_chains(
    states, cotangent, lengths, span_starts, span_ends, query_weight, query_bias, key_weight, value_weight, value_bias,
    output_weight, output_bias, first_gain, first_shift, inner_weight, inner_bias, down_weight, down_bias, second_gain, second_shift,
):
    t = lax.axis_index("tensor")
    rows = states.shape[0]
    chains = rows // SEQ
    row = lambda a: a.reshape(1, -1)
    q, k, v, wqkv, wo, wi, wd, bias = gather(
        states, query_weight, key_weight, value_weight, row(query_bias), row(value_bias), row(inner_bias),
        output_weight, inner_weight, down_weight,
    )
    vec = jnp.stack([output_bias, first_gain, first_shift, down_bias, second_gain, second_shift] + [jnp.zeros((512,), bf16)] * 2)
    g, small, dq, dk, dv, gf = live_rows(lengths, span_starts, span_ends, states, cotangent, q, k, v, wo, wi, wd, bias, vec)
    mine = lax.dynamic_slice_in_dim(lengths, t * chains, chains)
    lens = jnp.broadcast_to(jnp.repeat(mine, SEQ)[:, None], (rows, 128))
    summed, small, output, input_grad = rest(g, small, states, q, k, v, lens, dq, dk, dv, gf, wqkv, wo, wi, wd, bias, vec)
    w = {name: part.astype(f32) for name, part in unpack_half(summed).items()}
    half = lambda line: lax.dynamic_slice_in_dim(line, t * 256, 256)
    return (
        output, input_grad, w["query"], half(small[6]), w["key"], w["value"], half(small[7]), w["output"],
        small[0], small[1], small[2], w["inner"], lax.dynamic_slice_in_dim(small[8:12].reshape(2048), t * 1024, 1024),
        w["down"], small[3], small[4], small[5],
    )


def local(*arguments):
    rows, hidden = arguments[0].shape[0], arguments[14].shape[1]
    if rows % SEQ == 0 and lax.axis_size("dp") == 16 and lax.axis_size("tensor") == 2:
        return whole_chains(*arguments)
    return general(*arguments)


def solution(mesh):
    placed = (
        P(("dp", "tensor"), None),
        P(("dp", "tensor"), None),
        P("dp"),
        P("dp"),
        P("dp"),
        P(None, "tensor"),
        P("tensor"),
        P(None, "tensor"),
        P(None, "tensor"),
        P("tensor"),
        P("tensor", None),
        P(),
        P(),
        P(),
        P(None, "tensor"),
        P("tensor"),
        P("tensor", None),
        P(),
        P(),
        P(),
    )
    return jax.shard_map(
        local,
        mesh=mesh,
        in_specs=placed,
        out_specs=(
            P(("dp", "tensor"), None),
            P(("dp", "tensor"), None),
            P(None, "tensor"),
            P("tensor"),
            P(None, "tensor"),
            P(None, "tensor"),
            P("tensor"),
            P("tensor", None),
            P(),
            P(),
            P(),
            P(None, "tensor"),
            P("tensor"),
            P("tensor", None),
            P(),
            P(),
            P(),
        ),
        check_vma=False,
    )
```

```python
import functools

import jax
import jax.numpy as jnp
from jax import lax
from jax.experimental import pallas as pl
from jax.experimental.pallas import tpu as pltpu
from jax.sharding import PartitionSpec as P

MESH = pl.DeviceIdType.MESH
f32, bf16 = jnp.float32, jnp.bfloat16
HEAD_DIM = 64
SEQ = 160
ROWS = 3072
SCALE = HEAD_DIM ** (-0.5)
ATT_BLOCK = 32
FFN_BLOCK = 256
EPSILON = 1e-12


def product(left, right):
    return jnp.dot(left, right, preferred_element_type=jnp.float32)


def product_left(left, right):
    return lax.dot_general(
        left, right, (((0,), (0,)), ((), ())), preferred_element_type=jnp.float32
    )


def product_right(left, right):
    return lax.dot_general(
        left, right, (((1,), (1,)), ((), ())), preferred_element_type=jnp.float32
    )


def layer_norm(values, gain, shift):
    center = values - jnp.mean(values, axis=-1, keepdims=True)
    spread = jnp.mean(center * center, axis=-1, keepdims=True)
    return center * lax.rsqrt(spread + EPSILON) * gain + shift


def exact_gelu(values):
    return jax.nn.gelu(values, approximate=False)


def attention_scores(queries, keys, key_live):
    scores = jnp.einsum(
        "cqhd,ckhd->chqk", queries, keys, preferred_element_type=jnp.float32
    ) * HEAD_DIM ** (-0.5)
    return jnp.where(key_live[:, None, None, :], scores, -1000000000.0)


def per_row(table, picker):
    return jnp.sum(jnp.where(picker, table[None, :], 0), axis=1)


def column_sum(values):
    return jnp.sum(values.astype(jnp.float32), axis=0)


def general(
    states,
    cotangent,
    lengths,
    span_starts,
    span_ends,
    query_weight,
    query_bias,
    key_weight,
    value_weight,
    value_bias,
    output_weight,
    output_bias,
    first_gain,
    first_shift,
    inner_weight,
    inner_bias,
    down_weight,
    down_bias,
    second_gain,
    second_shift,
):
    slice_rows = states.shape[0]
    chains = lengths.shape[0]
    group_rows = chains * SEQ
    heads_local = query_weight.shape[1] // HEAD_DIM
    layout = (chains, SEQ, heads_local, HEAD_DIM)
    whole = lax.all_gather(states, "tensor", axis=0, tiled=True)
    queries = (product(whole, query_weight) + query_bias).astype(jnp.bfloat16).reshape(layout)
    keys_low = product(whole, key_weight).astype(jnp.bfloat16).reshape(layout)
    values_low = (product(whole, value_weight) + value_bias).astype(jnp.bfloat16).reshape(layout)
    key_live = jnp.arange(SEQ, dtype=jnp.int32)[None, :] < lengths[:, None]
    scores = attention_scores(queries, keys_low, key_live)
    highest = jnp.max(scores, axis=-1, keepdims=True)
    logsum = highest + jnp.log(jnp.sum(jnp.exp(scores - highest), axis=-1, keepdims=True))
    probs_low = jnp.exp(scores - logsum).astype(jnp.bfloat16)
    context = jnp.einsum(
        "chqk,ckhd->cqhd", probs_low, values_low, preferred_element_type=jnp.float32
    )
    context = context.reshape(group_rows, heads_local * HEAD_DIM).astype(jnp.bfloat16)
    attended = lax.psum_scatter(
        product(context, output_weight), "tensor", scatter_dimension=0, tiled=True
    ) + output_bias.astype(jnp.float32)
    first_sum = states.astype(jnp.float32) + attended
    normed, first_pull = jax.vjp(
        layer_norm, first_sum, first_gain.astype(jnp.float32), first_shift.astype(jnp.float32)
    )
    normed_low = normed.astype(jnp.bfloat16)
    normed_all = lax.all_gather(normed_low, "tensor", axis=0, tiled=True)
    hidden = product(normed_all, inner_weight) + inner_bias.astype(jnp.float32)
    activation, gelu_pull = jax.vjp(exact_gelu, hidden)
    activation_low = activation.astype(jnp.bfloat16)
    branch = lax.psum_scatter(
        product(activation_low, down_weight), "tensor", scatter_dimension=0, tiled=True
    )
    second_sum = normed + (branch + down_bias.astype(jnp.float32))
    output, second_pull = jax.vjp(
        layer_norm, second_sum, second_gain.astype(jnp.float32), second_shift.astype(jnp.float32)
    )
    row_ids = lax.axis_index("tensor") * slice_rows + jnp.arange(slice_rows, dtype=jnp.int32)
    chain_ids = row_ids // SEQ
    position = row_ids % SEQ
    picker = chain_ids[:, None] == jnp.arange(chains, dtype=jnp.int32)[None, :]
    live = (
        (position >= per_row(span_starts, picker))
        & (position < per_row(span_ends, picker))
        & (position < per_row(lengths, picker))
    )
    grad_out = jnp.where(live[:, None], cotangent.astype(jnp.float32), 0.0)
    grad_second, second_gain_part, second_shift_part = second_pull(grad_out)
    grad_branch = grad_second.astype(jnp.bfloat16)
    down_bias_part = column_sum(grad_branch)
    grad_branch_all = lax.all_gather(grad_branch, "tensor", axis=0, tiled=True)
    down_weight_part = product_left(activation_low, grad_branch_all)
    grad_activation = product_right(grad_branch_all, down_weight)
    (grad_hidden,) = gelu_pull(grad_activation)
    grad_hidden_low = grad_hidden.astype(jnp.bfloat16)
    inner_weight_part = product_left(normed_all, grad_hidden_low)
    inner_bias_part = column_sum(grad_hidden_low)
    grad_normed = lax.psum_scatter(
        product_right(grad_hidden_low, inner_weight), "tensor", scatter_dimension=0, tiled=True
    )
    grad_first, first_gain_part, first_shift_part = first_pull(grad_second + grad_normed)
    grad_attended = grad_first.astype(jnp.bfloat16)
    output_bias_part = column_sum(grad_attended)
    grad_attended_all = lax.all_gather(grad_attended, "tensor", axis=0, tiled=True)
    output_weight_part = product_left(context, grad_attended_all)
    grad_context = (
        product_right(grad_attended_all, output_weight).astype(jnp.bfloat16).reshape(layout)
    )
    probs = jnp.exp(attention_scores(queries, keys_low, key_live) - logsum)
    grad_probs = jnp.einsum(
        "cqhd,ckhd->chqk", grad_context, values_low, preferred_element_type=jnp.float32
    )
    grad_scores = probs * (grad_probs - jnp.sum(probs * grad_probs, axis=-1, keepdims=True))
    grad_scores_low = grad_scores.astype(jnp.bfloat16)
    scale = HEAD_DIM ** (-0.5)
    grad_queries = (
        jnp.einsum("chqk,ckhd->cqhd", grad_scores_low, keys_low, preferred_element_type=jnp.float32)
        * scale
    )
    grad_keys = (
        jnp.einsum("chqk,cqhd->ckhd", grad_scores_low, queries, preferred_element_type=jnp.float32)
        * scale
    )
    grad_values = jnp.einsum(
        "chqk,cqhd->ckhd", probs_low, grad_context, preferred_element_type=jnp.float32
    )
    flat = (group_rows, heads_local * HEAD_DIM)
    grad_queries = grad_queries.reshape(flat).astype(jnp.bfloat16)
    grad_keys = grad_keys.reshape(flat).astype(jnp.bfloat16)
    grad_values = grad_values.reshape(flat).astype(jnp.bfloat16)
    query_weight_part = product_left(whole, grad_queries)
    key_weight_part = product_left(whole, grad_keys)
    value_weight_part = product_left(whole, grad_values)
    query_bias_part = column_sum(grad_queries)
    value_bias_part = column_sum(grad_values)
    grad_whole = (
        product_right(grad_queries, query_weight)
        + product_right(grad_keys, key_weight)
        + product_right(grad_values, value_weight)
    )
    input_grad = (
        lax.psum_scatter(
            grad_whole.astype(jnp.bfloat16), "tensor", scatter_dimension=0, tiled=True
        ).astype(jnp.float32)
        + grad_first
    )
    (
        query_weight_grad,
        query_bias_grad,
        key_weight_grad,
        value_weight_grad,
        value_bias_grad,
        output_weight_grad,
        inner_weight_grad,
        inner_bias_grad,
        down_weight_grad,
    ) = (
        lax.psum(query_weight_part.astype(jnp.bfloat16), "dp").astype(jnp.float32),
        lax.psum(query_bias_part.astype(jnp.bfloat16), "dp").astype(jnp.float32),
        lax.psum(key_weight_part.astype(jnp.bfloat16), "dp").astype(jnp.float32),
        lax.psum(value_weight_part.astype(jnp.bfloat16), "dp").astype(jnp.float32),
        lax.psum(value_bias_part.astype(jnp.bfloat16), "dp").astype(jnp.float32),
        lax.psum(output_weight_part.astype(jnp.bfloat16), "dp").astype(jnp.float32),
        lax.psum(inner_weight_part.astype(jnp.bfloat16), "dp").astype(jnp.float32),
        lax.psum(inner_bias_part.astype(jnp.bfloat16), "dp").astype(jnp.float32),
        lax.psum(down_weight_part.astype(jnp.bfloat16), "dp").astype(jnp.float32),
    )
    (
        output_bias_grad,
        first_gain_grad,
        first_shift_grad,
        down_bias_grad,
        second_gain_grad,
        second_shift_grad,
    ) = lax.psum(
        (
            output_bias_part,
            first_gain_part,
            first_shift_part,
            down_bias_part,
            second_gain_part,
            second_shift_part,
        ),
        ("dp", "tensor"),
    )
    return (
        output.astype(jnp.bfloat16),
        input_grad,
        query_weight_grad,
        query_bias_grad,
        key_weight_grad,
        value_weight_grad,
        value_bias_grad,
        output_weight_grad,
        output_bias_grad,
        first_gain_grad,
        first_shift_grad,
        inner_weight_grad,
        inner_bias_grad,
        down_weight_grad,
        down_bias_grad,
        second_gain_grad,
        second_shift_grad,
    )


class Comm:
    NSTAGE = 10
    def __init__(self, K, g, small, out, sout, bufs, stride=1):
        self.stride = stride
        self.K = K; self.CH = ROWS // K; self.SB = self.CH // 3
        self.g, self.small, self.out_hbm, self.sout = g, small, out, sout
        (self.core_buf, self.acc, self.r1, self.r2, self.r3, self.r4, self.out, self.sm, self.csem, self.rsem, self.asem, self.smsem, self.fsem) = bufs
        dp = lax.axis_index("dp"); t = lax.axis_index("tensor")
        self.t = t
        x = lax.rem(dp, 2); y = lax.rem(dp // 2, 2); p = lax.rem(dp // 4, 2); q = dp // 8
        self.bits = (x, y, p, q)
        self.parts = tuple(dp + w * (1 - 2 * b) for w, b in ((1, x), (2, y), (4, p), (8, q)))
        self.dp = dp
    def barrier(self):
        b = pltpu.get_barrier_semaphore()
        pl.semaphore_signal(b, inc=1, device_id=(self.dp, 1 - self.t), device_id_type=MESH)
        for n in self.parts:
            pl.semaphore_signal(b, inc=1, device_id=(n, self.t), device_id_type=MESH)
        pl.semaphore_wait(b, 5)
    def rc(self, src, dst, s, r, n):
        return pltpu.make_async_remote_copy(src_ref=src, dst_ref=dst, send_sem=s, recv_sem=r, device_id=(n, self.t), device_id_type=MESH)
    def core_copy(self, k):
        return pltpu.make_async_remote_copy(src_ref=self.g.at[1 - self.t, pl.ds(k * self.CH, self.CH)], dst_ref=self.core_buf.at[k],
            send_sem=self.csem.at[0, k], recv_sem=self.csem.at[1, k], device_id=(self.dp, 1 - self.t), device_id_type=MESH)
    def order(self, k, r):
        B, N = self.bits, self.parts
        X, Y, Pp, Qq = ((B[i], N[i]) for i in range(4))
        if r == 0: return X, Y, Pp, Qq
        if r == 1: return Y, X, Pp, Qq
        even = lax.rem(k, 2) == 0
        U = (jnp.where(even, B[0], B[1]), jnp.where(even, N[0], N[1]))
        V = (jnp.where(even, B[1], B[0]), jnp.where(even, N[1], N[0]))
        return Pp, U, V, Qq
    def region(self, k, r, depth, keep):
        o = self.order(k, r)
        rows, cols = self.SB, 512
        r0, c0 = k * self.CH + r * self.SB, 0
        for i in range(depth):
            b = o[i][0]
            if i == depth - 1 and not keep: b = 1 - b
            if i < 2:
                rows //= 2; r0 = r0 + b * rows
            else:
                cols //= 2; c0 = c0 + b * cols
        if depth > 2: c0 = pl.multiple_of(c0, 128)
        return pl.ds(pl.multiple_of(r0, 16), rows), pl.ds(c0, cols)
    def rs(self, k, r, i):
        n = self.order(k, r)[i][1]
        buf = (self.r1, self.r2, self.r3, self.r4)[i]
        return self.rc(self.acc.at[self.region(k, r, i + 1, False)], buf.at[k, r], self.rsem.at[0, i, k, r], self.rsem.at[1, i, k, r], n)
    def ag(self, k, r, i):
        n = self.order(k, r)[i][1]
        sl = self.region(k, r, i + 1, True)
        return self.rc(self.out.at[sl], self.out.at[sl], self.asem.at[0, i, k, r], self.asem.at[1, i, k, r], n)
    def small_copy(self, i):
        dev = (self.dp, 1 - self.t) if i == 0 else (self.parts[i - 1], self.t)
        src = self.small if i == 0 else self.sm.at[1, i - 1]
        return pltpu.make_async_remote_copy(src_ref=src, dst_ref=self.sm.at[0, i], send_sem=self.smsem.at[0, i], recv_sem=self.smsem.at[1, i], device_id=dev, device_id_type=MESH)
    def stage(self, s, k):
        if s == 0:
            self.core_copy(k).start()
        elif s == 1:
            self.core_copy(k).wait_recv()
            sl = pl.ds(pl.multiple_of(k * self.CH, 16), self.CH)
            self.acc[sl] = (self.g[self.t, sl].astype(f32) + self.core_buf[k].astype(f32)).astype(bf16)
            for r in range(3): self.rs(k, r, 0).start()
        elif s <= 5:
            i = s - 2
            buf = (self.r1, self.r2, self.r3, self.r4)[i]
            for r in range(3):
                self.rs(k, r, i).wait_recv()
                sl = self.region(k, r, i + 1, True)
                v = (self.acc[sl].astype(f32) + buf[k, r].astype(f32)).astype(bf16)
                if i < 3:
                    self.acc[sl] = v
                    self.rs(k, r, i + 1).start()
                else:
                    self.out[sl] = v
                    self.ag(k, r, 3).start()
        else:
            i = 9 - s
            for r in range(3):
                self.ag(k, r, i).wait_recv()
                if i > 0: self.ag(k, r, i - 1).start()
            if i == 0: self.final_copy(k).start()
    def final_copy(self, k):
        sl = pl.ds(k * self.CH, self.CH)
        return pltpu.make_async_copy(self.out.at[sl], self.out_hbm.at[sl], self.fsem.at[k])
    def small_stage(self, i):
        if i > 0:
            self.small_copy(i - 1).wait_recv()
            own = self.small[...] if i == 1 else self.sm[1, i - 2]
            v = own + self.sm[0, i - 1]
            if i < 5: self.sm[1, i - 1] = v
            else: self.sout[...] = v
        if i < 5: self.small_copy(i).start()
    def iteration(self, it):
        for s in reversed(range(self.NSTAGE)):
            k = it - s * self.stride
            @pl.when((k >= 0) & (k < self.K))
            def _(s=s, k=k):
                self.stage(s, k)
        for i in range(6):
            @pl.when(it == i * self.stride + 1)
            def _(i=i): self.small_stage(i)
    @property
    def iterations(self): return self.K + (self.NSTAGE - 1) * self.stride
    def finish(self):
        def body(k, c):
            self.core_copy(k).wait_send(); self.final_copy(k).wait()
            for r in range(3):
                for i in range(4):
                    self.rs(k, r, i).wait_send(); self.ag(k, r, i).wait_send()
            return c
        lax.fori_loop(0, self.K, body, 0)
        for i in range(5): self.small_copy(i).wait_send()
    @staticmethod
    def scratch(K, S):
        SB = ROWS // K // 3
        D = pltpu.SemaphoreType.DMA
        return [pltpu.VMEM((K, 3 * SB, 512), bf16), pltpu.VMEM((ROWS, 512), bf16),
            pltpu.VMEM((K, 3, SB // 2, 512), bf16), pltpu.VMEM((K, 3, SB // 4, 512), bf16),
            pltpu.VMEM((K, 3, SB // 4, 256), bf16), pltpu.VMEM((K, 3, SB // 4, 128), bf16),
            pltpu.VMEM((ROWS, 512), bf16), pltpu.VMEM((2, 5, S, 512), f32),
            D((2, K)), D((2, 4, K, 3)), D((2, 4, K, 3)), D((2, 5)), D((K,))]


def gather_kernel(
    x_ref, wq_ref, wk_ref, wv_ref, bq_ref, bv_ref, bi_ref, wo_ref, wi_ref, wd_ref,
    q_ref, k_ref, v_ref, wqkv_out, wo_out, wi_out, wd_out, bias_out,
    wqkv, wo, wi, wd, bias, near, sent, came,
):
    step = pl.program_id(0)
    dp, t = lax.axis_index("dp"), lax.axis_index("tensor")

    def pair(i, src, dst):
        return pltpu.make_async_remote_copy(
            src_ref=src, dst_ref=dst, send_sem=sent.at[i], recv_sem=came.at[i],
            device_id=(dp, 1 - t), device_id_type=MESH,
        )

    first = [
        pair(0, wq_ref, wqkv.at[t, 0]), pair(1, wk_ref, wqkv.at[t, 1]), pair(2, wv_ref, wqkv.at[t, 2]),
        pair(3, bias.at[t], bias.at[t]),
    ]
    later = [pair(4, wo.at[t], wo.at[t]), pair(5, wi.at[t], wi.at[t]), pair(6, wd.at[t], wd.at[t])]
    own = [pltpu.make_async_copy(a, b.at[t], near.at[i]) for i, (a, b) in enumerate(((wo_ref, wo), (wi_ref, wi), (wd_ref, wd)))]
    keep = [pltpu.make_async_copy(wqkv, wqkv_out, near.at[3]), pltpu.make_async_copy(bias, bias_out, near.at[4])]
    keep_later = [pltpu.make_async_copy(a, b, near.at[5 + i]) for i, (a, b) in enumerate(((wo, wo_out), (wi, wi_out), (wd, wd_out)))]

    @pl.when(step == 0)
    def _():
        barrier = pltpu.get_barrier_semaphore()
        pl.semaphore_signal(barrier, inc=1, device_id=(dp, 1 - t), device_id_type=MESH)
        bias[t, 0:1] = bq_ref[...].astype(f32)
        bias[t, 1:2] = bv_ref[...].astype(f32)
        for i in range(4):
            bias[t, 2 + i : 3 + i] = bi_ref[:, 256 * i : 256 * i + 256].astype(f32)
        bias[t, 6:8] = jnp.zeros((2, 256), f32)
        for copy in own:
            copy.start()
        pl.semaphore_wait(barrier, 1)
        for copy in first:
            copy.start()
        for j, ref in enumerate((wq_ref, wk_ref, wv_ref)):
            wqkv[t, j] = ref[...]
        for copy in first:
            copy.wait_recv()
        for copy in keep:
            copy.start()
        for mine, copy in zip(own, later):
            mine.wait()
            copy.start()

    x = x_ref[...]
    for h in range(2):
        cols = slice(256 * h, 256 * h + 256)
        q_ref[:, cols] = ((product(x, wqkv[h, 0]) + bias[h, 0:1]).astype(bf16).astype(f32) * SCALE).astype(bf16)
        k_ref[:, cols] = product(x, wqkv[h, 1]).astype(bf16)
        v_ref[:, cols] = (product(x, wqkv[h, 2]) + bias[h, 1:2]).astype(bf16)

    @pl.when(step == pl.num_programs(0) // 2)
    def _():
        for copy, out in zip(later, keep_later):
            copy.wait_recv()
            out.start()

    @pl.when(step == pl.num_programs(0) - 1)
    def _():
        for copy in first:
            copy.wait_send()
        for copy in later:
            copy.wait_send()
        for copy in keep + keep_later:
            copy.wait()


def gather(states, wq, wk, wv, bq, bv, bi, wo, wi, wd):
    rows = states.shape[0]
    block = 2 * SEQ
    whole = lambda a: pl.BlockSpec(a.shape, lambda i: (0,) * a.ndim)
    tile = pl.BlockSpec((block, 512), lambda i: (i, 0))
    hbm = pl.BlockSpec(memory_space=pl.ANY)
    D = pltpu.SemaphoreType.DMA
    S = jax.ShapeDtypeStruct
    return pl.pallas_call(
        gather_kernel,
        grid=(rows // block,),
        in_specs=[tile, whole(wq), whole(wk), whole(wv), whole(bq), whole(bv), whole(bi), hbm, hbm, hbm],
        out_specs=[tile, tile, tile, hbm, hbm, hbm, hbm, hbm],
        out_shape=[S((rows, 512), bf16)] * 3 + [
            S((2, 3, 512, 256), bf16), S((2, 256, 512), bf16), S((2, 512, 1024), bf16), S((2, 1024, 512), bf16), S((2, 8, 256), f32),
        ],
        scratch_shapes=[
            pltpu.VMEM((2, 3, 512, 256), bf16), pltpu.VMEM((2, 256, 512), bf16), pltpu.VMEM((2, 512, 1024), bf16),
            pltpu.VMEM((2, 1024, 512), bf16), pltpu.VMEM((2, 8, 256), f32), D((8,)), D((7,)), D((7,)),
        ],
        compiler_params=pltpu.CompilerParams(collective_id=1, has_side_effects=True, vmem_limit_bytes=60 << 20),
        name="gather",
    )(states, wq, wk, wv, bq, bv, bi, wo, wi, wd)


def normal_cdf(h):
    return 0.5 + 0.5 * lax.erf(h * 0.7071067811865476)


def inverse(a):
    return pltpu.reciprocal(a, approx=True)


def row_mean(a):
    return jnp.sum(a, axis=-1, keepdims=True) * (1.0 / 512)


WINDOW = 64
FRONT = 8


def live_kernel(
    len_ref, start_ref, end_ref,
    x_hbm, cot_hbm, q_hbm, k_hbm, v_hbm, wqkv_hbm, wo_hbm, wi_hbm, wd_hbm, bias_ref, vec_ref,
    g_out, dk_out, dv_out, dx_out, small_out,
    x_all, cot_all, q_all, k_all, v_all, wq, wo, wi, wd, context, inputs, upstream, first, dv_all, acc_k, acc_v,
    acc_d, acc_i, acc_o, gelu_grad, act, stage, win_chain, win_pos, win_dst, chain_win, in_sems, w_sems, out_sems, dx_sems,
):
    chains = len_ref.shape[0] // 2
    t = lax.axis_index("tensor")
    W, R = WINDOW, FFN_BLOCK
    half = chains // 2
    rows_all = chains * SEQ
    dk_all = cot_all
    spread = gelu_grad

    def chain_loads(c):
        rows = pl.ds(c * SEQ, SEQ)
        return [
            pltpu.make_async_copy(a.at[rows], b.at[rows], in_sems.at[i, c])
            for i, (a, b) in enumerate(((q_hbm, q_all), (k_hbm, k_all), (v_hbm, v_all), (cot_hbm, cot_all), (x_hbm, x_all)))
        ]

    loads = [
        pltpu.make_async_copy(a, b, w_sems.at[i])
        for i, (a, b) in enumerate((
            (wo_hbm, wo), (wi_hbm, wi), (wd_hbm, wd), (wqkv_hbm.at[0, 0], wq.at[0]), (wqkv_hbm.at[1, 0], wq.at[1]),
        ))
    ]

    def start_loads(c, carry):
        for copy in chain_loads(c):
            copy.start()
        return carry

    lax.fori_loop(0, chains, start_loads, 0)
    for copy in loads:
        copy.start()

    def list_chain(c, carry):
        at, offset = carry
        start = start_ref[t * chains + c]
        end = jnp.minimum(end_ref[t * chains + c], len_ref[t * chains + c])
        r16 = (start // 16) * 16
        r8 = (start // 8) * 8
        count = jnp.maximum((end - r16 + W - 1) // W, 1)
        chain_win[c] = at

        def put(i, carry):
            win_chain[at + i] = c
            win_pos[at + i] = r16 + W * i
            win_dst[at + i] = offset + r16 - r8 + W * i
            return carry

        lax.fori_loop(0, count, put, 0)
        return at + count, offset + jnp.maximum(((end + 7) // 8) * 8 - r8, 0)

    n_win, n_end = lax.fori_loop(0, chains, list_chain, (0, FRONT))
    chain_win[chains] = n_win
    trash = context.shape[0] - W
    win_chain[n_win] = chains - 1
    win_pos[n_win] = SEQ
    win_dst[n_win] = trash
    n = n_end - FRONT

    acc_d[...] = jnp.zeros_like(acc_d)
    acc_i[...] = jnp.zeros_like(acc_i)
    acc_o[...] = jnp.zeros_like(acc_o)
    acc_k[...] = jnp.zeros_like(acc_k)
    acc_v[...] = jnp.zeros_like(acc_v)
    small_out[...] = jnp.zeros_like(small_out)
    for ref in (context, upstream, first):
        ref[pl.ds(trash, W)] = jnp.zeros((W, 512), f32)
    for ref in (x_all, cot_all, q_all):
        ref[pl.ds(rows_all, W)] = jnp.zeros((W, 512), bf16)

    lane_head = lax.broadcasted_iota(jnp.int32, (W, 256), 1) // HEAD_DIM
    own = lax.broadcasted_iota(jnp.int32, (4 * W, 256), 1) // HEAD_DIM == lax.broadcasted_iota(jnp.int32, (4 * W, 256), 0) // W
    key_row = lax.broadcasted_iota(jnp.int32, (SEQ, 4 * W), 0)
    row_id = lax.broadcasted_iota(jnp.int32, (W, 512), 0)

    def heads_apart(rows):
        return jnp.where(own, jnp.concatenate([rows] * 4, axis=0), jnp.zeros((), bf16))

    def heads_together(full):
        out = full[3 * W :]
        for h in (2, 1, 0):
            out = jnp.where(lane_head == h, full[h * W : (h + 1) * W], out)
        return out

    def window(i):
        c = win_chain[i]
        pos = win_pos[i]
        start = start_ref[t * chains + c]
        length = len_ref[t * chains + c]
        end = jnp.minimum(end_ref[t * chains + c], length)
        src = pl.ds(pl.multiple_of(c * SEQ + pos, 16), W)
        dst = pl.multiple_of(win_dst[i], 8)
        keys = pl.ds(pl.multiple_of(c * SEQ, 32), SEQ)
        live = (row_id + pos >= start) & (row_id + pos < end)
        whole = pos + 8 > start
        return c, pos, length, src, dst, keys, live, whole

    def put_rows(ref, dst, whole, rows):
        head = pl.ds(dst, 8)
        ref[head] = jnp.where(whole, rows[:8], ref[head])
        ref[pl.ds(pl.multiple_of(dst + 8, 8), W - 8)] = rows[8:]

    def probabilities(qs, k, length):
        scores = product_right(k, qs)
        scores = jnp.where(key_row < length, scores, -1e9)
        e = jnp.exp(scores - jnp.max(scores, axis=0, keepdims=True))
        return e * inverse(jnp.sum(e, axis=0, keepdims=True))

    def forward(i, waited):
        last = win_chain[2 * i + 1]

        def wait_chain(c, carry):
            for copy in chain_loads(c):
                copy.wait()
            return carry

        lax.fori_loop(waited, last + 1, wait_chain, 0)
        done = []
        for u in range(2):
            c, pos, length, src, dst, keys, live, whole = window(2 * i + u)
            q = q_all[src]
            out = []
            for g in range(2):
                cols = slice(256 * g, 256 * g + 256)
                p = probabilities(heads_apart(q[:, cols]), k_all[keys, cols], length)
                out.append(heads_together(product_left(p.astype(bf16), v_all[keys, cols])))
            done.append((jnp.concatenate(out, axis=1), x_all[src].astype(f32), jnp.where(live, cot_all[src].astype(f32), 0.0), dst, whole))
        for ctx, x, cot, dst, whole in done:
            put_rows(context, dst, whole, ctx)
            put_rows(inputs, dst, whole, x)
            put_rows(upstream, dst, whole, cot)
        return last + 1

    steps = (n_win + 1) // 2
    waited = lax.fori_loop(0, steps, forward, 0)

    tail = pl.ds(pl.multiple_of(n_end, 8), R)
    for ref in (context, inputs, upstream):
        ref[tail] = jnp.zeros((R, 512), f32)
    for copy in loads:
        copy.wait()
    vec = vec_ref[...].astype(f32)
    bo, g1, s1, bd, g2, s2 = (vec[i : i + 1] for i in range(6))
    blocks = (n + R - 1) // R

    def feed_forward(b, carry):
        rows = pl.ds(pl.multiple_of(FRONT + b * R, 8), R)
        ctx = context[rows].astype(bf16)
        attended = product(ctx[:, :256], wo[0]) + product(ctx[:, 256:], wo[1]) + bo
        s = inputs[rows] + attended
        center = s - row_mean(s)
        rstd1 = lax.rsqrt(row_mean(center * center) + EPSILON)
        hat1 = center * rstd1
        normed = hat1 * g1 + s1
        low = normed.astype(bf16)
        branch = jnp.zeros((R, 512), f32) + bd
        for j in range(4):
            h, o = j // 2, 512 * (j % 2)
            bi = jnp.concatenate([bias_ref[h, 2 + o // 256 : 3 + o // 256], bias_ref[h, 3 + o // 256 : 4 + o // 256]], axis=1)
            hid = product(low, wi[h, :, o : o + 512]) + bi
            cdf = normal_cdf(hid)
            a = (hid * cdf).astype(bf16)
            gelu_grad[j] = cdf + hid * (0.3989422804014327 * jnp.exp(-0.5 * hid * hid))
            act[j] = a
            branch = branch + product(a, wd[h, o : o + 512])
        s = normed + branch
        center = s - row_mean(s)
        rstd2 = lax.rsqrt(row_mean(center * center) + EPSILON)
        hat2 = center * rstd2
        up = upstream[rows]
        gy = up * g2
        grad = rstd2 * (gy - row_mean(gy) - hat2 * row_mean(gy * hat2))
        gb = grad.astype(bf16)
        gn = grad
        for j in range(4):
            h, o = j // 2, 512 * (j % 2)
            gh = (product_right(gb, wd[h, o : o + 512]) * gelu_grad[j]).astype(bf16)
            acc_d[h, o : o + 512] += product_left(act[j], gb)
            acc_i[j] += product_left(low, gh)
            small_out[8 + j : 9 + j] += jnp.sum(gh.astype(f32), axis=0, keepdims=True)
            gn = gn + product_right(gh, wi[h, :, o : o + 512])
        small_out[1:2] += jnp.sum(gn * hat1, axis=0, keepdims=True)
        small_out[2:3] += jnp.sum(gn, axis=0, keepdims=True)
        small_out[3:4] += jnp.sum(gb.astype(f32), axis=0, keepdims=True)
        small_out[4:5] += jnp.sum(up * hat2, axis=0, keepdims=True)
        small_out[5:6] += jnp.sum(up, axis=0, keepdims=True)
        gy = gn * g1
        grad = rstd1 * (gy - row_mean(gy) - hat1 * row_mean(gy * hat1))
        first[rows] = grad
        ga = grad.astype(bf16)
        small_out[0:1] += jnp.sum(ga.astype(f32), axis=0, keepdims=True)
        acc_o[...] += product_left(ctx, ga)
        upstream[rows] = jnp.concatenate([product_right(ga, wo[0]), product_right(ga, wo[1])], axis=1)
        return carry

    lax.fori_loop(0, blocks, feed_forward, 0)

    def out_copy(h, part):
        rows = pl.ds(0, 2048) if part == 0 else pl.ds(2048, 1024)
        return pltpu.make_async_copy(stage.at[h, rows], g_out.at[h, rows], out_sems.at[2 * part + h])

    for h in range(2):
        stage[h, 0:1024] = acc_d[h].astype(bf16)
        stage[h, 1024:1536] = acc_i[2 * h].astype(bf16)
        stage[h, 1536:2048] = acc_i[2 * h + 1].astype(bf16)
        out_copy(h, 0).start()
        stage[h, 2560:2816, 256:512] = acc_o[256 * h : 256 * h + 256, 0:256].astype(bf16)
        stage[h, 2816:3072, 256:512] = acc_o[256 * h : 256 * h + 256, 256:512].astype(bf16)

    def backward(i, carry):
        done = []
        for u in range(2):
            c, pos, length, src, dst, keys, live, whole = window(2 * i + u)
            same = jnp.where((i + u > 0) & (win_chain[jnp.maximum(2 * i + u - 1, 0)] == c), 1.0, 0.0)
            q = q_all[src]
            gc = jnp.where(live, upstream[pl.ds(dst, W)], 0.0).astype(bf16)
            out = []
            for g in range(2):
                cols = slice(256 * g, 256 * g + 256)
                qs, gs = heads_apart(q[:, cols]), heads_apart(gc[:, cols])
                p = probabilities(qs, k_all[keys, cols], length)
                gp = product_right(v_all[keys, cols], gs)
                ds = (p * (gp - jnp.sum(p * gp, axis=0, keepdims=True))).astype(bf16)
                dk = acc_k[:, cols] * same + product(ds, qs)
                dv = acc_v[:, cols] * same + product(p.astype(bf16), gs)
                acc_k[:, cols] = dk
                acc_v[:, cols] = dv
                dk_all[keys, cols] = dk.astype(bf16)
                dv_all[keys, cols] = dv.astype(bf16)
                out.append(heads_together(product_left(ds, k_all[keys, cols])) * SCALE)
            done.append((jnp.concatenate(out, axis=1), dst, whole))
        for dq, dst, whole in done:
            put_rows(context, dst, whole, dq)
        return carry

    lax.fori_loop(0, steps, backward, 0)
    keep = [
        pltpu.make_async_copy(dk_all.at[pl.ds(0, rows_all)], dk_out, out_sems.at[4]),
        pltpu.make_async_copy(dv_all, dv_out, out_sems.at[5]),
    ]
    for copy in keep:
        copy.start()
    context[tail] = jnp.zeros((R, 512), f32)
    acc_o[...] = jnp.zeros_like(acc_o)

    def query_weight(b, carry):
        rows = pl.ds(pl.multiple_of(FRONT + b * R, 8), R)
        dq = context[rows].astype(bf16)
        acc_o[...] += product_left(inputs[rows].astype(bf16), dq)
        small_out[6:7] += jnp.sum(dq.astype(f32), axis=0, keepdims=True)
        first[rows] = first[rows] + (product_right(dq[:, :256], wq[0]) + product_right(dq[:, 256:], wq[1]))
        return carry

    lax.fori_loop(0, blocks, query_weight, 0)
    small_out[7:8] = jnp.sum(dv_all[...].astype(f32), axis=0, keepdims=True)
    part = 4 * SEQ if chains % 4 == 0 else rows_all // 2

    def key_value_weight(b, carry):
        rows = pl.ds(pl.multiple_of(b * part, 32), part)
        x = x_all[rows]
        dk = product_left(x, dk_all[rows])
        dv = product_left(x, dv_all[rows])
        keep = jnp.where(b > 0, 1.0, 0.0)
        acc_d[0, 0:512] = acc_d[0, 0:512] * keep + dk
        acc_d[1, 0:512] = acc_d[1, 0:512] * keep + dv
        return carry

    lax.fori_loop(0, rows_all // part, key_value_weight, 0)
    dk, dv = acc_d[0, 0:512], acc_d[1, 0:512]
    for h in range(2):
        cols = slice(256 * h, 256 * h + 256)
        stage[h, 2048:2560, 0:256] = acc_o[:, cols].astype(bf16)
        stage[h, 2048:2560, 256:512] = dk[:, cols].astype(bf16)
        stage[h, 2560:3072, 0:256] = dv[:, cols].astype(bf16)
        out_copy(h, 1).start()

    def chain_out(c, slot):
        return pltpu.make_async_copy(spread.at[slot, pl.ds(0, SEQ)], dx_out.at[pl.ds(c * SEQ, SEQ)], dx_sems.at[slot])

    def scatter(i, carry):
        for slot in range(2):
            c = 2 * i + slot

            @pl.when(i > 0)
            def _():
                chain_out(c - 2, slot).wait()

            spread[slot, 0 : SEQ + W] = jnp.zeros((SEQ + W, 512), f32)

            def put(j, carry):
                _, pos, _, _, dst, _, live, _ = window(j)
                spread[slot, pl.ds(pl.multiple_of(pos, 16), W)] = jnp.where(live, first[pl.ds(dst, W)], 0.0)
                return carry

            lax.fori_loop(chain_win[c], chain_win[c + 1], put, 0)
            chain_out(c, slot).start()
        return carry

    lax.fori_loop(0, half, scatter, 0)
    for slot in range(2):
        chain_out(chains - 2 + slot, slot).wait()
    for copy in keep:
        copy.wait()
    for h in range(2):
        out_copy(h, 0).wait()
        out_copy(h, 1).wait()


def live_rows(lengths, starts, ends, states, cotangent, q, k, v, wqkv, wo, wi, wd, bias, vec):
    rows = states.shape[0]
    chains = rows // SEQ
    R, W = FFN_BLOCK, WINDOW
    C = -(-(FRONT + rows + R + W) // 8) * 8
    windows = 3 * chains + 2
    hbm, vm, sm = (pl.BlockSpec(memory_space=s) for s in (pl.ANY, pltpu.VMEM, pltpu.SMEM))
    S, V, D, M = jax.ShapeDtypeStruct, pltpu.VMEM, pltpu.SemaphoreType.DMA, pltpu.SMEM
    return pl.pallas_call(
        live_kernel,
        in_specs=[sm] * 3 + [hbm] * 9 + [vm, vm],
        out_specs=[hbm] * 4 + [vm],
        scratch_shapes=[
            V((rows + W, 512), bf16), V((rows + W, 512), bf16), V((rows + W, 512), bf16), V((rows, 512), bf16), V((rows, 512), bf16),
            V((2, 512, 256), bf16), V((2, 256, 512), bf16), V((2, 512, 1024), bf16), V((2, 1024, 512), bf16),
            V((C, 512), f32), V((C, 512), f32), V((C, 512), f32), V((C, 512), f32),
            V((rows, 512), bf16), V((SEQ, 512), f32), V((SEQ, 512), f32),
            V((2, 1024, 512), f32), V((4, 512, 512), f32), V((512, 512), f32),
            V((4, R, 512), f32), V((4, R, 512), bf16), V((2, 3072, 512), bf16),
            M((windows,), jnp.int32), M((windows,), jnp.int32), M((windows,), jnp.int32), M((chains + 1,), jnp.int32),
            D((5, chains)), D((5,)), D((6,)), D((2,)),
        ],
        out_shape=[S((2, ROWS, 512), bf16), S((rows, 512), bf16), S((rows, 512), bf16), S((rows, 512), f32), S((16, 512), f32)],
        compiler_params=pltpu.CompilerParams(vmem_limit_bytes=62 << 20),
        name="live_rows",
    )(lengths, starts, ends, states, cotangent, q, k, v, wqkv, wo, wi, wd, bias, vec)


def rest_kernel(
    SLOTS, K, STRIDE,
    g, small, x_ref, q_ref, k_ref, v_ref, len_ref, dk_ref, dv_ref, gf_ref, wqkv, wo, wi, wd, bias_ref, vec_ref,
    out, sout, y_ref, dx_ref, *bufs,
):
    step = pl.program_id(0)
    comm = Comm(K, g, small, out, sout, bufs, STRIDE)
    slots = SLOTS
    done = 0

    def slot(i):
        it = step * slots + i

        @pl.when(it < comm.iterations)
        def _():
            comm.iteration(it)

    @pl.when(step == 0)
    def _():
        comm.barrier()

    vec = vec_ref[...].astype(f32)
    bo, g1, s1, bd, g2, s2 = (vec[i : i + 1] for i in range(6))
    low_lane = lax.broadcasted_iota(jnp.int32, (SEQ, 128), 1) < HEAD_DIM
    key_row = lax.broadcasted_iota(jnp.int32, (SEQ, SEQ), 0)
    ctx = []
    for c in range(2):
        rows = slice(c * SEQ, c * SEQ + SEQ)
        length = len_ref[c * SEQ : c * SEQ + 1, 0:1]
        slot(c)
        parts = []
        for pair in range(4):
            cols = slice(128 * pair, 128 * pair + 128)
            qp, kp, vp = q_ref[rows, cols], k_ref[rows, cols], v_ref[rows, cols]
            outs = []
            for h in range(2):
                scores = product_right(jnp.where(low_lane == (h == 0), kp, jnp.zeros((), bf16)), qp)
                scores = jnp.where(key_row < length, scores, -1e9)
                e = jnp.exp(scores - jnp.max(scores, axis=0, keepdims=True))
                p = (e * inverse(jnp.sum(e, axis=0, keepdims=True))).astype(bf16)
                outs.append(product_left(p, vp))
            parts.append(jnp.where(low_lane, outs[0], outs[1]))
        ctx.append(jnp.concatenate(parts, axis=1).astype(bf16))
    ctx = jnp.concatenate(ctx, axis=0)
    slot(2)
    s = x_ref[...].astype(f32) + (product(ctx[:, :256], wo[0]) + product(ctx[:, 256:], wo[1]) + bo)
    center = s - row_mean(s)
    normed = center * lax.rsqrt(row_mean(center * center) + EPSILON) * g1 + s1
    low = normed.astype(bf16)
    branch = bd
    for j in range(4):
        h, o = j // 2, 512 * (j % 2)
        bi = jnp.concatenate([bias_ref[h, 2 + o // 256 : 3 + o // 256], bias_ref[h, 3 + o // 256 : 4 + o // 256]], axis=1)
        hid = product(low, wi[h, :, o : o + 512]) + bi
        branch = branch + product((hid * normal_cdf(hid)).astype(bf16), wd[h, o : o + 512])
        if j == 1:
            slot(3)
    s = normed + branch
    center = s - row_mean(s)
    y_ref[...] = (center * lax.rsqrt(row_mean(center * center) + EPSILON) * g2 + s2).astype(bf16)
    slot(4)
    dx = gf_ref[...]
    for h in range(2):
        cols = slice(256 * h, 256 * h + 256)
        for j, ref in ((1, dk_ref), (2, dv_ref)):
            dx = dx + product_right(ref[:, cols], wqkv[h, j])
    dx_ref[...] = dx

    @pl.when(step == pl.num_programs(0) - 1)
    def _():
        def body(it, carry):
            comm.iteration(it)
            return carry

        lax.fori_loop(slots * pl.num_programs(0), comm.iterations, body, 0)
        comm.finish()


def rest(g, small, states, q, k, v, lens, dk, dv, gf, wqkv, wo, wi, wd, bias, vec):
    rows = states.shape[0]
    block = 2 * SEQ
    K, STRIDE, SLOTS = 8, 2, 5
    tile = pl.BlockSpec((block, 512), lambda i: (i, 0))
    whole = lambda a: pl.BlockSpec(a.shape, lambda i: (0,) * a.ndim)
    vm = pl.BlockSpec(memory_space=pltpu.VMEM)
    S = jax.ShapeDtypeStruct
    return pl.pallas_call(
        functools.partial(rest_kernel, SLOTS, K, STRIDE),
        grid=(rows // block,),
        in_specs=[vm, vm, tile, tile, tile, tile, pl.BlockSpec((block, 128), lambda i: (i, 0)), tile, tile, tile,
                  whole(wqkv), whole(wo), whole(wi), whole(wd), whole(bias), whole(vec)],
        out_specs=[pl.BlockSpec(memory_space=pl.ANY), vm, tile, tile],
        out_shape=[S((ROWS, 512), bf16), S(small.shape, f32), S((rows, 512), bf16), S((rows, 512), f32)],
        scratch_shapes=Comm.scratch(K, small.shape[0]),
        compiler_params=pltpu.CompilerParams(collective_id=0, has_side_effects=True, vmem_limit_bytes=61 << 20),
        name="rest",
    )(g, small, states, q, k, v, lens, dk, dv, gf, wqkv, wo, wi, wd, bias, vec)


def unpack_half(w):
    do = w[2560:3072, 256:]
    return dict(
        down=w[:1024], inner=jnp.concatenate([w[1024:1536], w[1536:2048]], axis=1),
        query=w[2048:2560, :256], key=w[2048:2560, 256:], value=w[2560:3072, :256],
        output=jnp.concatenate([do[:256], do[256:]], axis=1),
    )


def whole_chains(
    states, cotangent, lengths, span_starts, span_ends, query_weight, query_bias, key_weight, value_weight, value_bias,
    output_weight, output_bias, first_gain, first_shift, inner_weight, inner_bias, down_weight, down_bias, second_gain, second_shift,
):
    t = lax.axis_index("tensor")
    rows = states.shape[0]
    chains = rows // SEQ
    row = lambda a: a.reshape(1, -1)
    q, k, v, wqkv, wo, wi, wd, bias = gather(
        states, query_weight, key_weight, value_weight, row(query_bias), row(value_bias), row(inner_bias),
        output_weight, inner_weight, down_weight,
    )
    vec = jnp.stack([output_bias, first_gain, first_shift, down_bias, second_gain, second_shift] + [jnp.zeros((512,), bf16)] * 2)
    g, dk, dv, gf, small = live_rows(lengths, span_starts, span_ends, states, cotangent, q, k, v, wqkv, wo, wi, wd, bias, vec)
    mine = lax.dynamic_slice_in_dim(lengths, t * chains, chains)
    lens = jnp.broadcast_to(jnp.repeat(mine, SEQ)[:, None], (rows, 128))
    summed, small, output, input_grad = rest(g, small, states, q, k, v, lens, dk, dv, gf, wqkv, wo, wi, wd, bias, vec)
    w = {name: part.astype(f32) for name, part in unpack_half(summed).items()}
    half = lambda line: lax.dynamic_slice_in_dim(line, t * 256, 256)
    return (
        output, input_grad, w["query"], half(small[6]), w["key"], w["value"], half(small[7]), w["output"],
        small[0], small[1], small[2], w["inner"], lax.dynamic_slice_in_dim(small[8:12].reshape(2048), t * 1024, 1024),
        w["down"], small[3], small[4], small[5],
    )


def local(*arguments):
    rows, hidden = arguments[0].shape[0], arguments[14].shape[1]
    if rows % SEQ == 0 and lax.axis_size("dp") == 16 and lax.axis_size("tensor") == 2:
        return whole_chains(*arguments)
    return general(*arguments)


def solution(mesh):
    placed = (
        P(("dp", "tensor"), None),
        P(("dp", "tensor"), None),
        P("dp"),
        P("dp"),
        P("dp"),
        P(None, "tensor"),
        P("tensor"),
        P(None, "tensor"),
        P(None, "tensor"),
        P("tensor"),
        P("tensor", None),
        P(),
        P(),
        P(),
        P(None, "tensor"),
        P("tensor"),
        P("tensor", None),
        P(),
        P(),
        P(),
    )
    return jax.shard_map(
        local,
        mesh=mesh,
        in_specs=placed,
        out_specs=(
            P(("dp", "tensor"), None),
            P(("dp", "tensor"), None),
            P(None, "tensor"),
            P("tensor"),
            P(None, "tensor"),
            P(None, "tensor"),
            P("tensor"),
            P("tensor", None),
            P(),
            P(),
            P(),
            P(None, "tensor"),
            P("tensor"),
            P("tensor", None),
            P(),
            P(),
            P(),
        ),
        check_vma=False,
    )
```

```python
import functools

import jax
import jax.numpy as jnp
from jax import lax
from jax.experimental import pallas as pl
from jax.experimental.pallas import tpu as pltpu
from jax.sharding import PartitionSpec as P

MESH = pl.DeviceIdType.MESH
f32, bf16 = jnp.float32, jnp.bfloat16
HEAD_DIM = 64
SEQ = 160
ROWS = 3072
SCALE = HEAD_DIM ** (-0.5)
ATT_BLOCK = 32
FFN_BLOCK = 256
EPSILON = 1e-12


def product(left, right):
    return jnp.dot(left, right, preferred_element_type=jnp.float32)


def product_left(left, right):
    return lax.dot_general(
        left, right, (((0,), (0,)), ((), ())), preferred_element_type=jnp.float32
    )


def product_right(left, right):
    return lax.dot_general(
        left, right, (((1,), (1,)), ((), ())), preferred_element_type=jnp.float32
    )


def layer_norm(values, gain, shift):
    center = values - jnp.mean(values, axis=-1, keepdims=True)
    spread = jnp.mean(center * center, axis=-1, keepdims=True)
    return center * lax.rsqrt(spread + EPSILON) * gain + shift


def exact_gelu(values):
    return jax.nn.gelu(values, approximate=False)


def attention_scores(queries, keys, key_live):
    scores = jnp.einsum(
        "cqhd,ckhd->chqk", queries, keys, preferred_element_type=jnp.float32
    ) * HEAD_DIM ** (-0.5)
    return jnp.where(key_live[:, None, None, :], scores, -1000000000.0)


def per_row(table, picker):
    return jnp.sum(jnp.where(picker, table[None, :], 0), axis=1)


def column_sum(values):
    return jnp.sum(values.astype(jnp.float32), axis=0)


def general(
    states,
    cotangent,
    lengths,
    span_starts,
    span_ends,
    query_weight,
    query_bias,
    key_weight,
    value_weight,
    value_bias,
    output_weight,
    output_bias,
    first_gain,
    first_shift,
    inner_weight,
    inner_bias,
    down_weight,
    down_bias,
    second_gain,
    second_shift,
):
    slice_rows = states.shape[0]
    chains = lengths.shape[0]
    group_rows = chains * SEQ
    heads_local = query_weight.shape[1] // HEAD_DIM
    layout = (chains, SEQ, heads_local, HEAD_DIM)
    whole = lax.all_gather(states, "tensor", axis=0, tiled=True)
    queries = (product(whole, query_weight) + query_bias).astype(jnp.bfloat16).reshape(layout)
    keys_low = product(whole, key_weight).astype(jnp.bfloat16).reshape(layout)
    values_low = (product(whole, value_weight) + value_bias).astype(jnp.bfloat16).reshape(layout)
    key_live = jnp.arange(SEQ, dtype=jnp.int32)[None, :] < lengths[:, None]
    scores = attention_scores(queries, keys_low, key_live)
    highest = jnp.max(scores, axis=-1, keepdims=True)
    logsum = highest + jnp.log(jnp.sum(jnp.exp(scores - highest), axis=-1, keepdims=True))
    probs_low = jnp.exp(scores - logsum).astype(jnp.bfloat16)
    context = jnp.einsum(
        "chqk,ckhd->cqhd", probs_low, values_low, preferred_element_type=jnp.float32
    )
    context = context.reshape(group_rows, heads_local * HEAD_DIM).astype(jnp.bfloat16)
    attended = lax.psum_scatter(
        product(context, output_weight), "tensor", scatter_dimension=0, tiled=True
    ) + output_bias.astype(jnp.float32)
    first_sum = states.astype(jnp.float32) + attended
    normed, first_pull = jax.vjp(
        layer_norm, first_sum, first_gain.astype(jnp.float32), first_shift.astype(jnp.float32)
    )
    normed_low = normed.astype(jnp.bfloat16)
    normed_all = lax.all_gather(normed_low, "tensor", axis=0, tiled=True)
    hidden = product(normed_all, inner_weight) + inner_bias.astype(jnp.float32)
    activation, gelu_pull = jax.vjp(exact_gelu, hidden)
    activation_low = activation.astype(jnp.bfloat16)
    branch = lax.psum_scatter(
        product(activation_low, down_weight), "tensor", scatter_dimension=0, tiled=True
    )
    second_sum = normed + (branch + down_bias.astype(jnp.float32))
    output, second_pull = jax.vjp(
        layer_norm, second_sum, second_gain.astype(jnp.float32), second_shift.astype(jnp.float32)
    )
    row_ids = lax.axis_index("tensor") * slice_rows + jnp.arange(slice_rows, dtype=jnp.int32)
    chain_ids = row_ids // SEQ
    position = row_ids % SEQ
    picker = chain_ids[:, None] == jnp.arange(chains, dtype=jnp.int32)[None, :]
    live = (
        (position >= per_row(span_starts, picker))
        & (position < per_row(span_ends, picker))
        & (position < per_row(lengths, picker))
    )
    grad_out = jnp.where(live[:, None], cotangent.astype(jnp.float32), 0.0)
    grad_second, second_gain_part, second_shift_part = second_pull(grad_out)
    grad_branch = grad_second.astype(jnp.bfloat16)
    down_bias_part = column_sum(grad_branch)
    grad_branch_all = lax.all_gather(grad_branch, "tensor", axis=0, tiled=True)
    down_weight_part = product_left(activation_low, grad_branch_all)
    grad_activation = product_right(grad_branch_all, down_weight)
    (grad_hidden,) = gelu_pull(grad_activation)
    grad_hidden_low = grad_hidden.astype(jnp.bfloat16)
    inner_weight_part = product_left(normed_all, grad_hidden_low)
    inner_bias_part = column_sum(grad_hidden_low)
    grad_normed = lax.psum_scatter(
        product_right(grad_hidden_low, inner_weight), "tensor", scatter_dimension=0, tiled=True
    )
    grad_first, first_gain_part, first_shift_part = first_pull(grad_second + grad_normed)
    grad_attended = grad_first.astype(jnp.bfloat16)
    output_bias_part = column_sum(grad_attended)
    grad_attended_all = lax.all_gather(grad_attended, "tensor", axis=0, tiled=True)
    output_weight_part = product_left(context, grad_attended_all)
    grad_context = (
        product_right(grad_attended_all, output_weight).astype(jnp.bfloat16).reshape(layout)
    )
    probs = jnp.exp(attention_scores(queries, keys_low, key_live) - logsum)
    grad_probs = jnp.einsum(
        "cqhd,ckhd->chqk", grad_context, values_low, preferred_element_type=jnp.float32
    )
    grad_scores = probs * (grad_probs - jnp.sum(probs * grad_probs, axis=-1, keepdims=True))
    grad_scores_low = grad_scores.astype(jnp.bfloat16)
    scale = HEAD_DIM ** (-0.5)
    grad_queries = (
        jnp.einsum("chqk,ckhd->cqhd", grad_scores_low, keys_low, preferred_element_type=jnp.float32)
        * scale
    )
    grad_keys = (
        jnp.einsum("chqk,cqhd->ckhd", grad_scores_low, queries, preferred_element_type=jnp.float32)
        * scale
    )
    grad_values = jnp.einsum(
        "chqk,cqhd->ckhd", probs_low, grad_context, preferred_element_type=jnp.float32
    )
    flat = (group_rows, heads_local * HEAD_DIM)
    grad_queries = grad_queries.reshape(flat).astype(jnp.bfloat16)
    grad_keys = grad_keys.reshape(flat).astype(jnp.bfloat16)
    grad_values = grad_values.reshape(flat).astype(jnp.bfloat16)
    query_weight_part = product_left(whole, grad_queries)
    key_weight_part = product_left(whole, grad_keys)
    value_weight_part = product_left(whole, grad_values)
    query_bias_part = column_sum(grad_queries)
    value_bias_part = column_sum(grad_values)
    grad_whole = (
        product_right(grad_queries, query_weight)
        + product_right(grad_keys, key_weight)
        + product_right(grad_values, value_weight)
    )
    input_grad = (
        lax.psum_scatter(
            grad_whole.astype(jnp.bfloat16), "tensor", scatter_dimension=0, tiled=True
        ).astype(jnp.float32)
        + grad_first
    )
    (
        query_weight_grad,
        query_bias_grad,
        key_weight_grad,
        value_weight_grad,
        value_bias_grad,
        output_weight_grad,
        inner_weight_grad,
        inner_bias_grad,
        down_weight_grad,
    ) = (
        lax.psum(query_weight_part.astype(jnp.bfloat16), "dp").astype(jnp.float32),
        lax.psum(query_bias_part.astype(jnp.bfloat16), "dp").astype(jnp.float32),
        lax.psum(key_weight_part.astype(jnp.bfloat16), "dp").astype(jnp.float32),
        lax.psum(value_weight_part.astype(jnp.bfloat16), "dp").astype(jnp.float32),
        lax.psum(value_bias_part.astype(jnp.bfloat16), "dp").astype(jnp.float32),
        lax.psum(output_weight_part.astype(jnp.bfloat16), "dp").astype(jnp.float32),
        lax.psum(inner_weight_part.astype(jnp.bfloat16), "dp").astype(jnp.float32),
        lax.psum(inner_bias_part.astype(jnp.bfloat16), "dp").astype(jnp.float32),
        lax.psum(down_weight_part.astype(jnp.bfloat16), "dp").astype(jnp.float32),
    )
    (
        output_bias_grad,
        first_gain_grad,
        first_shift_grad,
        down_bias_grad,
        second_gain_grad,
        second_shift_grad,
    ) = lax.psum(
        (
            output_bias_part,
            first_gain_part,
            first_shift_part,
            down_bias_part,
            second_gain_part,
            second_shift_part,
        ),
        ("dp", "tensor"),
    )
    return (
        output.astype(jnp.bfloat16),
        input_grad,
        query_weight_grad,
        query_bias_grad,
        key_weight_grad,
        value_weight_grad,
        value_bias_grad,
        output_weight_grad,
        output_bias_grad,
        first_gain_grad,
        first_shift_grad,
        inner_weight_grad,
        inner_bias_grad,
        down_weight_grad,
        down_bias_grad,
        second_gain_grad,
        second_shift_grad,
    )


class Comm:
    NSTAGE = 10
    def __init__(self, K, g, small, out, sout, bufs, stride=1):
        self.stride = stride
        self.K = K; self.CH = ROWS // K; self.SB = self.CH // 3
        self.g, self.small, self.out_hbm, self.sout = g, small, out, sout
        (self.core_buf, self.acc, self.r1, self.r2, self.r3, self.r4, self.out, self.sm, self.csem, self.rsem, self.asem, self.smsem, self.fsem) = bufs
        dp = lax.axis_index("dp"); t = lax.axis_index("tensor")
        self.t = t
        x = lax.rem(dp, 2); y = lax.rem(dp // 2, 2); p = lax.rem(dp // 4, 2); q = dp // 8
        self.bits = (x, y, p, q)
        self.parts = tuple(dp + w * (1 - 2 * b) for w, b in ((1, x), (2, y), (4, p), (8, q)))
        self.dp = dp
    def barrier(self):
        b = pltpu.get_barrier_semaphore()
        pl.semaphore_signal(b, inc=1, device_id=(self.dp, 1 - self.t), device_id_type=MESH)
        for n in self.parts:
            pl.semaphore_signal(b, inc=1, device_id=(n, self.t), device_id_type=MESH)
        pl.semaphore_wait(b, 5)
    def rc(self, src, dst, s, r, n):
        return pltpu.make_async_remote_copy(src_ref=src, dst_ref=dst, send_sem=s, recv_sem=r, device_id=(n, self.t), device_id_type=MESH)
    def core_copy(self, k):
        return pltpu.make_async_remote_copy(src_ref=self.g.at[1 - self.t, pl.ds(k * self.CH, self.CH)], dst_ref=self.core_buf.at[k],
            send_sem=self.csem.at[0, k], recv_sem=self.csem.at[1, k], device_id=(self.dp, 1 - self.t), device_id_type=MESH)
    def own_copy(self, k):
        sl = pl.ds(k * self.CH, self.CH)
        return pltpu.make_async_copy(self.g.at[self.t, sl], self.acc.at[sl], self.csem.at[2, k])
    def order(self, k, r):
        B, N = self.bits, self.parts
        X, Y, Pp, Qq = ((B[i], N[i]) for i in range(4))
        if r == 0: return X, Y, Pp, Qq
        if r == 1: return Y, X, Pp, Qq
        even = lax.rem(k, 2) == 0
        U = (jnp.where(even, B[0], B[1]), jnp.where(even, N[0], N[1]))
        V = (jnp.where(even, B[1], B[0]), jnp.where(even, N[1], N[0]))
        return Pp, U, V, Qq
    def region(self, k, r, depth, keep):
        o = self.order(k, r)
        rows, cols = self.SB, 512
        r0, c0 = k * self.CH + r * self.SB, 0
        for i in range(depth):
            b = o[i][0]
            if i == depth - 1 and not keep: b = 1 - b
            if i < 2:
                rows //= 2; r0 = r0 + b * rows
            else:
                cols //= 2; c0 = c0 + b * cols
        if depth > 2: c0 = pl.multiple_of(c0, 128)
        return pl.ds(pl.multiple_of(r0, 16), rows), pl.ds(c0, cols)
    def rs(self, k, r, i):
        n = self.order(k, r)[i][1]
        buf = (self.r1, self.r2, self.r3, self.r4)[i]
        return self.rc(self.acc.at[self.region(k, r, i + 1, False)], buf.at[k, r], self.rsem.at[0, i, k, r], self.rsem.at[1, i, k, r], n)
    def ag(self, k, r, i):
        n = self.order(k, r)[i][1]
        sl = self.region(k, r, i + 1, True)
        return self.rc(self.out.at[sl], self.out.at[sl], self.asem.at[0, i, k, r], self.asem.at[1, i, k, r], n)
    def small_copy(self, i):
        dev = (self.dp, 1 - self.t) if i == 0 else (self.parts[i - 1], self.t)
        src = self.small if i == 0 else self.sm.at[1, i - 1]
        return pltpu.make_async_remote_copy(src_ref=src, dst_ref=self.sm.at[0, i], send_sem=self.smsem.at[0, i], recv_sem=self.smsem.at[1, i], device_id=dev, device_id_type=MESH)
    def stage(self, s, k):
        if s == 0:
            self.core_copy(k).start()
            self.own_copy(k).start()
        elif s == 1:
            self.core_copy(k).wait_recv()
            sl = pl.ds(pl.multiple_of(k * self.CH, 16), self.CH)
            self.own_copy(k).wait()
            self.acc[sl] = (self.acc[sl].astype(f32) + self.core_buf[k].astype(f32)).astype(bf16)
            for r in range(3): self.rs(k, r, 0).start()
        elif s <= 5:
            i = s - 2
            buf = (self.r1, self.r2, self.r3, self.r4)[i]
            for r in range(3):
                self.rs(k, r, i).wait_recv()
                sl = self.region(k, r, i + 1, True)
                v = (self.acc[sl].astype(f32) + buf[k, r].astype(f32)).astype(bf16)
                if i < 3:
                    self.acc[sl] = v
                    self.rs(k, r, i + 1).start()
                else:
                    self.out[sl] = v
                    self.ag(k, r, 3).start()
        else:
            i = 9 - s
            for r in range(3):
                self.ag(k, r, i).wait_recv()
                if i > 0: self.ag(k, r, i - 1).start()
            if i == 0: self.final_copy(k).start()
    def final_copy(self, k):
        sl = pl.ds(k * self.CH, self.CH)
        return pltpu.make_async_copy(self.out.at[sl], self.out_hbm.at[sl], self.fsem.at[k])
    def small_stage(self, i):
        if i > 0:
            self.small_copy(i - 1).wait_recv()
            own = self.small[...] if i == 1 else self.sm[1, i - 2]
            v = own + self.sm[0, i - 1]
            if i < 5: self.sm[1, i - 1] = v
            else: self.sout[...] = v
        if i < 5: self.small_copy(i).start()
    def iteration(self, it):
        for s in reversed(range(self.NSTAGE)):
            k = it - s * self.stride
            @pl.when((k >= 0) & (k < self.K))
            def _(s=s, k=k):
                self.stage(s, k)
        for i in range(6):
            @pl.when(it == i * self.stride + 1)
            def _(i=i): self.small_stage(i)
    @property
    def iterations(self): return self.K + (self.NSTAGE - 1) * self.stride
    def finish(self):
        def body(k, c):
            self.core_copy(k).wait_send(); self.final_copy(k).wait()
            for r in range(3):
                for i in range(4):
                    self.rs(k, r, i).wait_send(); self.ag(k, r, i).wait_send()
            return c
        lax.fori_loop(0, self.K, body, 0)
        for i in range(5): self.small_copy(i).wait_send()
    @staticmethod
    def scratch(K, S):
        SB = ROWS // K // 3
        D = pltpu.SemaphoreType.DMA
        return [pltpu.VMEM((K, 3 * SB, 512), bf16), pltpu.VMEM((ROWS, 512), bf16),
            pltpu.VMEM((K, 3, SB // 2, 512), bf16), pltpu.VMEM((K, 3, SB // 4, 512), bf16),
            pltpu.VMEM((K, 3, SB // 4, 256), bf16), pltpu.VMEM((K, 3, SB // 4, 128), bf16),
            pltpu.VMEM((ROWS, 512), bf16), pltpu.VMEM((2, 5, S, 512), f32),
            D((3, K)), D((2, 4, K, 3)), D((2, 4, K, 3)), D((2, 5)), D((K,))]


def gather_kernel(
    x_ref, wq_ref, wk_ref, wv_ref, bq_ref, bv_ref, bi_ref, bo_ref, g1_ref, s1_ref, bd_ref, g2_ref, s2_ref, wo_ref, wi_ref, wd_ref,
    q_ref, k_ref, v_ref, vec_ref, wqkv_out, wo_out, wi_out, wd_out, bias_out,
    wqkv, wo, wi, wd, bias, near, sent, came,
):
    step = pl.program_id(0)
    dp, t = lax.axis_index("dp"), lax.axis_index("tensor")

    def pair(i, src, dst):
        return pltpu.make_async_remote_copy(
            src_ref=src, dst_ref=dst, send_sem=sent.at[i], recv_sem=came.at[i],
            device_id=(dp, 1 - t), device_id_type=MESH,
        )

    first = [
        pair(0, wq_ref, wqkv.at[t, 0]), pair(1, wk_ref, wqkv.at[t, 1]), pair(2, wv_ref, wqkv.at[t, 2]),
        pair(3, bias.at[t], bias.at[t]),
    ]
    later = [pair(4, wo.at[t], wo.at[t]), pair(5, wi.at[t], wi.at[t]), pair(6, wd.at[t], wd.at[t])]
    own = [pltpu.make_async_copy(a, b.at[t], near.at[i]) for i, (a, b) in enumerate(((wo_ref, wo), (wi_ref, wi), (wd_ref, wd)))]
    keep = [pltpu.make_async_copy(wqkv, wqkv_out, near.at[3]), pltpu.make_async_copy(bias, bias_out, near.at[4])]
    keep_later = [pltpu.make_async_copy(a, b, near.at[5 + i]) for i, (a, b) in enumerate(((wo, wo_out), (wi, wi_out), (wd, wd_out)))]

    @pl.when(step == 0)
    def _():
        barrier = pltpu.get_barrier_semaphore()
        pl.semaphore_signal(barrier, inc=1, device_id=(dp, 1 - t), device_id_type=MESH)
        bias[t, 0:1] = bq_ref[...].astype(f32).reshape(1, 256)
        bias[t, 1:2] = bv_ref[...].astype(f32).reshape(1, 256)
        for i in range(4):
            bias[t, 2 + i : 3 + i] = bi_ref[pl.ds(256 * i, 256)].astype(f32).reshape(1, 256)
        bias[t, 6:8] = jnp.zeros((2, 256), f32)
        for copy in own:
            copy.start()
        for i, ref in enumerate((bo_ref, g1_ref, s1_ref, bd_ref, g2_ref, s2_ref)):
            vec_ref[i : i + 1] = ref[...].astype(f32).reshape(1, 512)
        vec_ref[6:8] = jnp.zeros((2, 512), f32)
        pl.semaphore_wait(barrier, 1)
        for copy in first:
            copy.start()
        for j, ref in enumerate((wq_ref, wk_ref, wv_ref)):
            wqkv[t, j] = ref[...]
        for copy in first:
            copy.wait_recv()
        for copy in keep:
            copy.start()
        for mine, copy in zip(own, later):
            mine.wait()
            copy.start()

    x = x_ref[...]
    for h in range(2):
        cols = slice(256 * h, 256 * h + 256)
        q_ref[:, cols] = ((product(x, wqkv[h, 0]) + bias[h, 0:1]).astype(bf16).astype(f32) * SCALE).astype(bf16)
        k_ref[:, cols] = product(x, wqkv[h, 1]).astype(bf16)
        v_ref[:, cols] = (product(x, wqkv[h, 2]) + bias[h, 1:2]).astype(bf16)

    @pl.when(step == pl.num_programs(0) // 2)
    def _():
        for copy, out in zip(later, keep_later):
            copy.wait_recv()
            out.start()

    @pl.when(step == pl.num_programs(0) - 1)
    def _():
        for copy in first:
            copy.wait_send()
        for copy in later:
            copy.wait_send()
        for copy in keep + keep_later:
            copy.wait()


def gather(states, wq, wk, wv, bq, bv, bi, vectors, wo, wi, wd):
    rows = states.shape[0]
    block = 2 * SEQ
    whole = lambda a: pl.BlockSpec(a.shape, lambda i: (0,) * a.ndim)
    tile = pl.BlockSpec((block, 512), lambda i: (i, 0))
    hbm, vm = pl.BlockSpec(memory_space=pl.ANY), pl.BlockSpec(memory_space=pltpu.VMEM)
    D = pltpu.SemaphoreType.DMA
    S = jax.ShapeDtypeStruct
    return pl.pallas_call(
        gather_kernel,
        grid=(rows // block,),
        in_specs=[tile, whole(wq), whole(wk), whole(wv)] + [vm] * 9 + [hbm, hbm, hbm],
        out_specs=[tile, tile, tile, vm, hbm, hbm, hbm, hbm, hbm],
        out_shape=[S((rows, 512), bf16)] * 3 + [
            S((8, 512), f32),
            S((2, 3, 512, 256), bf16), S((2, 256, 512), bf16), S((2, 512, 1024), bf16), S((2, 1024, 512), bf16), S((2, 8, 256), f32),
        ],
        scratch_shapes=[
            pltpu.VMEM((2, 3, 512, 256), bf16), pltpu.VMEM((2, 256, 512), bf16), pltpu.VMEM((2, 512, 1024), bf16),
            pltpu.VMEM((2, 1024, 512), bf16), pltpu.VMEM((2, 8, 256), f32), D((8,)), D((7,)), D((7,)),
        ],
        compiler_params=pltpu.CompilerParams(collective_id=1, has_side_effects=True, vmem_limit_bytes=60 << 20),
        name="gather",
    )(states, wq, wk, wv, bq, bv, bi, *vectors, wo, wi, wd)


def normal_cdf(h):
    return 0.5 + 0.5 * lax.erf(h * 0.7071067811865476)


def inverse(a):
    return pltpu.reciprocal(a, approx=True)


def row_mean(a):
    return jnp.sum(a, axis=-1, keepdims=True) * (1.0 / 512)


WINDOW = 64
FRONT = 8


def live_kernel(
    len_ref, start_ref, end_ref,
    x_hbm, cot_hbm, q_hbm, k_hbm, v_hbm, wqkv_hbm, wo_hbm, wi_hbm, wd_hbm, bias_ref, vec_ref,
    g_out, dk_out, dv_out, dx_out, small_out,
    x_all, cot_all, q_all, k_all, v_all, wq, wo, wi, wd, context, inputs, upstream, first, dv_all, acc_k, acc_v,
    acc_d, acc_i, acc_o, gelu_grad, act, stage, win_chain, win_pos, win_dst, chain_win, in_sems, w_sems, out_sems, dx_sems,
):
    chains = len_ref.shape[0] // 2
    t = lax.axis_index("tensor")
    W, R = WINDOW, FFN_BLOCK
    half = chains // 2
    rows_all = chains * SEQ
    dk_all = cot_all
    spread = gelu_grad

    def chain_loads(c):
        rows = pl.ds(c * SEQ, SEQ)
        return [
            pltpu.make_async_copy(a.at[rows], b.at[rows], in_sems.at[i, c])
            for i, (a, b) in enumerate(((q_hbm, q_all), (k_hbm, k_all), (v_hbm, v_all), (cot_hbm, cot_all), (x_hbm, x_all)))
        ]

    loads = [
        pltpu.make_async_copy(a, b, w_sems.at[i])
        for i, (a, b) in enumerate((
            (wo_hbm, wo), (wi_hbm, wi), (wd_hbm, wd), (wqkv_hbm.at[0, 0], wq.at[0]), (wqkv_hbm.at[1, 0], wq.at[1]),
        ))
    ]

    def start_loads(c, carry):
        for copy in chain_loads(c):
            copy.start()
        return carry

    lax.fori_loop(0, chains, start_loads, 0)
    for copy in loads:
        copy.start()

    def list_chain(c, carry):
        at, offset = carry
        start = start_ref[t * chains + c]
        end = jnp.minimum(end_ref[t * chains + c], len_ref[t * chains + c])
        r16 = (start // 16) * 16
        r8 = (start // 8) * 8
        count = jnp.maximum((end - r16 + W - 1) // W, 1)
        chain_win[c] = at

        def put(i, carry):
            win_chain[at + i] = c
            win_pos[at + i] = r16 + W * i
            win_dst[at + i] = offset + r16 - r8 + W * i
            return carry

        lax.fori_loop(0, count, put, 0)
        return at + count, offset + jnp.maximum(((end + 7) // 8) * 8 - r8, 0)

    n_win, n_end = lax.fori_loop(0, chains, list_chain, (0, FRONT))
    chain_win[chains] = n_win
    trash = context.shape[0] - W
    win_chain[n_win] = chains - 1
    win_pos[n_win] = SEQ
    win_dst[n_win] = trash
    n = n_end - FRONT

    acc_d[...] = jnp.zeros_like(acc_d)
    acc_i[...] = jnp.zeros_like(acc_i)
    acc_o[...] = jnp.zeros_like(acc_o)
    acc_k[...] = jnp.zeros_like(acc_k)
    acc_v[...] = jnp.zeros_like(acc_v)
    small_out[...] = jnp.zeros_like(small_out)
    for ref in (context, upstream, first):
        ref[pl.ds(trash, W)] = jnp.zeros((W, 512), f32)
    for ref in (x_all, cot_all, q_all):
        ref[pl.ds(rows_all, W)] = jnp.zeros((W, 512), bf16)

    lane_head = lax.broadcasted_iota(jnp.int32, (W, 256), 1) // HEAD_DIM
    own = lax.broadcasted_iota(jnp.int32, (4 * W, 256), 1) // HEAD_DIM == lax.broadcasted_iota(jnp.int32, (4 * W, 256), 0) // W
    key_row = lax.broadcasted_iota(jnp.int32, (SEQ, 4 * W), 0)
    row_id = lax.broadcasted_iota(jnp.int32, (W, 512), 0)

    def heads_apart(rows):
        return jnp.where(own, jnp.concatenate([rows] * 4, axis=0), jnp.zeros((), bf16))

    def heads_together(full):
        out = full[3 * W :]
        for h in (2, 1, 0):
            out = jnp.where(lane_head == h, full[h * W : (h + 1) * W], out)
        return out

    def window(i):
        c = win_chain[i]
        pos = win_pos[i]
        start = start_ref[t * chains + c]
        length = len_ref[t * chains + c]
        end = jnp.minimum(end_ref[t * chains + c], length)
        src = pl.ds(pl.multiple_of(c * SEQ + pos, 16), W)
        dst = pl.multiple_of(win_dst[i], 8)
        keys = pl.ds(pl.multiple_of(c * SEQ, 32), SEQ)
        live = (row_id + pos >= start) & (row_id + pos < end)
        whole = pos + 8 > start
        return c, pos, length, src, dst, keys, live, whole

    def put_rows(ref, dst, whole, rows):
        head = pl.ds(dst, 8)
        ref[head] = jnp.where(whole, rows[:8], ref[head])
        ref[pl.ds(pl.multiple_of(dst + 8, 8), W - 8)] = rows[8:]

    def probabilities(qs, k, length):
        scores = product_right(k, qs)
        scores = jnp.where(key_row < length, scores, -1e9)
        e = jnp.exp(scores - jnp.max(scores, axis=0, keepdims=True))
        return e * inverse(jnp.sum(e, axis=0, keepdims=True))

    def forward(i, waited):
        last = win_chain[2 * i + 1]

        def wait_chain(c, carry):
            for copy in chain_loads(c):
                copy.wait()
            return carry

        lax.fori_loop(waited, last + 1, wait_chain, 0)
        done = []
        for u in range(2):
            c, pos, length, src, dst, keys, live, whole = window(2 * i + u)
            q = q_all[src]
            out = []
            for g in range(2):
                cols = slice(256 * g, 256 * g + 256)
                p = probabilities(heads_apart(q[:, cols]), k_all[keys, cols], length)
                out.append(heads_together(product_left(p.astype(bf16), v_all[keys, cols])))
            done.append((jnp.concatenate(out, axis=1), x_all[src].astype(f32), jnp.where(live, cot_all[src].astype(f32), 0.0), dst, whole))
        for ctx, x, cot, dst, whole in done:
            put_rows(context, dst, whole, ctx)
            put_rows(inputs, dst, whole, x)
            put_rows(upstream, dst, whole, cot)
        return last + 1

    steps = (n_win + 1) // 2
    waited = lax.fori_loop(0, steps, forward, 0)

    tail = pl.ds(pl.multiple_of(n_end, 8), R)
    for ref in (context, inputs, upstream):
        ref[tail] = jnp.zeros((R, 512), f32)
    for copy in loads:
        copy.wait()
    vec = vec_ref[...]
    bo, g1, s1, bd, g2, s2 = (vec[i : i + 1] for i in range(6))
    blocks = (n + R - 1) // R

    def feed_forward(b, carry):
        rows = pl.ds(pl.multiple_of(FRONT + b * R, 8), R)
        ctx = context[rows].astype(bf16)
        attended = product(ctx[:, :256], wo[0]) + product(ctx[:, 256:], wo[1]) + bo
        s = inputs[rows] + attended
        center = s - row_mean(s)
        rstd1 = lax.rsqrt(row_mean(center * center) + EPSILON)
        hat1 = center * rstd1
        normed = hat1 * g1 + s1
        low = normed.astype(bf16)
        branch = jnp.zeros((R, 512), f32) + bd
        for j in range(4):
            h, o = j // 2, 512 * (j % 2)
            bi = jnp.concatenate([bias_ref[h, 2 + o // 256 : 3 + o // 256], bias_ref[h, 3 + o // 256 : 4 + o // 256]], axis=1)
            hid = product(low, wi[h, :, o : o + 512]) + bi
            cdf = normal_cdf(hid)
            a = (hid * cdf).astype(bf16)
            gelu_grad[j] = cdf + hid * (0.3989422804014327 * jnp.exp(-0.5 * hid * hid))
            act[j] = a
            branch = branch + product(a, wd[h, o : o + 512])
        s = normed + branch
        center = s - row_mean(s)
        rstd2 = lax.rsqrt(row_mean(center * center) + EPSILON)
        hat2 = center * rstd2
        up = upstream[rows]
        gy = up * g2
        grad = rstd2 * (gy - row_mean(gy) - hat2 * row_mean(gy * hat2))
        gb = grad.astype(bf16)
        gn = grad
        for j in range(4):
            h, o = j // 2, 512 * (j % 2)
            gh = (product_right(gb, wd[h, o : o + 512]) * gelu_grad[j]).astype(bf16)
            acc_d[h, o : o + 512] += product_left(act[j], gb)
            acc_i[j] += product_left(low, gh)
            small_out[8 + j : 9 + j] += jnp.sum(gh.astype(f32), axis=0, keepdims=True)
            gn = gn + product_right(gh, wi[h, :, o : o + 512])
        small_out[1:2] += jnp.sum(gn * hat1, axis=0, keepdims=True)
        small_out[2:3] += jnp.sum(gn, axis=0, keepdims=True)
        small_out[3:4] += jnp.sum(gb.astype(f32), axis=0, keepdims=True)
        small_out[4:5] += jnp.sum(up * hat2, axis=0, keepdims=True)
        small_out[5:6] += jnp.sum(up, axis=0, keepdims=True)
        gy = gn * g1
        grad = rstd1 * (gy - row_mean(gy) - hat1 * row_mean(gy * hat1))
        first[rows] = grad
        ga = grad.astype(bf16)
        small_out[0:1] += jnp.sum(ga.astype(f32), axis=0, keepdims=True)
        acc_o[...] += product_left(ctx, ga)
        upstream[rows] = jnp.concatenate([product_right(ga, wo[0]), product_right(ga, wo[1])], axis=1)
        return carry

    lax.fori_loop(0, blocks, feed_forward, 0)

    def out_copy(h, part):
        rows = pl.ds(0, 2048) if part == 0 else pl.ds(2048, 1024)
        return pltpu.make_async_copy(stage.at[h, rows], g_out.at[h, rows], out_sems.at[2 * part + h])

    for h in range(2):
        stage[h, 0:1024] = acc_d[h].astype(bf16)
        stage[h, 1024:1536] = acc_i[2 * h].astype(bf16)
        stage[h, 1536:2048] = acc_i[2 * h + 1].astype(bf16)
        out_copy(h, 0).start()
        stage[h, 2560:2816, 256:512] = acc_o[256 * h : 256 * h + 256, 0:256].astype(bf16)
        stage[h, 2816:3072, 256:512] = acc_o[256 * h : 256 * h + 256, 256:512].astype(bf16)

    def backward(i, carry):
        done = []
        for u in range(2):
            c, pos, length, src, dst, keys, live, whole = window(2 * i + u)
            same = jnp.where((i + u > 0) & (win_chain[jnp.maximum(2 * i + u - 1, 0)] == c), 1.0, 0.0)
            q = q_all[src]
            gc = jnp.where(live, upstream[pl.ds(dst, W)], 0.0).astype(bf16)
            out = []
            for g in range(2):
                cols = slice(256 * g, 256 * g + 256)
                qs, gs = heads_apart(q[:, cols]), heads_apart(gc[:, cols])
                p = probabilities(qs, k_all[keys, cols], length)
                gp = product_right(v_all[keys, cols], gs)
                ds = (p * (gp - jnp.sum(p * gp, axis=0, keepdims=True))).astype(bf16)
                dk = acc_k[:, cols] * same + product(ds, qs)
                dv = acc_v[:, cols] * same + product(p.astype(bf16), gs)
                acc_k[:, cols] = dk
                acc_v[:, cols] = dv
                dk_all[keys, cols] = dk.astype(bf16)
                dv_all[keys, cols] = dv.astype(bf16)
                out.append(heads_together(product_left(ds, k_all[keys, cols])) * SCALE)
            done.append((jnp.concatenate(out, axis=1), dst, whole))
        for dq, dst, whole in done:
            put_rows(context, dst, whole, dq)
        return carry

    lax.fori_loop(0, steps, backward, 0)
    keep = [
        pltpu.make_async_copy(dk_all.at[pl.ds(0, rows_all)], dk_out, out_sems.at[4]),
        pltpu.make_async_copy(dv_all, dv_out, out_sems.at[5]),
    ]
    for copy in keep:
        copy.start()
    context[tail] = jnp.zeros((R, 512), f32)
    acc_o[...] = jnp.zeros_like(acc_o)

    def query_weight(b, carry):
        rows = pl.ds(pl.multiple_of(FRONT + b * R, 8), R)
        dq = context[rows].astype(bf16)
        acc_o[...] += product_left(inputs[rows].astype(bf16), dq)
        small_out[6:7] += jnp.sum(dq.astype(f32), axis=0, keepdims=True)
        first[rows] = first[rows] + (product_right(dq[:, :256], wq[0]) + product_right(dq[:, 256:], wq[1]))
        return carry

    lax.fori_loop(0, blocks, query_weight, 0)
    small_out[7:8] = jnp.sum(dv_all[...].astype(f32), axis=0, keepdims=True)
    part = 4 * SEQ if chains % 4 == 0 else rows_all // 2

    def key_value_weight(b, carry):
        rows = pl.ds(pl.multiple_of(b * part, 32), part)
        x = x_all[rows]
        dk = product_left(x, dk_all[rows])
        dv = product_left(x, dv_all[rows])
        keep = jnp.where(b > 0, 1.0, 0.0)
        acc_d[0, 0:512] = acc_d[0, 0:512] * keep + dk
        acc_d[1, 0:512] = acc_d[1, 0:512] * keep + dv
        return carry

    lax.fori_loop(0, rows_all // part, key_value_weight, 0)
    dk, dv = acc_d[0, 0:512], acc_d[1, 0:512]
    for h in range(2):
        cols = slice(256 * h, 256 * h + 256)
        stage[h, 2048:2560, 0:256] = acc_o[:, cols].astype(bf16)
        stage[h, 2048:2560, 256:512] = dk[:, cols].astype(bf16)
        stage[h, 2560:3072, 0:256] = dv[:, cols].astype(bf16)
        out_copy(h, 1).start()

    def chain_out(c, slot):
        return pltpu.make_async_copy(spread.at[slot, pl.ds(0, SEQ)], dx_out.at[pl.ds(c * SEQ, SEQ)], dx_sems.at[slot])

    def scatter(i, carry):
        for slot in range(2):
            c = 2 * i + slot

            @pl.when(i > 0)
            def _():
                chain_out(c - 2, slot).wait()

            spread[slot, 0 : SEQ + W] = jnp.zeros((SEQ + W, 512), f32)

            def put(j, carry):
                _, pos, _, _, dst, _, live, _ = window(j)
                spread[slot, pl.ds(pl.multiple_of(pos, 16), W)] = jnp.where(live, first[pl.ds(dst, W)], 0.0)
                return carry

            lax.fori_loop(chain_win[c], chain_win[c + 1], put, 0)
            chain_out(c, slot).start()
        return carry

    lax.fori_loop(0, half, scatter, 0)
    for slot in range(2):
        chain_out(chains - 2 + slot, slot).wait()
    for copy in keep:
        copy.wait()
    for h in range(2):
        out_copy(h, 0).wait()
        out_copy(h, 1).wait()


def live_rows(lengths, starts, ends, states, cotangent, q, k, v, wqkv, wo, wi, wd, bias, vec):
    rows = states.shape[0]
    chains = rows // SEQ
    R, W = FFN_BLOCK, WINDOW
    C = -(-(FRONT + rows + R + W) // 8) * 8
    windows = 3 * chains + 2
    hbm, vm, sm = (pl.BlockSpec(memory_space=s) for s in (pl.ANY, pltpu.VMEM, pltpu.SMEM))
    S, V, D, M = jax.ShapeDtypeStruct, pltpu.VMEM, pltpu.SemaphoreType.DMA, pltpu.SMEM
    return pl.pallas_call(
        live_kernel,
        in_specs=[sm] * 3 + [hbm] * 9 + [vm, vm],
        out_specs=[hbm] * 4 + [vm],
        scratch_shapes=[
            V((rows + W, 512), bf16), V((rows + W, 512), bf16), V((rows + W, 512), bf16), V((rows, 512), bf16), V((rows, 512), bf16),
            V((2, 512, 256), bf16), V((2, 256, 512), bf16), V((2, 512, 1024), bf16), V((2, 1024, 512), bf16),
            V((C, 512), f32), V((C, 512), f32), V((C, 512), f32), V((C, 512), f32),
            V((rows, 512), bf16), V((SEQ, 512), f32), V((SEQ, 512), f32),
            V((2, 1024, 512), f32), V((4, 512, 512), f32), V((512, 512), f32),
            V((4, R, 512), f32), V((4, R, 512), bf16), V((2, 3072, 512), bf16),
            M((windows,), jnp.int32), M((windows,), jnp.int32), M((windows,), jnp.int32), M((chains + 1,), jnp.int32),
            D((5, chains)), D((5,)), D((6,)), D((2,)),
        ],
        out_shape=[S((2, ROWS, 512), bf16), S((rows, 512), bf16), S((rows, 512), bf16), S((rows, 512), f32), S((16, 512), f32)],
        compiler_params=pltpu.CompilerParams(vmem_limit_bytes=62 << 20),
        name="live_rows",
    )(lengths, starts, ends, states, cotangent, q, k, v, wqkv, wo, wi, wd, bias, vec)


def rest_kernel(
    SLOTS, K, STRIDE,
    g, small, x_ref, q_ref, k_ref, v_ref, len_ref, dk_ref, dv_ref, gf_ref, wqkv_hbm, wo_hbm, wi_hbm, wd_hbm, bias_ref, vec_ref,
    out, sout, y_ref, dx_ref, wqkv, wo, wi, wd, w_sems, *bufs,
):
    step = pl.program_id(0)
    comm = Comm(K, g, small, out, sout, bufs, STRIDE)
    slots = SLOTS
    loads = [
        pltpu.make_async_copy(a, b, w_sems.at[i])
        for i, (a, b) in enumerate(((wo_hbm, wo), (wi_hbm, wi), (wd_hbm, wd), (wqkv_hbm, wqkv)))
    ]

    def slot(i):
        if i < slots:
            it = step * slots + i

            @pl.when(it < comm.iterations)
            def _():
                comm.iteration(it)

    @pl.when(step == 0)
    def _():
        for copy in loads:
            copy.start()
        comm.barrier()

    vec = vec_ref[...]
    bo, g1, s1, bd, g2, s2 = (vec[i : i + 1] for i in range(6))
    low_lane = lax.broadcasted_iota(jnp.int32, (SEQ, 128), 1) < HEAD_DIM
    key_row = lax.broadcasted_iota(jnp.int32, (SEQ, SEQ), 0)
    ctx = []
    for c in range(2):
        rows = slice(c * SEQ, c * SEQ + SEQ)
        length = len_ref[comm.t * (2 * pl.num_programs(0)) + 2 * step + c]
        slot(c)
        parts = []
        for pair in range(4):
            cols = slice(128 * pair, 128 * pair + 128)
            qp, kp, vp = q_ref[rows, cols], k_ref[rows, cols], v_ref[rows, cols]
            outs = []
            for h in range(2):
                scores = product_right(jnp.where(low_lane == (h == 0), kp, jnp.zeros((), bf16)), qp)
                scores = jnp.where(key_row < length, scores, -1e9)
                e = jnp.exp(scores - jnp.max(scores, axis=0, keepdims=True))
                p = (e * inverse(jnp.sum(e, axis=0, keepdims=True))).astype(bf16)
                outs.append(product_left(p, vp))
            parts.append(jnp.where(low_lane, outs[0], outs[1]))
        ctx.append(jnp.concatenate(parts, axis=1).astype(bf16))
    ctx = jnp.concatenate(ctx, axis=0)
    slot(2)

    @pl.when(step == 0)
    def _():
        for copy in loads:
            copy.wait()

    s = x_ref[...].astype(f32) + (product(ctx[:, :256], wo[0]) + product(ctx[:, 256:], wo[1]) + bo)
    center = s - row_mean(s)
    normed = center * lax.rsqrt(row_mean(center * center) + EPSILON) * g1 + s1
    low = normed.astype(bf16)
    branch = bd
    for j in range(4):
        h, o = j // 2, 512 * (j % 2)
        bi = jnp.concatenate([bias_ref[h, 2 + o // 256 : 3 + o // 256], bias_ref[h, 3 + o // 256 : 4 + o // 256]], axis=1)
        hid = product(low, wi[h, :, o : o + 512]) + bi
        branch = branch + product((hid * normal_cdf(hid)).astype(bf16), wd[h, o : o + 512])
        if j == 1:
            slot(3)
    s = normed + branch
    center = s - row_mean(s)
    y_ref[...] = (center * lax.rsqrt(row_mean(center * center) + EPSILON) * g2 + s2).astype(bf16)
    slot(4)
    dx = gf_ref[...]
    for h in range(2):
        cols = slice(256 * h, 256 * h + 256)
        for j, ref in ((1, dk_ref), (2, dv_ref)):
            dx = dx + product_right(ref[:, cols], wqkv[h, j])
    dx_ref[...] = dx

    @pl.when(step == pl.num_programs(0) - 1)
    def _():
        def body(it, carry):
            comm.iteration(it)
            return carry

        lax.fori_loop(slots * pl.num_programs(0), comm.iterations, body, 0)
        comm.finish()


def rest(g, small, states, q, k, v, lens, dk, dv, gf, wqkv, wo, wi, wd, bias, vec):
    rows = states.shape[0]
    block = 2 * SEQ
    K, STRIDE, SLOTS = 8, 2, 4
    tile = pl.BlockSpec((block, 512), lambda i: (i, 0))
    vm, hbm = pl.BlockSpec(memory_space=pltpu.VMEM), pl.BlockSpec(memory_space=pl.ANY)
    S = jax.ShapeDtypeStruct
    return pl.pallas_call(
        functools.partial(rest_kernel, SLOTS, K, STRIDE),
        grid=(rows // block,),
        in_specs=[hbm, vm, tile, tile, tile, tile, pl.BlockSpec(memory_space=pltpu.SMEM), tile, tile, tile,
                  hbm, hbm, hbm, hbm, vm, vm],
        out_specs=[hbm, vm, tile, tile],
        out_shape=[S((ROWS, 512), bf16), S(small.shape, f32), S((rows, 512), bf16), S((rows, 512), f32)],
        scratch_shapes=[
            pltpu.VMEM(wqkv.shape, bf16), pltpu.VMEM(wo.shape, bf16), pltpu.VMEM(wi.shape, bf16), pltpu.VMEM(wd.shape, bf16),
            pltpu.SemaphoreType.DMA((4,)),
        ] + Comm.scratch(K, small.shape[0]),
        compiler_params=pltpu.CompilerParams(collective_id=0, has_side_effects=True, vmem_limit_bytes=61 << 20),
        name="rest",
    )(g, small, states, q, k, v, lens, dk, dv, gf, wqkv, wo, wi, wd, bias, vec)


def finish_kernel(
    sums_ref, small_ref, y_in, dx_in,
    y_ref, dx_ref, dq_ref, dk_ref, dv_ref, do_ref, di_ref, dd_ref, bq_ref, bv_ref, bo_ref, g1_ref, s1_ref, bi_ref, bd_ref, g2_ref, s2_ref,
    dd, di, dqkvo, sems,
):
    step = pl.program_id(0)
    t = lax.axis_index("tensor")
    y_ref[...] = y_in[...]
    dx_ref[...] = dx_in[...]
    w = [
        (2, pltpu.make_async_copy(dd, dd_ref, sems.at[0])), (4, pltpu.make_async_copy(di, di_ref, sems.at[1])),
        (5, pltpu.make_async_copy(dqkvo.at[0], dq_ref, sems.at[2])), (5, pltpu.make_async_copy(dqkvo.at[1], dk_ref, sems.at[3])),
        (6, pltpu.make_async_copy(dqkvo.at[2], dv_ref, sems.at[4])),
    ]

    def part(rows):
        return sums_ref[rows].astype(f32)

    @pl.when(step == 0)
    def _():
        pick = lambda i: jnp.where(t == 0, small_ref[i : i + 1, 0:256], small_ref[i : i + 1, 256:512])
        bq_ref[...] = pick(6)
        bv_ref[...] = pick(7)
        bi_ref[...] = jnp.where(
            t == 0, jnp.concatenate([small_ref[8:9], small_ref[9:10]], axis=1), jnp.concatenate([small_ref[10:11], small_ref[11:12]], axis=1)
        )
        for i, ref in enumerate((bo_ref, g1_ref, s1_ref, bd_ref, g2_ref, s2_ref)):
            ref[...] = small_ref[i : i + 1]

    @pl.when(step == 1)
    def _():
        dd[...] = part(slice(0, 1024))
        pltpu.make_async_copy(dd, dd_ref, sems.at[0]).start()

    @pl.when(step == 2)
    def _():
        di[:, 0:512] = part(slice(1024, 1536))
        di[:, 512:1024] = part(slice(1536, 2048))
        pltpu.make_async_copy(di, di_ref, sems.at[1]).start()

    @pl.when(step == 3)
    def _():
        both = part(slice(2048, 2560))
        dqkvo[0], dqkvo[1] = both[:, :256], both[:, 256:]
        dqkvo[2] = part(slice(2560, 3072))[:, :256]
        do_ref[:, 0:256] = sums_ref[2560:2816, 256:512].astype(f32)
        do_ref[:, 256:512] = sums_ref[2816:3072, 256:512].astype(f32)
        for i, ref in enumerate((dq_ref, dk_ref, dv_ref)):
            pltpu.make_async_copy(dqkvo.at[i], ref, sems.at[2 + i]).start()

    @pl.when(step == pl.num_programs(0) - 1)
    def _():
        for _, copy in w:
            copy.wait()


def finish(sums, small, y, dx):
    rows = y.shape[0]
    block = 2 * SEQ
    tile = pl.BlockSpec((block, 512), lambda i: (i, 0))
    vm, hbm = pl.BlockSpec(memory_space=pltpu.VMEM), pl.BlockSpec(memory_space=pl.ANY)
    S, V = jax.ShapeDtypeStruct, pltpu.VMEM
    line = lambda n: S((1, n), f32)
    return pl.pallas_call(
        finish_kernel,
        grid=(rows // block,),
        in_specs=[vm, vm, tile, tile],
        out_specs=[tile, tile, hbm, hbm, hbm, vm, hbm, hbm] + [vm] * 9,
        out_shape=[
            S((rows, 512), bf16), S((rows, 512), f32), S((512, 256), f32), S((512, 256), f32), S((512, 256), f32), S((256, 512), f32),
            S((512, 1024), f32), S((1024, 512), f32), line(256), line(256), line(512), line(512), line(512), line(1024), line(512), line(512), line(512),
        ],
        scratch_shapes=[V((1024, 512), f32), V((512, 1024), f32), V((3, 512, 256), f32), pltpu.SemaphoreType.DMA((5,))],
        compiler_params=pltpu.CompilerParams(vmem_limit_bytes=60 << 20),
        name="finish",
    )(sums, small, y, dx)


def whole_chains(
    states, cotangent, lengths, span_starts, span_ends, query_weight, query_bias, key_weight, value_weight, value_bias,
    output_weight, output_bias, first_gain, first_shift, inner_weight, inner_bias, down_weight, down_bias, second_gain, second_shift,
):
    q, k, v, vec, wqkv, wo, wi, wd, bias = gather(
        states, query_weight, key_weight, value_weight, query_bias, value_bias, inner_bias,
        (output_bias, first_gain, first_shift, down_bias, second_gain, second_shift), output_weight, inner_weight, down_weight,
    )
    g, dk, dv, gf, small = live_rows(lengths, span_starts, span_ends, states, cotangent, q, k, v, wqkv, wo, wi, wd, bias, vec)
    summed, small, output, input_grad = rest(g, small, states, q, k, v, lengths, dk, dv, gf, wqkv, wo, wi, wd, bias, vec)
    (
        output, input_grad, query, key, value, out, inner, down, query_b, value_b, out_b, gain1, shift1, inner_b, down_b, gain2, shift2,
    ) = finish(summed, small, output, input_grad)
    flat = lambda a: a.reshape(-1)
    return (
        output, input_grad, query, flat(query_b), key, value, flat(value_b), out, flat(out_b), flat(gain1), flat(shift1),
        inner, flat(inner_b), down, flat(down_b), flat(gain2), flat(shift2),
    )


def local(*arguments):
    rows, hidden = arguments[0].shape[0], arguments[14].shape[1]
    if rows % SEQ == 0 and lax.axis_size("dp") == 16 and lax.axis_size("tensor") == 2:
        return whole_chains(*arguments)
    return general(*arguments)


def solution(mesh):
    placed = (
        P(("dp", "tensor"), None),
        P(("dp", "tensor"), None),
        P("dp"),
        P("dp"),
        P("dp"),
        P(None, "tensor"),
        P("tensor"),
        P(None, "tensor"),
        P(None, "tensor"),
        P("tensor"),
        P("tensor", None),
        P(),
        P(),
        P(),
        P(None, "tensor"),
        P("tensor"),
        P("tensor", None),
        P(),
        P(),
        P(),
    )
    return jax.shard_map(
        local,
        mesh=mesh,
        in_specs=placed,
        out_specs=(
            P(("dp", "tensor"), None),
            P(("dp", "tensor"), None),
            P(None, "tensor"),
            P("tensor"),
            P(None, "tensor"),
            P(None, "tensor"),
            P("tensor"),
            P("tensor", None),
            P(),
            P(),
            P(),
            P(None, "tensor"),
            P("tensor"),
            P("tensor", None),
            P(),
            P(),
            P(),
        ),
        check_vma=False,
    )
```

```python
import functools

import jax
import jax.numpy as jnp
from jax import lax
from jax.experimental import pallas as pl
from jax.experimental.pallas import tpu as pltpu
from jax.sharding import PartitionSpec as P

MESH = pl.DeviceIdType.MESH
f32, bf16 = jnp.float32, jnp.bfloat16
HEAD_DIM = 64
SEQ = 160
ROWS = 3072
SCALE = HEAD_DIM ** (-0.5)
ATT_BLOCK = 32
FFN_BLOCK = 256
EPSILON = 1e-12


def product(left, right):
    return jnp.dot(left, right, preferred_element_type=jnp.float32)


def product_left(left, right):
    return lax.dot_general(
        left, right, (((0,), (0,)), ((), ())), preferred_element_type=jnp.float32
    )


def product_right(left, right):
    return lax.dot_general(
        left, right, (((1,), (1,)), ((), ())), preferred_element_type=jnp.float32
    )


def layer_norm(values, gain, shift):
    center = values - jnp.mean(values, axis=-1, keepdims=True)
    spread = jnp.mean(center * center, axis=-1, keepdims=True)
    return center * lax.rsqrt(spread + EPSILON) * gain + shift


def exact_gelu(values):
    return jax.nn.gelu(values, approximate=False)


def attention_scores(queries, keys, key_live):
    scores = jnp.einsum(
        "cqhd,ckhd->chqk", queries, keys, preferred_element_type=jnp.float32
    ) * HEAD_DIM ** (-0.5)
    return jnp.where(key_live[:, None, None, :], scores, -1000000000.0)


def per_row(table, picker):
    return jnp.sum(jnp.where(picker, table[None, :], 0), axis=1)


def column_sum(values):
    return jnp.sum(values.astype(jnp.float32), axis=0)


def general(
    states,
    cotangent,
    lengths,
    span_starts,
    span_ends,
    query_weight,
    query_bias,
    key_weight,
    value_weight,
    value_bias,
    output_weight,
    output_bias,
    first_gain,
    first_shift,
    inner_weight,
    inner_bias,
    down_weight,
    down_bias,
    second_gain,
    second_shift,
):
    slice_rows = states.shape[0]
    chains = lengths.shape[0]
    group_rows = chains * SEQ
    heads_local = query_weight.shape[1] // HEAD_DIM
    layout = (chains, SEQ, heads_local, HEAD_DIM)
    whole = lax.all_gather(states, "tensor", axis=0, tiled=True)
    queries = (product(whole, query_weight) + query_bias).astype(jnp.bfloat16).reshape(layout)
    keys_low = product(whole, key_weight).astype(jnp.bfloat16).reshape(layout)
    values_low = (product(whole, value_weight) + value_bias).astype(jnp.bfloat16).reshape(layout)
    key_live = jnp.arange(SEQ, dtype=jnp.int32)[None, :] < lengths[:, None]
    scores = attention_scores(queries, keys_low, key_live)
    highest = jnp.max(scores, axis=-1, keepdims=True)
    logsum = highest + jnp.log(jnp.sum(jnp.exp(scores - highest), axis=-1, keepdims=True))
    probs_low = jnp.exp(scores - logsum).astype(jnp.bfloat16)
    context = jnp.einsum(
        "chqk,ckhd->cqhd", probs_low, values_low, preferred_element_type=jnp.float32
    )
    context = context.reshape(group_rows, heads_local * HEAD_DIM).astype(jnp.bfloat16)
    attended = lax.psum_scatter(
        product(context, output_weight), "tensor", scatter_dimension=0, tiled=True
    ) + output_bias.astype(jnp.float32)
    first_sum = states.astype(jnp.float32) + attended
    normed, first_pull = jax.vjp(
        layer_norm, first_sum, first_gain.astype(jnp.float32), first_shift.astype(jnp.float32)
    )
    normed_low = normed.astype(jnp.bfloat16)
    normed_all = lax.all_gather(normed_low, "tensor", axis=0, tiled=True)
    hidden = product(normed_all, inner_weight) + inner_bias.astype(jnp.float32)
    activation, gelu_pull = jax.vjp(exact_gelu, hidden)
    activation_low = activation.astype(jnp.bfloat16)
    branch = lax.psum_scatter(
        product(activation_low, down_weight), "tensor", scatter_dimension=0, tiled=True
    )
    second_sum = normed + (branch + down_bias.astype(jnp.float32))
    output, second_pull = jax.vjp(
        layer_norm, second_sum, second_gain.astype(jnp.float32), second_shift.astype(jnp.float32)
    )
    row_ids = lax.axis_index("tensor") * slice_rows + jnp.arange(slice_rows, dtype=jnp.int32)
    chain_ids = row_ids // SEQ
    position = row_ids % SEQ
    picker = chain_ids[:, None] == jnp.arange(chains, dtype=jnp.int32)[None, :]
    live = (
        (position >= per_row(span_starts, picker))
        & (position < per_row(span_ends, picker))
        & (position < per_row(lengths, picker))
    )
    grad_out = jnp.where(live[:, None], cotangent.astype(jnp.float32), 0.0)
    grad_second, second_gain_part, second_shift_part = second_pull(grad_out)
    grad_branch = grad_second.astype(jnp.bfloat16)
    down_bias_part = column_sum(grad_branch)
    grad_branch_all = lax.all_gather(grad_branch, "tensor", axis=0, tiled=True)
    down_weight_part = product_left(activation_low, grad_branch_all)
    grad_activation = product_right(grad_branch_all, down_weight)
    (grad_hidden,) = gelu_pull(grad_activation)
    grad_hidden_low = grad_hidden.astype(jnp.bfloat16)
    inner_weight_part = product_left(normed_all, grad_hidden_low)
    inner_bias_part = column_sum(grad_hidden_low)
    grad_normed = lax.psum_scatter(
        product_right(grad_hidden_low, inner_weight), "tensor", scatter_dimension=0, tiled=True
    )
    grad_first, first_gain_part, first_shift_part = first_pull(grad_second + grad_normed)
    grad_attended = grad_first.astype(jnp.bfloat16)
    output_bias_part = column_sum(grad_attended)
    grad_attended_all = lax.all_gather(grad_attended, "tensor", axis=0, tiled=True)
    output_weight_part = product_left(context, grad_attended_all)
    grad_context = (
        product_right(grad_attended_all, output_weight).astype(jnp.bfloat16).reshape(layout)
    )
    probs = jnp.exp(attention_scores(queries, keys_low, key_live) - logsum)
    grad_probs = jnp.einsum(
        "cqhd,ckhd->chqk", grad_context, values_low, preferred_element_type=jnp.float32
    )
    grad_scores = probs * (grad_probs - jnp.sum(probs * grad_probs, axis=-1, keepdims=True))
    grad_scores_low = grad_scores.astype(jnp.bfloat16)
    scale = HEAD_DIM ** (-0.5)
    grad_queries = (
        jnp.einsum("chqk,ckhd->cqhd", grad_scores_low, keys_low, preferred_element_type=jnp.float32)
        * scale
    )
    grad_keys = (
        jnp.einsum("chqk,cqhd->ckhd", grad_scores_low, queries, preferred_element_type=jnp.float32)
        * scale
    )
    grad_values = jnp.einsum(
        "chqk,cqhd->ckhd", probs_low, grad_context, preferred_element_type=jnp.float32
    )
    flat = (group_rows, heads_local * HEAD_DIM)
    grad_queries = grad_queries.reshape(flat).astype(jnp.bfloat16)
    grad_keys = grad_keys.reshape(flat).astype(jnp.bfloat16)
    grad_values = grad_values.reshape(flat).astype(jnp.bfloat16)
    query_weight_part = product_left(whole, grad_queries)
    key_weight_part = product_left(whole, grad_keys)
    value_weight_part = product_left(whole, grad_values)
    query_bias_part = column_sum(grad_queries)
    value_bias_part = column_sum(grad_values)
    grad_whole = (
        product_right(grad_queries, query_weight)
        + product_right(grad_keys, key_weight)
        + product_right(grad_values, value_weight)
    )
    input_grad = (
        lax.psum_scatter(
            grad_whole.astype(jnp.bfloat16), "tensor", scatter_dimension=0, tiled=True
        ).astype(jnp.float32)
        + grad_first
    )
    (
        query_weight_grad,
        query_bias_grad,
        key_weight_grad,
        value_weight_grad,
        value_bias_grad,
        output_weight_grad,
        inner_weight_grad,
        inner_bias_grad,
        down_weight_grad,
    ) = (
        lax.psum(query_weight_part.astype(jnp.bfloat16), "dp").astype(jnp.float32),
        lax.psum(query_bias_part.astype(jnp.bfloat16), "dp").astype(jnp.float32),
        lax.psum(key_weight_part.astype(jnp.bfloat16), "dp").astype(jnp.float32),
        lax.psum(value_weight_part.astype(jnp.bfloat16), "dp").astype(jnp.float32),
        lax.psum(value_bias_part.astype(jnp.bfloat16), "dp").astype(jnp.float32),
        lax.psum(output_weight_part.astype(jnp.bfloat16), "dp").astype(jnp.float32),
        lax.psum(inner_weight_part.astype(jnp.bfloat16), "dp").astype(jnp.float32),
        lax.psum(inner_bias_part.astype(jnp.bfloat16), "dp").astype(jnp.float32),
        lax.psum(down_weight_part.astype(jnp.bfloat16), "dp").astype(jnp.float32),
    )
    (
        output_bias_grad,
        first_gain_grad,
        first_shift_grad,
        down_bias_grad,
        second_gain_grad,
        second_shift_grad,
    ) = lax.psum(
        (
            output_bias_part,
            first_gain_part,
            first_shift_part,
            down_bias_part,
            second_gain_part,
            second_shift_part,
        ),
        ("dp", "tensor"),
    )
    return (
        output.astype(jnp.bfloat16),
        input_grad,
        query_weight_grad,
        query_bias_grad,
        key_weight_grad,
        value_weight_grad,
        value_bias_grad,
        output_weight_grad,
        output_bias_grad,
        first_gain_grad,
        first_shift_grad,
        inner_weight_grad,
        inner_bias_grad,
        down_weight_grad,
        down_bias_grad,
        second_gain_grad,
        second_shift_grad,
    )


class Comm:
    NSTAGE = 10
    def __init__(self, K, g, small, out, sout, bufs, stride=1):
        self.stride = stride
        self.K = K; self.CH = ROWS // K; self.SB = self.CH // 3
        self.g, self.small, self.out_hbm, self.sout = g, small, out, sout
        (self.core_buf, self.acc, self.r1, self.r2, self.r3, self.r4, self.out, self.sm, self.csem, self.rsem, self.asem, self.smsem, self.fsem) = bufs
        dp = lax.axis_index("dp"); t = lax.axis_index("tensor")
        self.t = t
        x = lax.rem(dp, 2); y = lax.rem(dp // 2, 2); p = lax.rem(dp // 4, 2); q = dp // 8
        self.bits = (x, y, p, q)
        self.parts = tuple(dp + w * (1 - 2 * b) for w, b in ((1, x), (2, y), (4, p), (8, q)))
        self.dp = dp
    def barrier(self):
        b = pltpu.get_barrier_semaphore()
        pl.semaphore_signal(b, inc=1, device_id=(self.dp, 1 - self.t), device_id_type=MESH)
        for n in self.parts:
            pl.semaphore_signal(b, inc=1, device_id=(n, self.t), device_id_type=MESH)
        pl.semaphore_wait(b, 5)
    def rc(self, src, dst, s, r, n):
        return pltpu.make_async_remote_copy(src_ref=src, dst_ref=dst, send_sem=s, recv_sem=r, device_id=(n, self.t), device_id_type=MESH)
    def core_copy(self, k):
        return pltpu.make_async_remote_copy(src_ref=self.g.at[1 - self.t, pl.ds(k * self.CH, self.CH)], dst_ref=self.core_buf.at[k],
            send_sem=self.csem.at[0, k], recv_sem=self.csem.at[1, k], device_id=(self.dp, 1 - self.t), device_id_type=MESH)
    def own_copy(self, k):
        sl = pl.ds(k * self.CH, self.CH)
        return pltpu.make_async_copy(self.g.at[self.t, sl], self.acc.at[sl], self.csem.at[2, k])
    def order(self, k, r):
        B, N = self.bits, self.parts
        X, Y, Pp, Qq = ((B[i], N[i]) for i in range(4))
        if r == 0: return X, Y, Pp, Qq
        if r == 1: return Y, X, Pp, Qq
        if isinstance(k, int):
            return (Pp, X, Y, Qq) if k % 2 == 0 else (Pp, Y, X, Qq)
        even = lax.rem(k, 2) == 0
        U = (jnp.where(even, B[0], B[1]), jnp.where(even, N[0], N[1]))
        V = (jnp.where(even, B[1], B[0]), jnp.where(even, N[1], N[0]))
        return Pp, U, V, Qq
    def region(self, k, r, depth, keep):
        o = self.order(k, r)
        rows, cols = self.SB, 512
        r0, c0 = k * self.CH + r * self.SB, 0
        for i in range(depth):
            b = o[i][0]
            if i == depth - 1 and not keep: b = 1 - b
            if i < 2:
                rows //= 2; r0 = r0 + b * rows
            else:
                cols //= 2; c0 = c0 + b * cols
        if depth > 2: c0 = pl.multiple_of(c0, 128)
        return pl.ds(pl.multiple_of(r0, 16), rows), pl.ds(c0, cols)
    def rs(self, k, r, i):
        n = self.order(k, r)[i][1]
        buf = (self.r1, self.r2, self.r3, self.r4)[i]
        return self.rc(self.acc.at[self.region(k, r, i + 1, False)], buf.at[k, r], self.rsem.at[0, i, k, r], self.rsem.at[1, i, k, r], n)
    def ag(self, k, r, i):
        n = self.order(k, r)[i][1]
        sl = self.region(k, r, i + 1, True)
        return self.rc(self.out.at[sl], self.out.at[sl], self.asem.at[0, i, k, r], self.asem.at[1, i, k, r], n)
    def small_copy(self, i):
        dev = (self.dp, 1 - self.t) if i == 0 else (self.parts[i - 1], self.t)
        src = self.small if i == 0 else self.sm.at[1, i - 1]
        return pltpu.make_async_remote_copy(src_ref=src, dst_ref=self.sm.at[0, i], send_sem=self.smsem.at[0, i], recv_sem=self.smsem.at[1, i], device_id=dev, device_id_type=MESH)
    def stage(self, s, k):
        if s == 0:
            self.core_copy(k).start()
            self.own_copy(k).start()
        elif s == 1:
            self.core_copy(k).wait_recv()
            sl = pl.ds(pl.multiple_of(k * self.CH, 16), self.CH)
            self.own_copy(k).wait()
            self.acc[sl] = (self.acc[sl].astype(f32) + self.core_buf[k].astype(f32)).astype(bf16)
            for r in range(3): self.rs(k, r, 0).start()
        elif s <= 5:
            i = s - 2
            buf = (self.r1, self.r2, self.r3, self.r4)[i]
            for r in range(3):
                self.rs(k, r, i).wait_recv()
                sl = self.region(k, r, i + 1, True)
                v = (self.acc[sl].astype(f32) + buf[k, r].astype(f32)).astype(bf16)
                if i < 3:
                    self.acc[sl] = v
                    self.rs(k, r, i + 1).start()
                else:
                    self.out[sl] = v
                    self.ag(k, r, 3).start()
        else:
            i = 9 - s
            for r in range(3):
                self.ag(k, r, i).wait_recv()
                if i > 0: self.ag(k, r, i - 1).start()
            if i == 0: self.final_copy(k).start()
    def final_copy(self, k):
        sl = pl.ds(k * self.CH, self.CH)
        return pltpu.make_async_copy(self.out.at[sl], self.out_hbm.at[sl], self.fsem.at[k])
    def small_stage(self, i):
        if i > 0:
            self.small_copy(i - 1).wait_recv()
            own = self.small[...] if i == 1 else self.sm[1, i - 2]
            v = own + self.sm[0, i - 1]
            if i < 5: self.sm[1, i - 1] = v
            else: self.sout[...] = v
        if i < 5: self.small_copy(i).start()
    def iteration_static(self, it):
        for s in reversed(range(self.NSTAGE)):
            k = it - s * self.stride
            if 0 <= k < self.K: self.stage(s, k)
        for i in range(6):
            if it == i * self.stride + 1: self.small_stage(i)
    def iteration(self, it):
        for s in reversed(range(self.NSTAGE)):
            k = it - s * self.stride
            @pl.when((k >= 0) & (k < self.K))
            def _(s=s, k=k):
                self.stage(s, k)
        for i in range(6):
            @pl.when(it == i * self.stride + 1)
            def _(i=i): self.small_stage(i)
    @property
    def iterations(self): return self.K + (self.NSTAGE - 1) * self.stride
    def finish(self):
        def body(k, c):
            self.core_copy(k).wait_send(); self.final_copy(k).wait()
            for r in range(3):
                for i in range(4):
                    self.rs(k, r, i).wait_send(); self.ag(k, r, i).wait_send()
            return c
        lax.fori_loop(0, self.K, body, 0)
        for i in range(5): self.small_copy(i).wait_send()
    @staticmethod
    def scratch(K, S):
        SB = ROWS // K // 3
        D = pltpu.SemaphoreType.DMA
        return [pltpu.VMEM((K, 3 * SB, 512), bf16), pltpu.VMEM((ROWS, 512), bf16),
            pltpu.VMEM((K, 3, SB // 2, 512), bf16), pltpu.VMEM((K, 3, SB // 4, 512), bf16),
            pltpu.VMEM((K, 3, SB // 4, 256), bf16), pltpu.VMEM((K, 3, SB // 4, 128), bf16),
            pltpu.VMEM((ROWS, 512), bf16), pltpu.VMEM((2, 5, S, 512), f32),
            D((3, K)), D((2, 4, K, 3)), D((2, 4, K, 3)), D((2, 5)), D((K,))]


def gather_kernel(
    x_ref, wq_ref, wk_ref, wv_ref, bq_ref, bv_ref, bi_ref, bo_ref, g1_ref, s1_ref, bd_ref, g2_ref, s2_ref, wo_ref, wi_ref, wd_ref,
    q_ref, k_ref, v_ref, vec_ref, wqkv_out, wo_out, wi_out, wd_out, bias_out,
    wqkv, wo, wi, wd, bias, near, sent, came,
):
    step = pl.program_id(0)
    dp, t = lax.axis_index("dp"), lax.axis_index("tensor")

    def pair(i, src, dst):
        return pltpu.make_async_remote_copy(
            src_ref=src, dst_ref=dst, send_sem=sent.at[i], recv_sem=came.at[i],
            device_id=(dp, 1 - t), device_id_type=MESH,
        )

    first = [
        pair(0, wq_ref, wqkv.at[t, 0]), pair(1, wk_ref, wqkv.at[t, 1]), pair(2, wv_ref, wqkv.at[t, 2]),
        pair(3, bias.at[t], bias.at[t]),
    ]
    later = [pair(4, wo.at[t], wo.at[t]), pair(5, wi.at[t], wi.at[t]), pair(6, wd.at[t], wd.at[t])]
    own = [pltpu.make_async_copy(a, b.at[t], near.at[i]) for i, (a, b) in enumerate(((wo_ref, wo), (wi_ref, wi), (wd_ref, wd)))]
    keep = [pltpu.make_async_copy(wqkv, wqkv_out, near.at[3]), pltpu.make_async_copy(bias, bias_out, near.at[4])]
    keep_later = [pltpu.make_async_copy(a, b, near.at[5 + i]) for i, (a, b) in enumerate(((wo, wo_out), (wi, wi_out), (wd, wd_out)))]

    @pl.when(step == 0)
    def _():
        barrier = pltpu.get_barrier_semaphore()
        pl.semaphore_signal(barrier, inc=1, device_id=(dp, 1 - t), device_id_type=MESH)
        bias[t, 0:1] = bq_ref[...].astype(f32).reshape(1, 256)
        bias[t, 1:2] = bv_ref[...].astype(f32).reshape(1, 256)
        for i in range(4):
            bias[t, 2 + i : 3 + i] = bi_ref[pl.ds(256 * i, 256)].astype(f32).reshape(1, 256)
        bias[t, 6:8] = jnp.zeros((2, 256), f32)
        for copy in own:
            copy.start()
        for i, ref in enumerate((bo_ref, g1_ref, s1_ref, bd_ref, g2_ref, s2_ref)):
            vec_ref[i : i + 1] = ref[...].astype(f32).reshape(1, 512)
        vec_ref[6:8] = jnp.zeros((2, 512), f32)
        pl.semaphore_wait(barrier, 1)
        for copy in first:
            copy.start()
        for j, ref in enumerate((wq_ref, wk_ref, wv_ref)):
            wqkv[t, j] = ref[...]
        for copy in first:
            copy.wait_recv()
        for copy in keep:
            copy.start()
        for mine, copy in zip(own, later):
            mine.wait()
            copy.start()

    x = x_ref[...]
    for h in range(2):
        cols = slice(256 * h, 256 * h + 256)
        q_ref[:, cols] = ((product(x, wqkv[h, 0]) + bias[h, 0:1]).astype(bf16).astype(f32) * SCALE).astype(bf16)
        k_ref[:, cols] = product(x, wqkv[h, 1]).astype(bf16)
        v_ref[:, cols] = (product(x, wqkv[h, 2]) + bias[h, 1:2]).astype(bf16)

    @pl.when(step == pl.num_programs(0) // 2)
    def _():
        for copy, out in zip(later, keep_later):
            copy.wait_recv()
            out.start()

    @pl.when(step == pl.num_programs(0) - 1)
    def _():
        for copy in first:
            copy.wait_send()
        for copy in later:
            copy.wait_send()
        for copy in keep + keep_later:
            copy.wait()


def gather(states, wq, wk, wv, bq, bv, bi, vectors, wo, wi, wd):
    rows = states.shape[0]
    block = 2 * SEQ
    whole = lambda a: pl.BlockSpec(a.shape, lambda i: (0,) * a.ndim)
    tile = pl.BlockSpec((block, 512), lambda i: (i, 0))
    hbm, vm = pl.BlockSpec(memory_space=pl.ANY), pl.BlockSpec(memory_space=pltpu.VMEM)
    D = pltpu.SemaphoreType.DMA
    S = jax.ShapeDtypeStruct
    return pl.pallas_call(
        gather_kernel,
        grid=(rows // block,),
        in_specs=[tile, whole(wq), whole(wk), whole(wv)] + [vm] * 9 + [hbm, hbm, hbm],
        out_specs=[tile, tile, tile, vm, hbm, hbm, hbm, hbm, hbm],
        out_shape=[S((rows, 512), bf16)] * 3 + [
            S((8, 512), f32),
            S((2, 3, 512, 256), bf16), S((2, 256, 512), bf16), S((2, 512, 1024), bf16), S((2, 1024, 512), bf16), S((2, 8, 256), f32),
        ],
        scratch_shapes=[
            pltpu.VMEM((2, 3, 512, 256), bf16), pltpu.VMEM((2, 256, 512), bf16), pltpu.VMEM((2, 512, 1024), bf16),
            pltpu.VMEM((2, 1024, 512), bf16), pltpu.VMEM((2, 8, 256), f32), D((8,)), D((7,)), D((7,)),
        ],
        compiler_params=pltpu.CompilerParams(collective_id=1, has_side_effects=True, vmem_limit_bytes=60 << 20),
        name="gather",
    )(states, wq, wk, wv, bq, bv, bi, *vectors, wo, wi, wd)


def normal_cdf(h):
    return 0.5 + 0.5 * lax.erf(h * 0.7071067811865476)


def inverse(a):
    return pltpu.reciprocal(a, approx=True)


def row_mean(a):
    return jnp.sum(a, axis=-1, keepdims=True) * (1.0 / 512)


WINDOW = 64
FRONT = 8


def live_kernel(
    len_ref, start_ref, end_ref,
    x_hbm, cot_hbm, q_hbm, k_hbm, v_hbm, wqkv_hbm, wo_hbm, wi_hbm, wd_hbm, bias_ref, vec_ref,
    g_out, dk_out, dv_out, dx_out, small_out,
    x_all, cot_all, q_all, k_all, v_all, wq, wo, wi, wd, context, inputs, upstream, first, dv_all, acc_k, acc_v,
    acc_d, acc_i, acc_o, gelu_grad, act, stage, apart, win_chain, win_pos, win_dst, chain_win, in_sems, w_sems, out_sems, dx_sems,
):
    chains = len_ref.shape[0] // 2
    t = lax.axis_index("tensor")
    W, R = WINDOW, FFN_BLOCK
    rows_all = chains * SEQ
    dk_all = cot_all
    spread = gelu_grad

    def chain_loads(c):
        rows = pl.ds(c * SEQ, SEQ)
        return [
            pltpu.make_async_copy(a.at[rows], b.at[rows], in_sems.at[i, c])
            for i, (a, b) in enumerate(((q_hbm, q_all), (k_hbm, k_all), (v_hbm, v_all), (cot_hbm, cot_all), (x_hbm, x_all)))
        ]

    loads = [
        pltpu.make_async_copy(a, b, w_sems.at[i])
        for i, (a, b) in enumerate((
            (wo_hbm, wo), (wi_hbm, wi), (wd_hbm, wd), (wqkv_hbm.at[0, 0], wq.at[0]), (wqkv_hbm.at[1, 0], wq.at[1]),
        ))
    ]

    def start_loads(c, carry):
        for copy in chain_loads(c):
            copy.start()
        return carry

    lax.fori_loop(0, chains, start_loads, 0)
    for copy in loads:
        copy.start()

    def list_chain(c, carry):
        at, offset = carry
        start = start_ref[t * chains + c]
        end = jnp.minimum(end_ref[t * chains + c], len_ref[t * chains + c])
        r16 = (start // 16) * 16
        r8 = (start // 8) * 8
        count = jnp.maximum((end - r16 + W - 1) // W, 1)
        chain_win[c] = at

        def put(i, carry):
            win_chain[at + i] = c
            win_pos[at + i] = r16 + W * i
            win_dst[at + i] = offset + r16 - r8 + W * i
            return carry

        lax.fori_loop(0, count, put, 0)
        return at + count, offset + jnp.maximum(((end + 7) // 8) * 8 - r8, 0)

    n_win, n_end = lax.fori_loop(0, chains, list_chain, (0, FRONT))
    chain_win[chains] = n_win
    trash = context.shape[0] - W
    win_chain[n_win] = chains - 1
    win_pos[n_win] = SEQ
    win_dst[n_win] = trash
    n = n_end - FRONT

    acc_d[...] = jnp.zeros_like(acc_d)
    acc_i[...] = jnp.zeros_like(acc_i)
    acc_o[...] = jnp.zeros_like(acc_o)
    acc_k[...] = jnp.zeros_like(acc_k)
    acc_v[...] = jnp.zeros_like(acc_v)
    small_out[...] = jnp.zeros_like(small_out)
    for ref in (context, upstream, first):
        ref[pl.ds(trash, W)] = jnp.zeros((W, 512), f32)
    for ref in (x_all, cot_all, q_all):
        ref[pl.ds(rows_all, W)] = jnp.zeros((W, 512), bf16)

    lane_head = lax.broadcasted_iota(jnp.int32, (W, 256), 1) // HEAD_DIM
    own = lax.broadcasted_iota(jnp.int32, (4 * W, 256), 1) // HEAD_DIM == lax.broadcasted_iota(jnp.int32, (4 * W, 256), 0) // W
    apart[...] = jnp.where(own, 1.0, 0.0).astype(bf16)
    key_row = lax.broadcasted_iota(jnp.int32, (SEQ, 4 * W), 0)
    row_id = lax.broadcasted_iota(jnp.int32, (W, 512), 0)

    def heads_apart(rows):
        return jnp.concatenate([rows] * 4, axis=0) * apart[...]

    def heads_together(full):
        out = full[3 * W :]
        for h in (2, 1, 0):
            out = jnp.where(lane_head == h, full[h * W : (h + 1) * W], out)
        return out

    def window(i):
        c = win_chain[i]
        pos = win_pos[i]
        start = start_ref[t * chains + c]
        length = len_ref[t * chains + c]
        end = jnp.minimum(end_ref[t * chains + c], length)
        src = pl.ds(pl.multiple_of(c * SEQ + pos, 16), W)
        dst = pl.multiple_of(win_dst[i], 8)
        keys = pl.ds(pl.multiple_of(c * SEQ, 32), SEQ)
        live = (row_id + pos >= start) & (row_id + pos < end)
        whole = pos + 8 > start
        return c, pos, length, src, dst, keys, live, whole

    def put_rows(ref, dst, whole, rows):
        head = pl.ds(dst, 8)
        ref[head] = jnp.where(whole, rows[:8], ref[head])
        ref[pl.ds(pl.multiple_of(dst + 8, 8), W - 8)] = rows[8:]

    def softmax(scores, length):
        scores = jnp.where(key_row < length, scores, -1e9)
        e = jnp.exp(scores - jnp.max(scores, axis=0, keepdims=True))
        return e * inverse(jnp.sum(e, axis=0, keepdims=True))

    def forward(i, waited):
        last = win_chain[2 * i + 1]

        def wait_chain(c, carry):
            for copy in chain_loads(c):
                copy.wait()
            return carry

        lax.fori_loop(waited, last + 1, wait_chain, 0)
        wins = [window(2 * i + u) for u in range(2)]
        streams = [(w, slice(256 * g, 256 * g + 256)) for w in wins for g in range(2)]
        qs = [heads_apart(q_all[w[3], cols]) for w, cols in streams]
        scores = [product_right(k_all[w[5], cols], q) for (w, cols), q in zip(streams, qs)]
        probs = [softmax(s, w[2]).astype(bf16) for (w, _), s in zip(streams, scores)]
        outs = [product_left(p, v_all[w[5], cols]) for (w, cols), p in zip(streams, probs)]
        outs = [heads_together(o) for o in outs]
        for u, (c, pos, length, src, dst, keys, live, whole) in enumerate(wins):
            put_rows(context, dst, whole, jnp.concatenate(outs[2 * u : 2 * u + 2], axis=1))
            put_rows(inputs, dst, whole, x_all[src].astype(f32))
            put_rows(upstream, dst, whole, jnp.where(live, cot_all[src].astype(f32), 0.0))
        return last + 1

    steps = (n_win + 1) // 2
    waited = lax.fori_loop(0, steps, forward, 0)

    tail = pl.ds(pl.multiple_of(n_end, 8), R)
    for ref in (context, inputs, upstream):
        ref[tail] = jnp.zeros((R, 512), f32)
    for copy in loads:
        copy.wait()
    vec = vec_ref[...]
    bo, g1, s1, bd, g2, s2 = (vec[i : i + 1] for i in range(6))
    blocks = (n + R - 1) // R

    def feed_forward(b, carry):
        rows = pl.ds(pl.multiple_of(FRONT + b * R, 8), R)
        ctx = context[rows].astype(bf16)
        attended = product(ctx[:, :256], wo[0]) + product(ctx[:, 256:], wo[1]) + bo
        s = inputs[rows] + attended
        center = s - row_mean(s)
        rstd1 = lax.rsqrt(row_mean(center * center) + EPSILON)
        hat1 = center * rstd1
        normed = hat1 * g1 + s1
        low = normed.astype(bf16)
        branch = jnp.zeros((R, 512), f32) + bd
        place = [(j // 2, 512 * (j % 2)) for j in range(4)]

        def up_part(j):
            h, o = place[j]
            bi = jnp.concatenate([bias_ref[h, 2 + o // 256 : 3 + o // 256], bias_ref[h, 3 + o // 256 : 4 + o // 256]], axis=1)
            return product(low, wi[h, :, o : o + 512]) + bi

        ahead = up_part(0)
        for j in range(4):
            h, o = place[j]
            hid, ahead = ahead, up_part(j + 1) if j < 3 else None
            cdf = normal_cdf(hid)
            a = (hid * cdf).astype(bf16)
            gelu_grad[j] = cdf + hid * (0.3989422804014327 * jnp.exp(-0.5 * hid * hid))
            act[j] = a
            branch = branch + product(a, wd[h, o : o + 512])
        s = normed + branch
        center = s - row_mean(s)
        rstd2 = lax.rsqrt(row_mean(center * center) + EPSILON)
        hat2 = center * rstd2
        up = upstream[rows]
        gy = up * g2
        grad = rstd2 * (gy - row_mean(gy) - hat2 * row_mean(gy * hat2))
        gb = grad.astype(bf16)
        gn = grad
        back_part = lambda j: product_right(gb, wd[place[j][0], place[j][1] : place[j][1] + 512])
        ahead = back_part(0)
        for j in range(4):
            h, o = place[j]
            ga, ahead = ahead, back_part(j + 1) if j < 3 else None
            acc_d[h, o : o + 512] += product_left(act[j], gb)
            gh = (ga * gelu_grad[j]).astype(bf16)
            gn = gn + product_right(gh, wi[h, :, o : o + 512])
            acc_i[j] += product_left(low, gh)
            small_out[8 + j : 9 + j] += jnp.sum(gh.astype(f32), axis=0, keepdims=True)
        small_out[1:2] += jnp.sum(gn * hat1, axis=0, keepdims=True)
        small_out[2:3] += jnp.sum(gn, axis=0, keepdims=True)
        small_out[3:4] += jnp.sum(gb.astype(f32), axis=0, keepdims=True)
        small_out[4:5] += jnp.sum(up * hat2, axis=0, keepdims=True)
        small_out[5:6] += jnp.sum(up, axis=0, keepdims=True)
        gy = gn * g1
        grad = rstd1 * (gy - row_mean(gy) - hat1 * row_mean(gy * hat1))
        first[rows] = grad
        ga = grad.astype(bf16)
        small_out[0:1] += jnp.sum(ga.astype(f32), axis=0, keepdims=True)
        acc_o[...] += product_left(ctx, ga)
        upstream[rows] = jnp.concatenate([product_right(ga, wo[0]), product_right(ga, wo[1])], axis=1)
        return carry

    lax.fori_loop(0, blocks, feed_forward, 0)

    def out_copy(h, part):
        rows = pl.ds(0, 2048) if part == 0 else pl.ds(2048, 1024)
        return pltpu.make_async_copy(stage.at[h, rows], g_out.at[h, rows], out_sems.at[2 * part + h])

    for h in range(2):
        stage[h, 0:1024] = acc_d[h].astype(bf16)
        stage[h, 1024:1536] = acc_i[2 * h].astype(bf16)
        stage[h, 1536:2048] = acc_i[2 * h + 1].astype(bf16)
        out_copy(h, 0).start()
        stage[h, 2560:2816, 256:512] = acc_o[256 * h : 256 * h + 256, 0:256].astype(bf16)
        stage[h, 2816:3072, 256:512] = acc_o[256 * h : 256 * h + 256, 256:512].astype(bf16)

    def backward(i, carry):
        wins = [window(2 * i + u) for u in range(2)]
        streams = [(w, slice(256 * g, 256 * g + 256)) for w in wins for g in range(2)]
        gcs = [jnp.where(w[6], upstream[pl.ds(w[4], W)], 0.0).astype(bf16) for w in wins]
        qs = [heads_apart(q_all[w[3], cols]) for w, cols in streams]
        gs = [heads_apart(gcs[s // 2][:, cols]) for s, (_, cols) in enumerate(streams)]
        scores = [product_right(k_all[w[5], cols], q) for (w, cols), q in zip(streams, qs)]
        gps = [product_right(v_all[w[5], cols], g) for (w, cols), g in zip(streams, gs)]
        probs = [softmax(s, w[2]) for (w, _), s in zip(streams, scores)]
        dss = [(p * (gp - jnp.sum(p * gp, axis=0, keepdims=True))).astype(bf16) for p, gp in zip(probs, gps)]
        dvs = [product(p.astype(bf16), g) for p, g in zip(probs, gs)]
        dks = [product(ds, q) for ds, q in zip(dss, qs)]
        dqs = [product_left(ds, k_all[w[5], cols]) for (w, cols), ds in zip(streams, dss)]
        for u, w in enumerate(wins):
            same = jnp.where((i + u > 0) & (win_chain[jnp.maximum(2 * i + u - 1, 0)] == w[0]), 1.0, 0.0)
            dk = acc_k[...] * same + jnp.concatenate(dks[2 * u : 2 * u + 2], axis=1)
            dv = acc_v[...] * same + jnp.concatenate(dvs[2 * u : 2 * u + 2], axis=1)
            acc_k[...] = dk
            acc_v[...] = dv
            dk_all[w[5]] = dk.astype(bf16)
            dv_all[w[5]] = dv.astype(bf16)
        outs = [heads_together(dq) * SCALE for dq in dqs]
        for u, w in enumerate(wins):
            put_rows(context, w[4], w[7], jnp.concatenate(outs[2 * u : 2 * u + 2], axis=1))
        return carry

    lax.fori_loop(0, steps, backward, 0)
    keep = [
        pltpu.make_async_copy(dk_all.at[pl.ds(0, rows_all)], dk_out, out_sems.at[4]),
        pltpu.make_async_copy(dv_all, dv_out, out_sems.at[5]),
    ]
    for copy in keep:
        copy.start()
    context[tail] = jnp.zeros((R, 512), f32)
    acc_o[...] = jnp.zeros_like(acc_o)

    def query_weight(b, carry):
        rows = pl.ds(pl.multiple_of(FRONT + b * R, 8), R)
        dq = context[rows].astype(bf16)
        acc_o[...] += product_left(inputs[rows].astype(bf16), dq)
        small_out[6:7] += jnp.sum(dq.astype(f32), axis=0, keepdims=True)
        first[rows] = first[rows] + (product_right(dq[:, :256], wq[0]) + product_right(dq[:, 256:], wq[1]))
        return carry

    lax.fori_loop(0, blocks, query_weight, 0)
    def chain_out(c):
        return pltpu.make_async_copy(spread.at[c % 4, pl.ds(0, SEQ)], dx_out.at[pl.ds(c * SEQ, SEQ)], dx_sems.at[c % 4])

    def scatter(c, carry):
        slot = c % 4

        @pl.when(c >= 4)
        def _():
            chain_out(c - 4).wait()

        spread[slot, 0 : SEQ + W] = jnp.zeros((SEQ + W, 512), f32)

        def put(j, carry):
            _, pos, _, _, dst, _, live, _ = window(j)
            spread[slot, pl.ds(pl.multiple_of(pos, 16), W)] = jnp.where(live, first[pl.ds(dst, W)], 0.0)
            return carry

        lax.fori_loop(chain_win[c], chain_win[c + 1], put, 0)
        chain_out(c).start()
        return carry

    lax.fori_loop(0, chains, scatter, 0)
    small_out[7:8] = jnp.sum(dv_all[...].astype(f32), axis=0, keepdims=True)
    part = 4 * SEQ if chains % 4 == 0 else rows_all // 2

    def key_value_weight(b, carry):
        rows = pl.ds(pl.multiple_of(b * part, 32), part)
        x = x_all[rows]
        dk = product_left(x, dk_all[rows])
        dv = product_left(x, dv_all[rows])
        keep = jnp.where(b > 0, 1.0, 0.0)
        acc_d[0, 0:512] = acc_d[0, 0:512] * keep + dk
        acc_d[1, 0:512] = acc_d[1, 0:512] * keep + dv
        return carry

    lax.fori_loop(0, rows_all // part, key_value_weight, 0)
    dk, dv = acc_d[0, 0:512], acc_d[1, 0:512]
    for h in range(2):
        cols = slice(256 * h, 256 * h + 256)
        stage[h, 2048:2560, 0:256] = acc_o[:, cols].astype(bf16)
        stage[h, 2048:2560, 256:512] = dk[:, cols].astype(bf16)
        stage[h, 2560:3072, 0:256] = dv[:, cols].astype(bf16)
        out_copy(h, 1).start()

    for slot in range(4):
        chain_out(chains - 4 + slot).wait()
    for copy in keep:
        copy.wait()
    for h in range(2):
        out_copy(h, 0).wait()
        out_copy(h, 1).wait()


def live_rows(lengths, starts, ends, states, cotangent, q, k, v, wqkv, wo, wi, wd, bias, vec):
    rows = states.shape[0]
    chains = rows // SEQ
    R, W = FFN_BLOCK, WINDOW
    C = -(-(FRONT + rows + R + W) // 8) * 8
    windows = 3 * chains + 2
    hbm, vm, sm = (pl.BlockSpec(memory_space=s) for s in (pl.ANY, pltpu.VMEM, pltpu.SMEM))
    S, V, D, M = jax.ShapeDtypeStruct, pltpu.VMEM, pltpu.SemaphoreType.DMA, pltpu.SMEM
    return pl.pallas_call(
        live_kernel,
        in_specs=[sm] * 3 + [hbm] * 9 + [vm, vm],
        out_specs=[hbm] * 4 + [vm],
        scratch_shapes=[
            V((rows + W, 512), bf16), V((rows + W, 512), bf16), V((rows + W, 512), bf16), V((rows, 512), bf16), V((rows, 512), bf16),
            V((2, 512, 256), bf16), V((2, 256, 512), bf16), V((2, 512, 1024), bf16), V((2, 1024, 512), bf16),
            V((C, 512), f32), V((C, 512), f32), V((C, 512), f32), V((C, 512), f32),
            V((rows, 512), bf16), V((SEQ, 512), f32), V((SEQ, 512), f32),
            V((2, 1024, 512), f32), V((4, 512, 512), f32), V((512, 512), f32),
            V((4, R, 512), f32), V((4, R, 512), bf16), V((2, 3072, 512), bf16), V((4 * W, 256), bf16),
            M((windows,), jnp.int32), M((windows,), jnp.int32), M((windows,), jnp.int32), M((chains + 1,), jnp.int32),
            D((5, chains)), D((5,)), D((6,)), D((4,)),
        ],
        out_shape=[S((2, ROWS, 512), bf16), S((rows, 512), bf16), S((rows, 512), bf16), S((rows, 512), f32), S((16, 512), f32)],
        compiler_params=pltpu.CompilerParams(vmem_limit_bytes=62 << 20),
        name="live_rows",
    )(lengths, starts, ends, states, cotangent, q, k, v, wqkv, wo, wi, wd, bias, vec)


def rest_kernel(
    SLOTS, K, STRIDE,
    g, small, x_ref, q_ref, k_ref, v_ref, len_ref, dk_ref, dv_ref, gf_ref, wqkv_hbm, wo_hbm, wi_hbm, wd_hbm, bias_ref, vec_ref,
    out, sout, y_ref, dx_ref, wqkv, wo, wi, wd, w_sems, *bufs,
):
    step = pl.program_id(0)
    comm = Comm(K, g, small, out, sout, bufs, STRIDE)
    slots = SLOTS
    loads = [
        pltpu.make_async_copy(a, b, w_sems.at[i])
        for i, (a, b) in enumerate(((wo_hbm, wo), (wi_hbm, wi), (wd_hbm, wd), (wqkv_hbm, wqkv)))
    ]

    def slot(i):
        if i < slots:
            it = step * slots + i

            @pl.when(it < comm.iterations)
            def _():
                comm.iteration(it)

    @pl.when(step == 0)
    def _():
        for copy in loads:
            copy.start()
        comm.barrier()

    vec = vec_ref[...]
    bo, g1, s1, bd, g2, s2 = (vec[i : i + 1] for i in range(6))
    low_lane = lax.broadcasted_iota(jnp.int32, (SEQ, 128), 1) < HEAD_DIM
    key_row = lax.broadcasted_iota(jnp.int32, (SEQ, SEQ), 0)
    ctx = []
    for c in range(2):
        rows = slice(c * SEQ, c * SEQ + SEQ)
        length = len_ref[comm.t * (2 * pl.num_programs(0)) + 2 * step + c]
        slot(c)
        parts = []
        for half in range(2):
            streams = [(slice(128 * pair, 128 * pair + 128), h) for pair in (2 * half, 2 * half + 1) for h in range(2)]
            keys = [jnp.where(low_lane == (h == 0), k_ref[rows, cols], jnp.zeros((), bf16)) for cols, h in streams]
            scores = [product_right(key, q_ref[rows, cols]) for (cols, _), key in zip(streams, keys)]
            scores = [jnp.where(key_row < length, s, -1e9) for s in scores]
            exps = [jnp.exp(s - jnp.max(s, axis=0, keepdims=True)) for s in scores]
            probs = [(e * inverse(jnp.sum(e, axis=0, keepdims=True))).astype(bf16) for e in exps]
            outs = [product_left(p, v_ref[rows, cols]) for (cols, _), p in zip(streams, probs)]
            parts += [jnp.where(low_lane, outs[0], outs[1]), jnp.where(low_lane, outs[2], outs[3])]
        ctx.append(jnp.concatenate(parts, axis=1).astype(bf16))
    ctx = jnp.concatenate(ctx, axis=0)
    slot(2)

    @pl.when(step == 0)
    def _():
        for copy in loads:
            copy.wait()

    s = x_ref[...].astype(f32) + (product(ctx[:, :256], wo[0]) + product(ctx[:, 256:], wo[1]) + bo)
    center = s - row_mean(s)
    normed = center * lax.rsqrt(row_mean(center * center) + EPSILON) * g1 + s1
    low = normed.astype(bf16)
    branch = bd

    def up_part(j):
        h, o = j // 2, 512 * (j % 2)
        bi = jnp.concatenate([bias_ref[h, 2 + o // 256 : 3 + o // 256], bias_ref[h, 3 + o // 256 : 4 + o // 256]], axis=1)
        return product(low, wi[h, :, o : o + 512]) + bi

    ahead = up_part(0)
    for j in range(4):
        hid, ahead = ahead, up_part(j + 1) if j < 3 else None
        branch = branch + product((hid * normal_cdf(hid)).astype(bf16), wd[j // 2, 512 * (j % 2) : 512 * (j % 2) + 512])
        if j == 1:
            slot(3)
    s = normed + branch
    center = s - row_mean(s)
    y_ref[...] = (center * lax.rsqrt(row_mean(center * center) + EPSILON) * g2 + s2).astype(bf16)
    slot(4)
    dx = gf_ref[...]
    for h in range(2):
        cols = slice(256 * h, 256 * h + 256)
        for j, ref in ((1, dk_ref), (2, dv_ref)):
            dx = dx + product_right(ref[:, cols], wqkv[h, j])
    dx_ref[...] = dx

    @pl.when(step == pl.num_programs(0) - 1)
    def _():
        def body(it, carry):
            comm.iteration(it)
            return carry

        lax.fori_loop(slots * pl.num_programs(0), comm.iterations, body, 0)
        comm.finish()


def rest(g, small, states, q, k, v, lens, dk, dv, gf, wqkv, wo, wi, wd, bias, vec):
    rows = states.shape[0]
    block = 2 * SEQ
    K, STRIDE, SLOTS = 8, 2, 4
    tile = pl.BlockSpec((block, 512), lambda i: (i, 0))
    vm, hbm = pl.BlockSpec(memory_space=pltpu.VMEM), pl.BlockSpec(memory_space=pl.ANY)
    S = jax.ShapeDtypeStruct
    return pl.pallas_call(
        functools.partial(rest_kernel, SLOTS, K, STRIDE),
        grid=(rows // block,),
        in_specs=[hbm, vm, tile, tile, tile, tile, pl.BlockSpec(memory_space=pltpu.SMEM), tile, tile, tile,
                  hbm, hbm, hbm, hbm, vm, vm],
        out_specs=[hbm, vm, tile, tile],
        out_shape=[S((ROWS, 512), bf16), S(small.shape, f32), S((rows, 512), bf16), S((rows, 512), f32)],
        scratch_shapes=[
            pltpu.VMEM(wqkv.shape, bf16), pltpu.VMEM(wo.shape, bf16), pltpu.VMEM(wi.shape, bf16), pltpu.VMEM(wd.shape, bf16),
            pltpu.SemaphoreType.DMA((4,)),
        ] + Comm.scratch(K, small.shape[0]),
        compiler_params=pltpu.CompilerParams(collective_id=0, has_side_effects=True, vmem_limit_bytes=61 << 20),
        name="rest",
    )(g, small, states, q, k, v, lens, dk, dv, gf, wqkv, wo, wi, wd, bias, vec)


def finish_kernel(
    sums_ref, small_ref, y_in, dx_in,
    y_ref, dx_ref, dq_ref, dk_ref, dv_ref, do_ref, di_ref, dd_ref, bq_ref, bv_ref, bo_ref, g1_ref, s1_ref, bi_ref, bd_ref, g2_ref, s2_ref,
    dd, di, dqkvo, sems,
):
    step = pl.program_id(0)
    t = lax.axis_index("tensor")
    y_ref[...] = y_in[...]
    dx_ref[...] = dx_in[...]
    w = [
        (2, pltpu.make_async_copy(dd, dd_ref, sems.at[0])), (4, pltpu.make_async_copy(di, di_ref, sems.at[1])),
        (5, pltpu.make_async_copy(dqkvo.at[0], dq_ref, sems.at[2])), (5, pltpu.make_async_copy(dqkvo.at[1], dk_ref, sems.at[3])),
        (6, pltpu.make_async_copy(dqkvo.at[2], dv_ref, sems.at[4])),
    ]

    def part(rows):
        return sums_ref[rows].astype(f32)

    @pl.when(step == 0)
    def _():
        pick = lambda i: jnp.where(t == 0, small_ref[i : i + 1, 0:256], small_ref[i : i + 1, 256:512])
        bq_ref[...] = pick(6)
        bv_ref[...] = pick(7)
        bi_ref[...] = jnp.where(
            t == 0, jnp.concatenate([small_ref[8:9], small_ref[9:10]], axis=1), jnp.concatenate([small_ref[10:11], small_ref[11:12]], axis=1)
        )
        for i, ref in enumerate((bo_ref, g1_ref, s1_ref, bd_ref, g2_ref, s2_ref)):
            ref[...] = small_ref[i : i + 1]

    @pl.when(step == 1)
    def _():
        dd[...] = part(slice(0, 1024))
        pltpu.make_async_copy(dd, dd_ref, sems.at[0]).start()

    @pl.when(step == 2)
    def _():
        di[:, 0:512] = part(slice(1024, 1536))
        di[:, 512:1024] = part(slice(1536, 2048))
        pltpu.make_async_copy(di, di_ref, sems.at[1]).start()

    @pl.when(step == 3)
    def _():
        both = part(slice(2048, 2560))
        dqkvo[0], dqkvo[1] = both[:, :256], both[:, 256:]
        dqkvo[2] = part(slice(2560, 3072))[:, :256]
        do_ref[:, 0:256] = sums_ref[2560:2816, 256:512].astype(f32)
        do_ref[:, 256:512] = sums_ref[2816:3072, 256:512].astype(f32)
        for i, ref in enumerate((dq_ref, dk_ref, dv_ref)):
            pltpu.make_async_copy(dqkvo.at[i], ref, sems.at[2 + i]).start()

    @pl.when(step == pl.num_programs(0) - 1)
    def _():
        for _, copy in w:
            copy.wait()


def finish(sums, small, y, dx):
    rows = y.shape[0]
    block = 2 * SEQ
    tile = pl.BlockSpec((block, 512), lambda i: (i, 0))
    vm, hbm = pl.BlockSpec(memory_space=pltpu.VMEM), pl.BlockSpec(memory_space=pl.ANY)
    S, V = jax.ShapeDtypeStruct, pltpu.VMEM
    line = lambda n: S((1, n), f32)
    return pl.pallas_call(
        finish_kernel,
        grid=(rows // block,),
        in_specs=[vm, vm, tile, tile],
        out_specs=[tile, tile, hbm, hbm, hbm, vm, hbm, hbm] + [vm] * 9,
        out_shape=[
            S((rows, 512), bf16), S((rows, 512), f32), S((512, 256), f32), S((512, 256), f32), S((512, 256), f32), S((256, 512), f32),
            S((512, 1024), f32), S((1024, 512), f32), line(256), line(256), line(512), line(512), line(512), line(1024), line(512), line(512), line(512),
        ],
        scratch_shapes=[V((1024, 512), f32), V((512, 1024), f32), V((3, 512, 256), f32), pltpu.SemaphoreType.DMA((5,))],
        compiler_params=pltpu.CompilerParams(vmem_limit_bytes=60 << 20),
        name="finish",
    )(sums, small, y, dx)


def whole_chains(
    states, cotangent, lengths, span_starts, span_ends, query_weight, query_bias, key_weight, value_weight, value_bias,
    output_weight, output_bias, first_gain, first_shift, inner_weight, inner_bias, down_weight, down_bias, second_gain, second_shift,
):
    q, k, v, vec, wqkv, wo, wi, wd, bias = gather(
        states, query_weight, key_weight, value_weight, query_bias, value_bias, inner_bias,
        (output_bias, first_gain, first_shift, down_bias, second_gain, second_shift), output_weight, inner_weight, down_weight,
    )
    g, dk, dv, gf, small = live_rows(lengths, span_starts, span_ends, states, cotangent, q, k, v, wqkv, wo, wi, wd, bias, vec)
    summed, small, output, input_grad = rest(g, small, states, q, k, v, lengths, dk, dv, gf, wqkv, wo, wi, wd, bias, vec)
    (
        output, input_grad, query, key, value, out, inner, down, query_b, value_b, out_b, gain1, shift1, inner_b, down_b, gain2, shift2,
    ) = finish(summed, small, output, input_grad)
    flat = lambda a: a.reshape(-1)
    return (
        output, input_grad, query, flat(query_b), key, value, flat(value_b), out, flat(out_b), flat(gain1), flat(shift1),
        inner, flat(inner_b), down, flat(down_b), flat(gain2), flat(shift2),
    )


def local(*arguments):
    rows, hidden = arguments[0].shape[0], arguments[14].shape[1]
    if rows % SEQ == 0 and lax.axis_size("dp") == 16 and lax.axis_size("tensor") == 2:
        return whole_chains(*arguments)
    return general(*arguments)


def solution(mesh):
    placed = (
        P(("dp", "tensor"), None),
        P(("dp", "tensor"), None),
        P("dp"),
        P("dp"),
        P("dp"),
        P(None, "tensor"),
        P("tensor"),
        P(None, "tensor"),
        P(None, "tensor"),
        P("tensor"),
        P("tensor", None),
        P(),
        P(),
        P(),
        P(None, "tensor"),
        P("tensor"),
        P("tensor", None),
        P(),
        P(),
        P(),
    )
    return jax.shard_map(
        local,
        mesh=mesh,
        in_specs=placed,
        out_specs=(
            P(("dp", "tensor"), None),
            P(("dp", "tensor"), None),
            P(None, "tensor"),
            P("tensor"),
            P(None, "tensor"),
            P(None, "tensor"),
            P("tensor"),
            P("tensor", None),
            P(),
            P(),
            P(),
            P(None, "tensor"),
            P("tensor"),
            P("tensor", None),
            P(),
            P(),
            P(),
        ),
        check_vma=False,
    )
```

```python
import functools

import jax
import jax.numpy as jnp
from jax import lax
from jax.experimental import pallas as pl
from jax.experimental.pallas import tpu as pltpu
from jax.sharding import PartitionSpec as P

MESH = pl.DeviceIdType.MESH
f32, bf16 = jnp.float32, jnp.bfloat16
HEAD_DIM = 64
SEQ = 160
ROWS = 3072
SCALE = HEAD_DIM ** (-0.5)
ATT_BLOCK = 32
FFN_BLOCK = 256
EPSILON = 1e-12


def product(left, right):
    return jnp.dot(left, right, preferred_element_type=jnp.float32)


def product_left(left, right):
    return lax.dot_general(
        left, right, (((0,), (0,)), ((), ())), preferred_element_type=jnp.float32
    )


def product_right(left, right):
    return lax.dot_general(
        left, right, (((1,), (1,)), ((), ())), preferred_element_type=jnp.float32
    )


def layer_norm(values, gain, shift):
    center = values - jnp.mean(values, axis=-1, keepdims=True)
    spread = jnp.mean(center * center, axis=-1, keepdims=True)
    return center * lax.rsqrt(spread + EPSILON) * gain + shift


def exact_gelu(values):
    return jax.nn.gelu(values, approximate=False)


def attention_scores(queries, keys, key_live):
    scores = jnp.einsum(
        "cqhd,ckhd->chqk", queries, keys, preferred_element_type=jnp.float32
    ) * HEAD_DIM ** (-0.5)
    return jnp.where(key_live[:, None, None, :], scores, -1000000000.0)


def per_row(table, picker):
    return jnp.sum(jnp.where(picker, table[None, :], 0), axis=1)


def column_sum(values):
    return jnp.sum(values.astype(jnp.float32), axis=0)


def general(
    states,
    cotangent,
    lengths,
    span_starts,
    span_ends,
    query_weight,
    query_bias,
    key_weight,
    value_weight,
    value_bias,
    output_weight,
    output_bias,
    first_gain,
    first_shift,
    inner_weight,
    inner_bias,
    down_weight,
    down_bias,
    second_gain,
    second_shift,
):
    slice_rows = states.shape[0]
    chains = lengths.shape[0]
    group_rows = chains * SEQ
    heads_local = query_weight.shape[1] // HEAD_DIM
    layout = (chains, SEQ, heads_local, HEAD_DIM)
    whole = lax.all_gather(states, "tensor", axis=0, tiled=True)
    queries = (product(whole, query_weight) + query_bias).astype(jnp.bfloat16).reshape(layout)
    keys_low = product(whole, key_weight).astype(jnp.bfloat16).reshape(layout)
    values_low = (product(whole, value_weight) + value_bias).astype(jnp.bfloat16).reshape(layout)
    key_live = jnp.arange(SEQ, dtype=jnp.int32)[None, :] < lengths[:, None]
    scores = attention_scores(queries, keys_low, key_live)
    highest = jnp.max(scores, axis=-1, keepdims=True)
    logsum = highest + jnp.log(jnp.sum(jnp.exp(scores - highest), axis=-1, keepdims=True))
    probs_low = jnp.exp(scores - logsum).astype(jnp.bfloat16)
    context = jnp.einsum(
        "chqk,ckhd->cqhd", probs_low, values_low, preferred_element_type=jnp.float32
    )
    context = context.reshape(group_rows, heads_local * HEAD_DIM).astype(jnp.bfloat16)
    attended = lax.psum_scatter(
        product(context, output_weight), "tensor", scatter_dimension=0, tiled=True
    ) + output_bias.astype(jnp.float32)
    first_sum = states.astype(jnp.float32) + attended
    normed, first_pull = jax.vjp(
        layer_norm, first_sum, first_gain.astype(jnp.float32), first_shift.astype(jnp.float32)
    )
    normed_low = normed.astype(jnp.bfloat16)
    normed_all = lax.all_gather(normed_low, "tensor", axis=0, tiled=True)
    hidden = product(normed_all, inner_weight) + inner_bias.astype(jnp.float32)
    activation, gelu_pull = jax.vjp(exact_gelu, hidden)
    activation_low = activation.astype(jnp.bfloat16)
    branch = lax.psum_scatter(
        product(activation_low, down_weight), "tensor", scatter_dimension=0, tiled=True
    )
    second_sum = normed + (branch + down_bias.astype(jnp.float32))
    output, second_pull = jax.vjp(
        layer_norm, second_sum, second_gain.astype(jnp.float32), second_shift.astype(jnp.float32)
    )
    row_ids = lax.axis_index("tensor") * slice_rows + jnp.arange(slice_rows, dtype=jnp.int32)
    chain_ids = row_ids // SEQ
    position = row_ids % SEQ
    picker = chain_ids[:, None] == jnp.arange(chains, dtype=jnp.int32)[None, :]
    live = (
        (position >= per_row(span_starts, picker))
        & (position < per_row(span_ends, picker))
        & (position < per_row(lengths, picker))
    )
    grad_out = jnp.where(live[:, None], cotangent.astype(jnp.float32), 0.0)
    grad_second, second_gain_part, second_shift_part = second_pull(grad_out)
    grad_branch = grad_second.astype(jnp.bfloat16)
    down_bias_part = column_sum(grad_branch)
    grad_branch_all = lax.all_gather(grad_branch, "tensor", axis=0, tiled=True)
    down_weight_part = product_left(activation_low, grad_branch_all)
    grad_activation = product_right(grad_branch_all, down_weight)
    (grad_hidden,) = gelu_pull(grad_activation)
    grad_hidden_low = grad_hidden.astype(jnp.bfloat16)
    inner_weight_part = product_left(normed_all, grad_hidden_low)
    inner_bias_part = column_sum(grad_hidden_low)
    grad_normed = lax.psum_scatter(
        product_right(grad_hidden_low, inner_weight), "tensor", scatter_dimension=0, tiled=True
    )
    grad_first, first_gain_part, first_shift_part = first_pull(grad_second + grad_normed)
    grad_attended = grad_first.astype(jnp.bfloat16)
    output_bias_part = column_sum(grad_attended)
    grad_attended_all = lax.all_gather(grad_attended, "tensor", axis=0, tiled=True)
    output_weight_part = product_left(context, grad_attended_all)
    grad_context = (
        product_right(grad_attended_all, output_weight).astype(jnp.bfloat16).reshape(layout)
    )
    probs = jnp.exp(attention_scores(queries, keys_low, key_live) - logsum)
    grad_probs = jnp.einsum(
        "cqhd,ckhd->chqk", grad_context, values_low, preferred_element_type=jnp.float32
    )
    grad_scores = probs * (grad_probs - jnp.sum(probs * grad_probs, axis=-1, keepdims=True))
    grad_scores_low = grad_scores.astype(jnp.bfloat16)
    scale = HEAD_DIM ** (-0.5)
    grad_queries = (
        jnp.einsum("chqk,ckhd->cqhd", grad_scores_low, keys_low, preferred_element_type=jnp.float32)
        * scale
    )
    grad_keys = (
        jnp.einsum("chqk,cqhd->ckhd", grad_scores_low, queries, preferred_element_type=jnp.float32)
        * scale
    )
    grad_values = jnp.einsum(
        "chqk,cqhd->ckhd", probs_low, grad_context, preferred_element_type=jnp.float32
    )
    flat = (group_rows, heads_local * HEAD_DIM)
    grad_queries = grad_queries.reshape(flat).astype(jnp.bfloat16)
    grad_keys = grad_keys.reshape(flat).astype(jnp.bfloat16)
    grad_values = grad_values.reshape(flat).astype(jnp.bfloat16)
    query_weight_part = product_left(whole, grad_queries)
    key_weight_part = product_left(whole, grad_keys)
    value_weight_part = product_left(whole, grad_values)
    query_bias_part = column_sum(grad_queries)
    value_bias_part = column_sum(grad_values)
    grad_whole = (
        product_right(grad_queries, query_weight)
        + product_right(grad_keys, key_weight)
        + product_right(grad_values, value_weight)
    )
    input_grad = (
        lax.psum_scatter(
            grad_whole.astype(jnp.bfloat16), "tensor", scatter_dimension=0, tiled=True
        ).astype(jnp.float32)
        + grad_first
    )
    (
        query_weight_grad,
        query_bias_grad,
        key_weight_grad,
        value_weight_grad,
        value_bias_grad,
        output_weight_grad,
        inner_weight_grad,
        inner_bias_grad,
        down_weight_grad,
    ) = (
        lax.psum(query_weight_part.astype(jnp.bfloat16), "dp").astype(jnp.float32),
        lax.psum(query_bias_part.astype(jnp.bfloat16), "dp").astype(jnp.float32),
        lax.psum(key_weight_part.astype(jnp.bfloat16), "dp").astype(jnp.float32),
        lax.psum(value_weight_part.astype(jnp.bfloat16), "dp").astype(jnp.float32),
        lax.psum(value_bias_part.astype(jnp.bfloat16), "dp").astype(jnp.float32),
        lax.psum(output_weight_part.astype(jnp.bfloat16), "dp").astype(jnp.float32),
        lax.psum(inner_weight_part.astype(jnp.bfloat16), "dp").astype(jnp.float32),
        lax.psum(inner_bias_part.astype(jnp.bfloat16), "dp").astype(jnp.float32),
        lax.psum(down_weight_part.astype(jnp.bfloat16), "dp").astype(jnp.float32),
    )
    (
        output_bias_grad,
        first_gain_grad,
        first_shift_grad,
        down_bias_grad,
        second_gain_grad,
        second_shift_grad,
    ) = lax.psum(
        (
            output_bias_part,
            first_gain_part,
            first_shift_part,
            down_bias_part,
            second_gain_part,
            second_shift_part,
        ),
        ("dp", "tensor"),
    )
    return (
        output.astype(jnp.bfloat16),
        input_grad,
        query_weight_grad,
        query_bias_grad,
        key_weight_grad,
        value_weight_grad,
        value_bias_grad,
        output_weight_grad,
        output_bias_grad,
        first_gain_grad,
        first_shift_grad,
        inner_weight_grad,
        inner_bias_grad,
        down_weight_grad,
        down_bias_grad,
        second_gain_grad,
        second_shift_grad,
    )


class Comm:
    NSTAGE = 10
    def __init__(self, K, g, small, out, sout, bufs, stride=1):
        self.stride = stride
        self.K = K; self.CH = ROWS // K; self.SB = self.CH // 3
        self.g, self.small, self.out_hbm, self.sout = g, small, out, sout
        (self.core_buf, self.acc, self.r1, self.r2, self.r3, self.r4, self.out, self.sm, self.csem, self.rsem, self.asem, self.smsem, self.fsem) = bufs
        dp = lax.axis_index("dp"); t = lax.axis_index("tensor")
        self.t = t
        x = lax.rem(dp, 2); y = lax.rem(dp // 2, 2); p = lax.rem(dp // 4, 2); q = dp // 8
        self.bits = (x, y, p, q)
        self.parts = tuple(dp + w * (1 - 2 * b) for w, b in ((1, x), (2, y), (4, p), (8, q)))
        self.dp = dp
    def barrier(self):
        b = pltpu.get_barrier_semaphore()
        pl.semaphore_signal(b, inc=1, device_id=(self.dp, 1 - self.t), device_id_type=MESH)
        for n in self.parts:
            pl.semaphore_signal(b, inc=1, device_id=(n, self.t), device_id_type=MESH)
        pl.semaphore_wait(b, 5)
    def rc(self, src, dst, s, r, n):
        return pltpu.make_async_remote_copy(src_ref=src, dst_ref=dst, send_sem=s, recv_sem=r, device_id=(n, self.t), device_id_type=MESH)
    def core_copy(self, k):
        return pltpu.make_async_remote_copy(src_ref=self.g.at[1 - self.t, pl.ds(k * self.CH, self.CH)], dst_ref=self.core_buf.at[k],
            send_sem=self.csem.at[0, k], recv_sem=self.csem.at[1, k], device_id=(self.dp, 1 - self.t), device_id_type=MESH)
    def own_copy(self, k):
        sl = pl.ds(k * self.CH, self.CH)
        return pltpu.make_async_copy(self.g.at[self.t, sl], self.acc.at[sl], self.csem.at[2, k])
    def order(self, k, r):
        B, N = self.bits, self.parts
        X, Y, Pp, Qq = ((B[i], N[i]) for i in range(4))
        if r == 0: return X, Y, Pp, Qq
        if r == 1: return Y, X, Pp, Qq
        if isinstance(k, int):
            return (Pp, X, Y, Qq) if k % 2 == 0 else (Pp, Y, X, Qq)
        even = lax.rem(k, 2) == 0
        U = (jnp.where(even, B[0], B[1]), jnp.where(even, N[0], N[1]))
        V = (jnp.where(even, B[1], B[0]), jnp.where(even, N[1], N[0]))
        return Pp, U, V, Qq
    def region(self, k, r, depth, keep):
        o = self.order(k, r)
        rows, cols = self.SB, 512
        r0, c0 = k * self.CH + r * self.SB, 0
        for i in range(depth):
            b = o[i][0]
            if i == depth - 1 and not keep: b = 1 - b
            if i < 2:
                rows //= 2; r0 = r0 + b * rows
            else:
                cols //= 2; c0 = c0 + b * cols
        if depth > 2: c0 = pl.multiple_of(c0, 128)
        return pl.ds(pl.multiple_of(r0, 16), rows), pl.ds(c0, cols)
    def rs(self, k, r, i):
        n = self.order(k, r)[i][1]
        buf = (self.r1, self.r2, self.r3, self.r4)[i]
        return self.rc(self.acc.at[self.region(k, r, i + 1, False)], buf.at[k, r], self.rsem.at[0, i, k, r], self.rsem.at[1, i, k, r], n)
    def ag(self, k, r, i):
        n = self.order(k, r)[i][1]
        sl = self.region(k, r, i + 1, True)
        return self.rc(self.out.at[sl], self.out.at[sl], self.asem.at[0, i, k, r], self.asem.at[1, i, k, r], n)
    def small_copy(self, i):
        dev = (self.dp, 1 - self.t) if i == 0 else (self.parts[i - 1], self.t)
        src = self.small if i == 0 else self.sm.at[1, i - 1]
        return pltpu.make_async_remote_copy(src_ref=src, dst_ref=self.sm.at[0, i], send_sem=self.smsem.at[0, i], recv_sem=self.smsem.at[1, i], device_id=dev, device_id_type=MESH)
    def stage(self, s, k):
        if s == 0:
            self.core_copy(k).start()
            self.own_copy(k).start()
        elif s == 1:
            self.core_copy(k).wait_recv()
            sl = pl.ds(pl.multiple_of(k * self.CH, 16), self.CH)
            self.own_copy(k).wait()
            self.acc[sl] = (self.acc[sl].astype(f32) + self.core_buf[k].astype(f32)).astype(bf16)
            for r in range(3): self.rs(k, r, 0).start()
        elif s <= 5:
            i = s - 2
            buf = (self.r1, self.r2, self.r3, self.r4)[i]
            for r in range(3):
                self.rs(k, r, i).wait_recv()
                sl = self.region(k, r, i + 1, True)
                v = (self.acc[sl].astype(f32) + buf[k, r].astype(f32)).astype(bf16)
                if i < 3:
                    self.acc[sl] = v
                    self.rs(k, r, i + 1).start()
                else:
                    self.out[sl] = v
                    self.ag(k, r, 3).start()
        else:
            i = 9 - s
            for r in range(3):
                self.ag(k, r, i).wait_recv()
                if i > 0: self.ag(k, r, i - 1).start()
            if i == 0: self.final_copy(k).start()
    def final_copy(self, k):
        sl = pl.ds(k * self.CH, self.CH)
        return pltpu.make_async_copy(self.out.at[sl], self.out_hbm.at[sl], self.fsem.at[k])
    def small_stage(self, i):
        if i > 0:
            self.small_copy(i - 1).wait_recv()
            own = self.small[...] if i == 1 else self.sm[1, i - 2]
            v = own + self.sm[0, i - 1]
            if i < 5: self.sm[1, i - 1] = v
            else: self.sout[...] = v
        if i < 5: self.small_copy(i).start()
    def iteration_static(self, it):
        if it == 0:
            for k in range(self.K): self.stage(0, k)
        for s in reversed(range(1, self.NSTAGE)):
            k = it - (s - 1) * self.stride
            if 0 <= k < self.K: self.stage(s, k)
        for i in range(6):
            if it == i * self.stride + 1: self.small_stage(i)
    @property
    def iterations(self): return self.K + (self.NSTAGE - 2) * self.stride
    def finish(self):
        def body(k, c):
            self.core_copy(k).wait_send(); self.final_copy(k).wait()
            for r in range(3):
                for i in range(4):
                    self.rs(k, r, i).wait_send(); self.ag(k, r, i).wait_send()
            return c
        lax.fori_loop(0, self.K, body, 0)
        for i in range(5): self.small_copy(i).wait_send()
    @staticmethod
    def scratch(K, S):
        SB = ROWS // K // 3
        D = pltpu.SemaphoreType.DMA
        return [pltpu.VMEM((K, 3 * SB, 512), bf16), pltpu.VMEM((ROWS, 512), bf16),
            pltpu.VMEM((K, 3, SB // 2, 512), bf16), pltpu.VMEM((K, 3, SB // 4, 512), bf16),
            pltpu.VMEM((K, 3, SB // 4, 256), bf16), pltpu.VMEM((K, 3, SB // 4, 128), bf16),
            pltpu.VMEM((ROWS, 512), bf16), pltpu.VMEM((2, 5, S, 512), f32),
            D((3, K)), D((2, 4, K, 3)), D((2, 4, K, 3)), D((2, 5)), D((K,))]


def gather_kernel(
    x_ref, wq_ref, wk_ref, wv_ref, bq_ref, bv_ref, bi_ref, bo_ref, g1_ref, s1_ref, bd_ref, g2_ref, s2_ref, wo_ref, wi_ref, wd_ref,
    q_ref, k_ref, v_ref, vec_ref, wqkv_out, wo_out, wi_out, wd_out, bias_out,
    wqkv, wo, wi, wd, bias, near, sent, came,
):
    step = pl.program_id(0)
    dp, t = lax.axis_index("dp"), lax.axis_index("tensor")

    def pair(i, src, dst):
        return pltpu.make_async_remote_copy(
            src_ref=src, dst_ref=dst, send_sem=sent.at[i], recv_sem=came.at[i],
            device_id=(dp, 1 - t), device_id_type=MESH,
        )

    first = [
        pair(0, wq_ref, wqkv.at[t, 0]), pair(1, wk_ref, wqkv.at[t, 1]), pair(2, wv_ref, wqkv.at[t, 2]),
        pair(3, bias.at[t], bias.at[t]),
    ]
    later = [pair(4, wo.at[t], wo.at[t]), pair(5, wi.at[t], wi.at[t]), pair(6, wd.at[t], wd.at[t])]
    own = [pltpu.make_async_copy(a, b.at[t], near.at[i]) for i, (a, b) in enumerate(((wo_ref, wo), (wi_ref, wi), (wd_ref, wd)))]
    keep = [pltpu.make_async_copy(wqkv, wqkv_out, near.at[3]), pltpu.make_async_copy(bias, bias_out, near.at[4])]
    keep_later = [pltpu.make_async_copy(a, b, near.at[5 + i]) for i, (a, b) in enumerate(((wo, wo_out), (wi, wi_out), (wd, wd_out)))]

    @pl.when(step == 0)
    def _():
        barrier = pltpu.get_barrier_semaphore()
        pl.semaphore_signal(barrier, inc=1, device_id=(dp, 1 - t), device_id_type=MESH)
        bias[t, 0:1] = bq_ref[...].astype(f32).reshape(1, 256)
        bias[t, 1:2] = bv_ref[...].astype(f32).reshape(1, 256)
        for i in range(4):
            bias[t, 2 + i : 3 + i] = bi_ref[pl.ds(256 * i, 256)].astype(f32).reshape(1, 256)
        bias[t, 6:8] = jnp.zeros((2, 256), f32)
        for copy in own:
            copy.start()
        for i, ref in enumerate((bo_ref, g1_ref, s1_ref, bd_ref, g2_ref, s2_ref)):
            vec_ref[i : i + 1] = ref[...].astype(f32).reshape(1, 512)
        vec_ref[6:8] = jnp.zeros((2, 512), f32)
        pl.semaphore_wait(barrier, 1)
        for copy in first:
            copy.start()
        for j, ref in enumerate((wq_ref, wk_ref, wv_ref)):
            wqkv[t, j] = ref[...]
        for copy in first:
            copy.wait_recv()
        for copy in keep:
            copy.start()
        for mine, copy in zip(own, later):
            mine.wait()
            copy.start()

    x = x_ref[...]
    for h in range(2):
        cols = slice(256 * h, 256 * h + 256)
        q_ref[:, cols] = ((product(x, wqkv[h, 0]) + bias[h, 0:1]).astype(bf16).astype(f32) * SCALE).astype(bf16)
        k_ref[:, cols] = product(x, wqkv[h, 1]).astype(bf16)
        v_ref[:, cols] = (product(x, wqkv[h, 2]) + bias[h, 1:2]).astype(bf16)

    @pl.when(step == pl.num_programs(0) // 2)
    def _():
        for copy, out in zip(later, keep_later):
            copy.wait_recv()
            out.start()

    @pl.when(step == pl.num_programs(0) - 1)
    def _():
        for copy in first:
            copy.wait_send()
        for copy in later:
            copy.wait_send()
        for copy in keep + keep_later:
            copy.wait()


def gather(states, wq, wk, wv, bq, bv, bi, vectors, wo, wi, wd):
    rows = states.shape[0]
    block = rows // 4
    whole = lambda a: pl.BlockSpec(a.shape, lambda i: (0,) * a.ndim)
    tile = pl.BlockSpec((block, 512), lambda i: (i, 0))
    hbm, vm = pl.BlockSpec(memory_space=pl.ANY), pl.BlockSpec(memory_space=pltpu.VMEM)
    D = pltpu.SemaphoreType.DMA
    S = jax.ShapeDtypeStruct
    return pl.pallas_call(
        gather_kernel,
        grid=(rows // block,),
        in_specs=[tile, whole(wq), whole(wk), whole(wv)] + [vm] * 9 + [hbm, hbm, hbm],
        out_specs=[tile, tile, tile, vm, hbm, hbm, hbm, hbm, hbm],
        out_shape=[S((rows, 512), bf16)] * 3 + [
            S((8, 512), f32),
            S((2, 3, 512, 256), bf16), S((2, 256, 512), bf16), S((2, 512, 1024), bf16), S((2, 1024, 512), bf16), S((2, 8, 256), f32),
        ],
        scratch_shapes=[
            pltpu.VMEM((2, 3, 512, 256), bf16), pltpu.VMEM((2, 256, 512), bf16), pltpu.VMEM((2, 512, 1024), bf16),
            pltpu.VMEM((2, 1024, 512), bf16), pltpu.VMEM((2, 8, 256), f32), D((8,)), D((7,)), D((7,)),
        ],
        compiler_params=pltpu.CompilerParams(collective_id=1, has_side_effects=True, vmem_limit_bytes=60 << 20),
        name="gather",
    )(states, wq, wk, wv, bq, bv, bi, *vectors, wo, wi, wd)


def normal_cdf(h):
    return 0.5 + 0.5 * lax.erf(h * 0.7071067811865476)


def inverse(a):
    return pltpu.reciprocal(a, approx=True)


def row_mean(a):
    return jnp.sum(a, axis=-1, keepdims=True) * (1.0 / 512)


WINDOW = 32
UNROLL = 4
FRONT = 8


def live_kernel(
    len_ref, start_ref, end_ref,
    x_hbm, cot_hbm, q_hbm, k_hbm, v_hbm, wqkv_hbm, wo_hbm, wi_hbm, wd_hbm, bias_ref, vec_ref,
    g_out, dk_out, dv_out, dx_out, small_out,
    x_all, cot_all, q_all, k_all, v_all, wq, wo, wi, wd, context, inputs, upstream, first, dv_all, acc_k, acc_v,
    acc_d, acc_i, acc_o, gelu_grad, act, stage, apart, win_chain, win_pos, win_dst, chain_win, in_sems, w_sems, out_sems, dx_sems,
):
    chains = len_ref.shape[0] // 2
    t = lax.axis_index("tensor")
    W, R, U = WINDOW, FFN_BLOCK, UNROLL
    rows_all = chains * SEQ
    dk_all = cot_all
    spread = gelu_grad

    def chain_loads(c):
        rows = pl.ds(c * SEQ, SEQ)
        return [
            pltpu.make_async_copy(a.at[rows], b.at[rows], in_sems.at[i, c])
            for i, (a, b) in enumerate(((q_hbm, q_all), (k_hbm, k_all), (v_hbm, v_all), (cot_hbm, cot_all), (x_hbm, x_all)))
        ]

    loads = [
        pltpu.make_async_copy(a, b, w_sems.at[i])
        for i, (a, b) in enumerate((
            (wo_hbm, wo), (wi_hbm, wi), (wd_hbm, wd), (wqkv_hbm.at[0, 0], wq.at[0]), (wqkv_hbm.at[1, 0], wq.at[1]),
        ))
    ]

    def start_loads(c, carry):
        for copy in chain_loads(c):
            copy.start()
        return carry

    lax.fori_loop(0, chains, start_loads, 0)
    for copy in loads:
        copy.start()

    def list_chain(c, carry):
        at, offset = carry
        start = start_ref[t * chains + c]
        end = jnp.minimum(end_ref[t * chains + c], len_ref[t * chains + c])
        r16 = (start // 16) * 16
        r8 = (start // 8) * 8
        count = jnp.maximum((end - r16 + W - 1) // W, 1)
        chain_win[c] = at

        def put(i, carry):
            win_chain[at + i] = c
            win_pos[at + i] = r16 + W * i
            win_dst[at + i] = offset + r16 - r8 + W * i
            return carry

        lax.fori_loop(0, count, put, 0)
        return at + count, offset + jnp.maximum(((end + 7) // 8) * 8 - r8, 0)

    n_win, n_end = lax.fori_loop(0, chains, list_chain, (0, FRONT))
    chain_win[chains] = n_win
    trash = context.shape[0] - W
    for extra in range(U - 1):
        win_chain[n_win + extra] = chains - 1
        win_pos[n_win + extra] = SEQ
        win_dst[n_win + extra] = trash
    n = n_end - FRONT

    acc_d[...] = jnp.zeros_like(acc_d)
    acc_i[...] = jnp.zeros_like(acc_i)
    acc_o[...] = jnp.zeros_like(acc_o)
    acc_k[...] = jnp.zeros_like(acc_k)
    acc_v[...] = jnp.zeros_like(acc_v)
    small_out[...] = jnp.zeros_like(small_out)
    for ref in (context, upstream, first):
        ref[pl.ds(trash, W)] = jnp.zeros((W, 512), f32)
    for ref in (x_all, cot_all, q_all):
        ref[pl.ds(rows_all, W)] = jnp.zeros((W, 512), bf16)

    lane_head = lax.broadcasted_iota(jnp.int32, (W, 256), 1) // HEAD_DIM
    own = lax.broadcasted_iota(jnp.int32, (4 * W, 256), 1) // HEAD_DIM == lax.broadcasted_iota(jnp.int32, (4 * W, 256), 0) // W
    apart[...] = jnp.where(own, 1.0, 0.0).astype(bf16)
    key_row = lax.broadcasted_iota(jnp.int32, (SEQ, 4 * W), 0)
    row_id = lax.broadcasted_iota(jnp.int32, (W, 512), 0)

    def heads_apart(rows):
        return jnp.concatenate([rows] * 4, axis=0) * apart[...]

    def heads_together(full):
        out = full[3 * W :]
        for h in (2, 1, 0):
            out = jnp.where(lane_head == h, full[h * W : (h + 1) * W], out)
        return out

    def window(i):
        c = win_chain[i]
        pos = win_pos[i]
        start = start_ref[t * chains + c]
        length = len_ref[t * chains + c]
        end = jnp.minimum(end_ref[t * chains + c], length)
        src = pl.ds(pl.multiple_of(c * SEQ + pos, 16), W)
        dst = pl.multiple_of(win_dst[i], 8)
        keys = pl.ds(pl.multiple_of(c * SEQ, 32), SEQ)
        live = (row_id + pos >= start) & (row_id + pos < end)
        whole = pos + 8 > start
        return c, pos, length, src, dst, keys, live, whole

    def put_rows(ref, dst, whole, rows):
        head = pl.ds(dst, 8)
        ref[head] = jnp.where(whole, rows[:8], ref[head])
        ref[pl.ds(pl.multiple_of(dst + 8, 8), W - 8)] = rows[8:]

    def softmax(scores, length):
        scores = jnp.where(key_row < length, scores, -1e9)
        e = jnp.exp(scores - jnp.max(scores, axis=0, keepdims=True))
        return e * inverse(jnp.sum(e, axis=0, keepdims=True))

    def forward(i, waited):
        last = win_chain[U * i + U - 1]

        def wait_chain(c, carry):
            for copy in chain_loads(c):
                copy.wait()
            return carry

        lax.fori_loop(waited, last + 1, wait_chain, 0)
        wins = [window(U * i + u) for u in range(U)]
        streams = [(w, slice(256 * g, 256 * g + 256)) for w in wins for g in range(2)]
        qs = [heads_apart(q_all[w[3], cols]) for w, cols in streams]
        scores = [product_right(k_all[w[5], cols], q) for (w, cols), q in zip(streams, qs)]
        probs = [softmax(s, w[2]).astype(bf16) for (w, _), s in zip(streams, scores)]
        outs = [product_left(p, v_all[w[5], cols]) for (w, cols), p in zip(streams, probs)]
        outs = [heads_together(o) for o in outs]
        for u, (c, pos, length, src, dst, keys, live, whole) in enumerate(wins):
            put_rows(context, dst, whole, jnp.concatenate(outs[2 * u : 2 * u + 2], axis=1))
            put_rows(inputs, dst, whole, x_all[src].astype(f32))
            put_rows(upstream, dst, whole, jnp.where(live, cot_all[src].astype(f32), 0.0))
        return last + 1

    steps = (n_win + U - 1) // U
    waited = lax.fori_loop(0, steps, forward, 0)

    tail = pl.ds(pl.multiple_of(n_end, 8), R)
    for ref in (context, inputs, upstream):
        ref[tail] = jnp.zeros((R, 512), f32)
    for copy in loads:
        copy.wait()
    vec = vec_ref[...]
    bo, g1, s1, bd, g2, s2 = (vec[i : i + 1] for i in range(6))
    blocks = (n + R - 1) // R

    def feed_forward(R, start):
        rows = pl.ds(pl.multiple_of(FRONT + start, 8), R)
        ctx = context[rows].astype(bf16)
        attended = product(ctx[:, :256], wo[0]) + product(ctx[:, 256:], wo[1]) + bo
        s = inputs[rows] + attended
        center = s - row_mean(s)
        rstd1 = lax.rsqrt(row_mean(center * center) + EPSILON)
        hat1 = center * rstd1
        normed = hat1 * g1 + s1
        low = normed.astype(bf16)
        branch = jnp.zeros((R, 512), f32) + bd
        place = [(j // 2, 512 * (j % 2)) for j in range(4)]

        def up_part(j):
            h, o = place[j]
            bi = jnp.concatenate([bias_ref[h, 2 + o // 256 : 3 + o // 256], bias_ref[h, 3 + o // 256 : 4 + o // 256]], axis=1)
            return product(low, wi[h, :, o : o + 512]) + bi

        ahead = up_part(0)
        for j in range(4):
            h, o = place[j]
            hid, ahead = ahead, up_part(j + 1) if j < 3 else None
            cdf = normal_cdf(hid)
            a = (hid * cdf).astype(bf16)
            gelu_grad[j, 0:R] = cdf + hid * (0.3989422804014327 * jnp.exp(-0.5 * hid * hid))
            act[j, 0:R] = a
            branch = branch + product(a, wd[h, o : o + 512])
        s = normed + branch
        center = s - row_mean(s)
        rstd2 = lax.rsqrt(row_mean(center * center) + EPSILON)
        hat2 = center * rstd2
        up = upstream[rows]
        gy = up * g2
        grad = rstd2 * (gy - row_mean(gy) - hat2 * row_mean(gy * hat2))
        gb = grad.astype(bf16)
        gn = grad
        back_part = lambda j: product_right(gb, wd[place[j][0], place[j][1] : place[j][1] + 512])
        ahead = back_part(0)
        for j in range(4):
            h, o = place[j]
            ga, ahead = ahead, back_part(j + 1) if j < 3 else None
            acc_d[h, o : o + 512] += product_left(act[j, 0:R], gb)
            gh = (ga * gelu_grad[j, 0:R]).astype(bf16)
            gn = gn + product_right(gh, wi[h, :, o : o + 512])
            acc_i[j] += product_left(low, gh)
            small_out[8 + j : 9 + j] += jnp.sum(gh.astype(f32), axis=0, keepdims=True)
        small_out[1:2] += jnp.sum(gn * hat1, axis=0, keepdims=True)
        small_out[2:3] += jnp.sum(gn, axis=0, keepdims=True)
        small_out[3:4] += jnp.sum(gb.astype(f32), axis=0, keepdims=True)
        small_out[4:5] += jnp.sum(up * hat2, axis=0, keepdims=True)
        small_out[5:6] += jnp.sum(up, axis=0, keepdims=True)
        gy = gn * g1
        grad = rstd1 * (gy - row_mean(gy) - hat1 * row_mean(gy * hat1))
        first[rows] = grad
        ga = grad.astype(bf16)
        small_out[0:1] += jnp.sum(ga.astype(f32), axis=0, keepdims=True)
        acc_o[...] += product_left(ctx, ga)
        upstream[rows] = jnp.concatenate([product_right(ga, wo[0]), product_right(ga, wo[1])], axis=1)

    def whole_block(b, carry):
        feed_forward(R, b * R)
        return carry

    wholes = (n + R // 2 - 1) // R
    lax.fori_loop(0, wholes, whole_block, 0)

    @pl.when(wholes < blocks)
    def _half_block():
        feed_forward(R // 2, wholes * R)

    def out_copy(h, part):
        rows = pl.ds(0, 2048) if part == 0 else pl.ds(2048, 1024)
        return pltpu.make_async_copy(stage.at[h, rows], g_out.at[h, rows], out_sems.at[2 * part + h])

    for h in range(2):
        stage[h, 0:1024] = acc_d[h].astype(bf16)
        stage[h, 1024:1536] = acc_i[2 * h].astype(bf16)
        stage[h, 1536:2048] = acc_i[2 * h + 1].astype(bf16)
        out_copy(h, 0).start()
        stage[h, 2560:2816, 256:512] = acc_o[256 * h : 256 * h + 256, 0:256].astype(bf16)
        stage[h, 2816:3072, 256:512] = acc_o[256 * h : 256 * h + 256, 256:512].astype(bf16)

    def backward(i, carry):
        wins = [window(U * i + u) for u in range(U)]
        streams = [(w, slice(256 * g, 256 * g + 256)) for w in wins for g in range(2)]
        gcs = [jnp.where(w[6], upstream[pl.ds(w[4], W)], 0.0).astype(bf16) for w in wins]
        qs = [heads_apart(q_all[w[3], cols]) for w, cols in streams]
        gs = [heads_apart(gcs[s // 2][:, cols]) for s, (_, cols) in enumerate(streams)]
        scores = [product_right(k_all[w[5], cols], q) for (w, cols), q in zip(streams, qs)]
        gps = [product_right(v_all[w[5], cols], g) for (w, cols), g in zip(streams, gs)]
        probs = [softmax(s, w[2]) for (w, _), s in zip(streams, scores)]
        dss = [(p * (gp - jnp.sum(p * gp, axis=0, keepdims=True))).astype(bf16) for p, gp in zip(probs, gps)]
        dvs = [product(p.astype(bf16), g) for p, g in zip(probs, gs)]
        dks = [product(ds, q) for ds, q in zip(dss, qs)]
        dqs = [product_left(ds, k_all[w[5], cols]) for (w, cols), ds in zip(streams, dss)]
        for u, w in enumerate(wins):
            same = jnp.where((i + u > 0) & (win_chain[jnp.maximum(U * i + u - 1, 0)] == w[0]), 1.0, 0.0)
            dk = acc_k[...] * same + jnp.concatenate(dks[2 * u : 2 * u + 2], axis=1)
            dv = acc_v[...] * same + jnp.concatenate(dvs[2 * u : 2 * u + 2], axis=1)
            acc_k[...] = dk
            acc_v[...] = dv
            dk_all[w[5]] = dk.astype(bf16)
            dv_all[w[5]] = dv.astype(bf16)
        outs = [heads_together(dq) * SCALE for dq in dqs]
        for u, w in enumerate(wins):
            put_rows(context, w[4], w[7], jnp.concatenate(outs[2 * u : 2 * u + 2], axis=1))
        return carry

    lax.fori_loop(0, steps, backward, 0)
    keep = [
        pltpu.make_async_copy(dk_all.at[pl.ds(0, rows_all)], dk_out, out_sems.at[4]),
        pltpu.make_async_copy(dv_all, dv_out, out_sems.at[5]),
    ]
    for copy in keep:
        copy.start()
    context[tail] = jnp.zeros((R, 512), f32)
    acc_o[...] = jnp.zeros_like(acc_o)

    def query_weight(b, carry):
        rows = pl.ds(pl.multiple_of(FRONT + b * R, 8), R)
        dq = context[rows].astype(bf16)
        acc_o[...] += product_left(inputs[rows].astype(bf16), dq)
        small_out[6:7] += jnp.sum(dq.astype(f32), axis=0, keepdims=True)
        first[rows] = first[rows] + (product_right(dq[:, :256], wq[0]) + product_right(dq[:, 256:], wq[1]))
        return carry

    lax.fori_loop(0, blocks, query_weight, 0)
    def chain_out(c):
        return pltpu.make_async_copy(spread.at[c % 4, pl.ds(0, SEQ)], dx_out.at[pl.ds(c * SEQ, SEQ)], dx_sems.at[c % 4])

    def scatter(c, carry):
        slot = c % 4

        @pl.when(c >= 4)
        def _():
            chain_out(c - 4).wait()

        spread[slot, 0 : SEQ + W] = jnp.zeros((SEQ + W, 512), f32)

        def put(j, carry):
            _, pos, _, _, dst, _, live, _ = window(j)
            spread[slot, pl.ds(pl.multiple_of(pos, 16), W)] = jnp.where(live, first[pl.ds(dst, W)], 0.0)
            return carry

        lax.fori_loop(chain_win[c], chain_win[c + 1], put, 0)
        chain_out(c).start()
        return carry

    lax.fori_loop(0, chains, scatter, 0)
    small_out[7:8] = jnp.sum(dv_all[...].astype(f32), axis=0, keepdims=True)
    part = 4 * SEQ if chains % 4 == 0 else rows_all // 2

    def key_value_weight(b, carry):
        rows = pl.ds(pl.multiple_of(b * part, 32), part)
        x = x_all[rows]
        dk = product_left(x, dk_all[rows])
        dv = product_left(x, dv_all[rows])
        keep = jnp.where(b > 0, 1.0, 0.0)
        acc_d[0, 0:512] = acc_d[0, 0:512] * keep + dk
        acc_d[1, 0:512] = acc_d[1, 0:512] * keep + dv
        return carry

    lax.fori_loop(0, rows_all // part, key_value_weight, 0)
    dk, dv = acc_d[0, 0:512], acc_d[1, 0:512]
    for h in range(2):
        cols = slice(256 * h, 256 * h + 256)
        stage[h, 2048:2560, 0:256] = acc_o[:, cols].astype(bf16)
        stage[h, 2048:2560, 256:512] = dk[:, cols].astype(bf16)
        stage[h, 2560:3072, 0:256] = dv[:, cols].astype(bf16)
        out_copy(h, 1).start()

    for slot in range(4):
        chain_out(chains - 4 + slot).wait()
    for copy in keep:
        copy.wait()
    for h in range(2):
        out_copy(h, 0).wait()
        out_copy(h, 1).wait()


def live_rows(lengths, starts, ends, states, cotangent, q, k, v, wqkv, wo, wi, wd, bias, vec):
    rows = states.shape[0]
    chains = rows // SEQ
    R, W = FFN_BLOCK, WINDOW
    C = -(-(FRONT + rows + R + W) // 8) * 8
    windows = SEQ // WINDOW * chains + UNROLL
    hbm, vm, sm = (pl.BlockSpec(memory_space=s) for s in (pl.ANY, pltpu.VMEM, pltpu.SMEM))
    S, V, D, M = jax.ShapeDtypeStruct, pltpu.VMEM, pltpu.SemaphoreType.DMA, pltpu.SMEM
    return pl.pallas_call(
        live_kernel,
        in_specs=[sm] * 3 + [hbm] * 9 + [vm, vm],
        out_specs=[hbm] * 4 + [vm],
        scratch_shapes=[
            V((rows + W, 512), bf16), V((rows + W, 512), bf16), V((rows + W, 512), bf16), V((rows, 512), bf16), V((rows, 512), bf16),
            V((2, 512, 256), bf16), V((2, 256, 512), bf16), V((2, 512, 1024), bf16), V((2, 1024, 512), bf16),
            V((C, 512), f32), V((C, 512), f32), V((C, 512), f32), V((C, 512), f32),
            V((rows, 512), bf16), V((SEQ, 512), f32), V((SEQ, 512), f32),
            V((2, 1024, 512), f32), V((4, 512, 512), f32), V((512, 512), f32),
            V((4, R, 512), f32), V((4, R, 512), bf16), V((2, 3072, 512), bf16), V((4 * W, 256), bf16),
            M((windows,), jnp.int32), M((windows,), jnp.int32), M((windows,), jnp.int32), M((chains + 1,), jnp.int32),
            D((5, chains)), D((5,)), D((6,)), D((4,)),
        ],
        out_shape=[S((2, ROWS, 512), bf16), S((rows, 512), bf16), S((rows, 512), bf16), S((rows, 512), f32), S((16, 512), f32)],
        compiler_params=pltpu.CompilerParams(vmem_limit_bytes=62 << 20),
        name="live_rows",
    )(lengths, starts, ends, states, cotangent, q, k, v, wqkv, wo, wi, wd, bias, vec)


def rest_kernel(
    STEPS, SLOTS, K, STRIDE,
    g, small, x_ref, q_ref, k_ref, v_ref, len_ref, dk_ref, dv_ref, gf_ref, wqkv_hbm, wo_hbm, wi_hbm, wd_hbm, bias_ref, vec_ref,
    out, sout, y_ref, dx_ref, wqkv, wo, wi, wd, w_sems, *bufs,
):
    step = pl.program_id(0)
    comm = Comm(K, g, small, out, sout, bufs, STRIDE)
    slots = SLOTS
    loads = [
        pltpu.make_async_copy(a, b, w_sems.at[i])
        for i, (a, b) in enumerate(((wo_hbm, wo), (wi_hbm, wi), (wd_hbm, wd), (wqkv_hbm, wqkv)))
    ]

    spots = [(at, i) for at in range(STEPS) for i in range(slots)]

    def slot(i):
        for at in range(STEPS):
            mine = [it for it in range(comm.iterations) if spots[it * len(spots) // comm.iterations] == (at, i)]
            if mine:

                @pl.when(step == at)
                def _(mine=mine):
                    for it in mine:
                        comm.iteration_static(it)

    @pl.when(step == 0)
    def _():
        for copy in loads:
            copy.start()
        comm.barrier()

    vec = vec_ref[...]
    bo, g1, s1, bd, g2, s2 = (vec[i : i + 1] for i in range(6))
    low_lane = lax.broadcasted_iota(jnp.int32, (SEQ, 128), 1) < HEAD_DIM
    key_row = lax.broadcasted_iota(jnp.int32, (SEQ, SEQ), 0)
    ctx = []
    for c in range(2):
        rows = slice(c * SEQ, c * SEQ + SEQ)
        length = len_ref[comm.t * (2 * pl.num_programs(0)) + 2 * step + c]
        slot(c)
        parts = []
        for half in range(2):
            streams = [(slice(128 * pair, 128 * pair + 128), h) for pair in (2 * half, 2 * half + 1) for h in range(2)]
            keys = [jnp.where(low_lane == (h == 0), k_ref[rows, cols], jnp.zeros((), bf16)) for cols, h in streams]
            scores = [product_right(key, q_ref[rows, cols]) for (cols, _), key in zip(streams, keys)]
            scores = [jnp.where(key_row < length, s, -1e9) for s in scores]
            exps = [jnp.exp(s - jnp.max(s, axis=0, keepdims=True)) for s in scores]
            probs = [(e * inverse(jnp.sum(e, axis=0, keepdims=True))).astype(bf16) for e in exps]
            outs = [product_left(p, v_ref[rows, cols]) for (cols, _), p in zip(streams, probs)]
            parts += [jnp.where(low_lane, outs[0], outs[1]), jnp.where(low_lane, outs[2], outs[3])]
        ctx.append(jnp.concatenate(parts, axis=1).astype(bf16))
    ctx = jnp.concatenate(ctx, axis=0)
    slot(2)

    @pl.when(step == 0)
    def _():
        for copy in loads:
            copy.wait()

    s = x_ref[...].astype(f32) + (product(ctx[:, :256], wo[0]) + product(ctx[:, 256:], wo[1]) + bo)
    center = s - row_mean(s)
    normed = center * lax.rsqrt(row_mean(center * center) + EPSILON) * g1 + s1
    low = normed.astype(bf16)
    branch = bd

    def up_part(j):
        h, o = j // 2, 512 * (j % 2)
        bi = jnp.concatenate([bias_ref[h, 2 + o // 256 : 3 + o // 256], bias_ref[h, 3 + o // 256 : 4 + o // 256]], axis=1)
        return product(low, wi[h, :, o : o + 512]) + bi

    ahead = up_part(0)
    for j in range(4):
        hid, ahead = ahead, up_part(j + 1) if j < 3 else None
        branch = branch + product((hid * normal_cdf(hid)).astype(bf16), wd[j // 2, 512 * (j % 2) : 512 * (j % 2) + 512])
        if j == 1:
            slot(3)
    s = normed + branch
    center = s - row_mean(s)
    y_ref[...] = (center * lax.rsqrt(row_mean(center * center) + EPSILON) * g2 + s2).astype(bf16)
    slot(4)
    dx = gf_ref[...]
    for h in range(2):
        cols = slice(256 * h, 256 * h + 256)
        for j, ref in ((1, dk_ref), (2, dv_ref)):
            dx = dx + product_right(ref[:, cols], wqkv[h, j])
    dx_ref[...] = dx

    @pl.when(step == pl.num_programs(0) - 1)
    def _():
        comm.finish()


def rest(g, small, states, q, k, v, lens, dk, dv, gf, wqkv, wo, wi, wd, bias, vec):
    rows = states.shape[0]
    block = 2 * SEQ
    K, STRIDE, SLOTS = 8, 2, 4
    tile = pl.BlockSpec((block, 512), lambda i: (i, 0))
    vm, hbm = pl.BlockSpec(memory_space=pltpu.VMEM), pl.BlockSpec(memory_space=pl.ANY)
    S = jax.ShapeDtypeStruct
    return pl.pallas_call(
        functools.partial(rest_kernel, rows // block, SLOTS, K, STRIDE),
        grid=(rows // block,),
        in_specs=[hbm, vm, tile, tile, tile, tile, pl.BlockSpec(memory_space=pltpu.SMEM), tile, tile, tile,
                  hbm, hbm, hbm, hbm, vm, vm],
        out_specs=[hbm, vm, tile, tile],
        out_shape=[S((ROWS, 512), bf16), S(small.shape, f32), S((rows, 512), bf16), S((rows, 512), f32)],
        scratch_shapes=[
            pltpu.VMEM(wqkv.shape, bf16), pltpu.VMEM(wo.shape, bf16), pltpu.VMEM(wi.shape, bf16), pltpu.VMEM(wd.shape, bf16),
            pltpu.SemaphoreType.DMA((4,)),
        ] + Comm.scratch(K, small.shape[0]),
        compiler_params=pltpu.CompilerParams(collective_id=0, has_side_effects=True, vmem_limit_bytes=61 << 20),
        name="rest",
    )(g, small, states, q, k, v, lens, dk, dv, gf, wqkv, wo, wi, wd, bias, vec)


def finish_kernel(
    sums_ref, small_ref, y_in, dx_in,
    y_ref, dx_ref, dq_ref, dk_ref, dv_ref, do_ref, di_ref, dd_ref, bq_ref, bv_ref, bo_ref, g1_ref, s1_ref, bi_ref, bd_ref, g2_ref, s2_ref,
    dd, di, dqkvo, sems,
):
    step = pl.program_id(0)
    t = lax.axis_index("tensor")
    y_ref[...] = y_in[...]
    dx_ref[...] = dx_in[...]
    w = [
        (2, pltpu.make_async_copy(dd, dd_ref, sems.at[0])), (4, pltpu.make_async_copy(di, di_ref, sems.at[1])),
        (5, pltpu.make_async_copy(dqkvo.at[0], dq_ref, sems.at[2])), (5, pltpu.make_async_copy(dqkvo.at[1], dk_ref, sems.at[3])),
        (6, pltpu.make_async_copy(dqkvo.at[2], dv_ref, sems.at[4])),
    ]

    def part(rows):
        return sums_ref[rows].astype(f32)

    @pl.when(step == 0)
    def _():
        pick = lambda i: jnp.where(t == 0, small_ref[i : i + 1, 0:256], small_ref[i : i + 1, 256:512])
        bq_ref[...] = pick(6)
        bv_ref[...] = pick(7)
        bi_ref[...] = jnp.where(
            t == 0, jnp.concatenate([small_ref[8:9], small_ref[9:10]], axis=1), jnp.concatenate([small_ref[10:11], small_ref[11:12]], axis=1)
        )
        for i, ref in enumerate((bo_ref, g1_ref, s1_ref, bd_ref, g2_ref, s2_ref)):
            ref[...] = small_ref[i : i + 1]

    @pl.when(step == 1)
    def _():
        dd[...] = part(slice(0, 1024))
        pltpu.make_async_copy(dd, dd_ref, sems.at[0]).start()

    @pl.when(step == 2)
    def _():
        di[:, 0:512] = part(slice(1024, 1536))
        di[:, 512:1024] = part(slice(1536, 2048))
        pltpu.make_async_copy(di, di_ref, sems.at[1]).start()

    @pl.when(step == 3)
    def _():
        both = part(slice(2048, 2560))
        dqkvo[0], dqkvo[1] = both[:, :256], both[:, 256:]
        dqkvo[2] = part(slice(2560, 3072))[:, :256]
        do_ref[:, 0:256] = sums_ref[2560:2816, 256:512].astype(f32)
        do_ref[:, 256:512] = sums_ref[2816:3072, 256:512].astype(f32)
        for i, ref in enumerate((dq_ref, dk_ref, dv_ref)):
            pltpu.make_async_copy(dqkvo.at[i], ref, sems.at[2 + i]).start()

    @pl.when(step == pl.num_programs(0) - 1)
    def _():
        for _, copy in w:
            copy.wait()


def finish(sums, small, y, dx):
    rows = y.shape[0]
    block = 2 * SEQ
    tile = pl.BlockSpec((block, 512), lambda i: (i, 0))
    vm, hbm = pl.BlockSpec(memory_space=pltpu.VMEM), pl.BlockSpec(memory_space=pl.ANY)
    S, V = jax.ShapeDtypeStruct, pltpu.VMEM
    line = lambda n: S((1, n), f32)
    return pl.pallas_call(
        finish_kernel,
        grid=(rows // block,),
        in_specs=[vm, vm, tile, tile],
        out_specs=[tile, tile, hbm, hbm, hbm, vm, hbm, hbm] + [vm] * 9,
        out_shape=[
            S((rows, 512), bf16), S((rows, 512), f32), S((512, 256), f32), S((512, 256), f32), S((512, 256), f32), S((256, 512), f32),
            S((512, 1024), f32), S((1024, 512), f32), line(256), line(256), line(512), line(512), line(512), line(1024), line(512), line(512), line(512),
        ],
        scratch_shapes=[V((1024, 512), f32), V((512, 1024), f32), V((3, 512, 256), f32), pltpu.SemaphoreType.DMA((5,))],
        compiler_params=pltpu.CompilerParams(vmem_limit_bytes=60 << 20),
        name="finish",
    )(sums, small, y, dx)


def whole_chains(
    states, cotangent, lengths, span_starts, span_ends, query_weight, query_bias, key_weight, value_weight, value_bias,
    output_weight, output_bias, first_gain, first_shift, inner_weight, inner_bias, down_weight, down_bias, second_gain, second_shift,
):
    q, k, v, vec, wqkv, wo, wi, wd, bias = gather(
        states, query_weight, key_weight, value_weight, query_bias, value_bias, inner_bias,
        (output_bias, first_gain, first_shift, down_bias, second_gain, second_shift), output_weight, inner_weight, down_weight,
    )
    g, dk, dv, gf, small = live_rows(lengths, span_starts, span_ends, states, cotangent, q, k, v, wqkv, wo, wi, wd, bias, vec)
    summed, small, output, input_grad = rest(g, small, states, q, k, v, lengths, dk, dv, gf, wqkv, wo, wi, wd, bias, vec)
    (
        output, input_grad, query, key, value, out, inner, down, query_b, value_b, out_b, gain1, shift1, inner_b, down_b, gain2, shift2,
    ) = finish(summed, small, output, input_grad)
    flat = lambda a: a.reshape(-1)
    return (
        output, input_grad, query, flat(query_b), key, value, flat(value_b), out, flat(out_b), flat(gain1), flat(shift1),
        inner, flat(inner_b), down, flat(down_b), flat(gain2), flat(shift2),
    )


def local(*arguments):
    rows, hidden = arguments[0].shape[0], arguments[14].shape[1]
    if rows % SEQ == 0 and lax.axis_size("dp") == 16 and lax.axis_size("tensor") == 2:
        return whole_chains(*arguments)
    return general(*arguments)


def solution(mesh):
    placed = (
        P(("dp", "tensor"), None),
        P(("dp", "tensor"), None),
        P("dp"),
        P("dp"),
        P("dp"),
        P(None, "tensor"),
        P("tensor"),
        P(None, "tensor"),
        P(None, "tensor"),
        P("tensor"),
        P("tensor", None),
        P(),
        P(),
        P(),
        P(None, "tensor"),
        P("tensor"),
        P("tensor", None),
        P(),
        P(),
        P(),
    )
    return jax.shard_map(
        local,
        mesh=mesh,
        in_specs=placed,
        out_specs=(
            P(("dp", "tensor"), None),
            P(("dp", "tensor"), None),
            P(None, "tensor"),
            P("tensor"),
            P(None, "tensor"),
            P(None, "tensor"),
            P("tensor"),
            P("tensor", None),
            P(),
            P(),
            P(),
            P(None, "tensor"),
            P("tensor"),
            P("tensor", None),
            P(),
            P(),
            P(),
        ),
        check_vma=False,
    )
```

```python
import functools

import jax
import jax.numpy as jnp
from jax import lax
from jax.experimental import pallas as pl
from jax.experimental.pallas import tpu as pltpu
from jax.sharding import PartitionSpec as P

MESH = pl.DeviceIdType.MESH
f32, bf16 = jnp.float32, jnp.bfloat16
HEAD_DIM = 64
SEQ = 160
ROWS = 3072
SCALE = HEAD_DIM ** (-0.5)
ATT_BLOCK = 32
FFN_BLOCK = 256
EPSILON = 1e-12


def product(left, right):
    return jnp.dot(left, right, preferred_element_type=jnp.float32)


def product_left(left, right):
    return lax.dot_general(
        left, right, (((0,), (0,)), ((), ())), preferred_element_type=jnp.float32
    )


def product_right(left, right):
    return lax.dot_general(
        left, right, (((1,), (1,)), ((), ())), preferred_element_type=jnp.float32
    )


def layer_norm(values, gain, shift):
    center = values - jnp.mean(values, axis=-1, keepdims=True)
    spread = jnp.mean(center * center, axis=-1, keepdims=True)
    return center * lax.rsqrt(spread + EPSILON) * gain + shift


def exact_gelu(values):
    return jax.nn.gelu(values, approximate=False)


def attention_scores(queries, keys, key_live):
    scores = jnp.einsum(
        "cqhd,ckhd->chqk", queries, keys, preferred_element_type=jnp.float32
    ) * HEAD_DIM ** (-0.5)
    return jnp.where(key_live[:, None, None, :], scores, -1000000000.0)


def per_row(table, picker):
    return jnp.sum(jnp.where(picker, table[None, :], 0), axis=1)


def column_sum(values):
    return jnp.sum(values.astype(jnp.float32), axis=0)


def general(
    states,
    cotangent,
    lengths,
    span_starts,
    span_ends,
    query_weight,
    query_bias,
    key_weight,
    value_weight,
    value_bias,
    output_weight,
    output_bias,
    first_gain,
    first_shift,
    inner_weight,
    inner_bias,
    down_weight,
    down_bias,
    second_gain,
    second_shift,
):
    slice_rows = states.shape[0]
    chains = lengths.shape[0]
    group_rows = chains * SEQ
    heads_local = query_weight.shape[1] // HEAD_DIM
    layout = (chains, SEQ, heads_local, HEAD_DIM)
    whole = lax.all_gather(states, "tensor", axis=0, tiled=True)
    queries = (product(whole, query_weight) + query_bias).astype(jnp.bfloat16).reshape(layout)
    keys_low = product(whole, key_weight).astype(jnp.bfloat16).reshape(layout)
    values_low = (product(whole, value_weight) + value_bias).astype(jnp.bfloat16).reshape(layout)
    key_live = jnp.arange(SEQ, dtype=jnp.int32)[None, :] < lengths[:, None]
    scores = attention_scores(queries, keys_low, key_live)
    highest = jnp.max(scores, axis=-1, keepdims=True)
    logsum = highest + jnp.log(jnp.sum(jnp.exp(scores - highest), axis=-1, keepdims=True))
    probs_low = jnp.exp(scores - logsum).astype(jnp.bfloat16)
    context = jnp.einsum(
        "chqk,ckhd->cqhd", probs_low, values_low, preferred_element_type=jnp.float32
    )
    context = context.reshape(group_rows, heads_local * HEAD_DIM).astype(jnp.bfloat16)
    attended = lax.psum_scatter(
        product(context, output_weight), "tensor", scatter_dimension=0, tiled=True
    ) + output_bias.astype(jnp.float32)
    first_sum = states.astype(jnp.float32) + attended
    normed, first_pull = jax.vjp(
        layer_norm, first_sum, first_gain.astype(jnp.float32), first_shift.astype(jnp.float32)
    )
    normed_low = normed.astype(jnp.bfloat16)
    normed_all = lax.all_gather(normed_low, "tensor", axis=0, tiled=True)
    hidden = product(normed_all, inner_weight) + inner_bias.astype(jnp.float32)
    activation, gelu_pull = jax.vjp(exact_gelu, hidden)
    activation_low = activation.astype(jnp.bfloat16)
    branch = lax.psum_scatter(
        product(activation_low, down_weight), "tensor", scatter_dimension=0, tiled=True
    )
    second_sum = normed + (branch + down_bias.astype(jnp.float32))
    output, second_pull = jax.vjp(
        layer_norm, second_sum, second_gain.astype(jnp.float32), second_shift.astype(jnp.float32)
    )
    row_ids = lax.axis_index("tensor") * slice_rows + jnp.arange(slice_rows, dtype=jnp.int32)
    chain_ids = row_ids // SEQ
    position = row_ids % SEQ
    picker = chain_ids[:, None] == jnp.arange(chains, dtype=jnp.int32)[None, :]
    live = (
        (position >= per_row(span_starts, picker))
        & (position < per_row(span_ends, picker))
        & (position < per_row(lengths, picker))
    )
    grad_out = jnp.where(live[:, None], cotangent.astype(jnp.float32), 0.0)
    grad_second, second_gain_part, second_shift_part = second_pull(grad_out)
    grad_branch = grad_second.astype(jnp.bfloat16)
    down_bias_part = column_sum(grad_branch)
    grad_branch_all = lax.all_gather(grad_branch, "tensor", axis=0, tiled=True)
    down_weight_part = product_left(activation_low, grad_branch_all)
    grad_activation = product_right(grad_branch_all, down_weight)
    (grad_hidden,) = gelu_pull(grad_activation)
    grad_hidden_low = grad_hidden.astype(jnp.bfloat16)
    inner_weight_part = product_left(normed_all, grad_hidden_low)
    inner_bias_part = column_sum(grad_hidden_low)
    grad_normed = lax.psum_scatter(
        product_right(grad_hidden_low, inner_weight), "tensor", scatter_dimension=0, tiled=True
    )
    grad_first, first_gain_part, first_shift_part = first_pull(grad_second + grad_normed)
    grad_attended = grad_first.astype(jnp.bfloat16)
    output_bias_part = column_sum(grad_attended)
    grad_attended_all = lax.all_gather(grad_attended, "tensor", axis=0, tiled=True)
    output_weight_part = product_left(context, grad_attended_all)
    grad_context = (
        product_right(grad_attended_all, output_weight).astype(jnp.bfloat16).reshape(layout)
    )
    probs = jnp.exp(attention_scores(queries, keys_low, key_live) - logsum)
    grad_probs = jnp.einsum(
        "cqhd,ckhd->chqk", grad_context, values_low, preferred_element_type=jnp.float32
    )
    grad_scores = probs * (grad_probs - jnp.sum(probs * grad_probs, axis=-1, keepdims=True))
    grad_scores_low = grad_scores.astype(jnp.bfloat16)
    scale = HEAD_DIM ** (-0.5)
    grad_queries = (
        jnp.einsum("chqk,ckhd->cqhd", grad_scores_low, keys_low, preferred_element_type=jnp.float32)
        * scale
    )
    grad_keys = (
        jnp.einsum("chqk,cqhd->ckhd", grad_scores_low, queries, preferred_element_type=jnp.float32)
        * scale
    )
    grad_values = jnp.einsum(
        "chqk,cqhd->ckhd", probs_low, grad_context, preferred_element_type=jnp.float32
    )
    flat = (group_rows, heads_local * HEAD_DIM)
    grad_queries = grad_queries.reshape(flat).astype(jnp.bfloat16)
    grad_keys = grad_keys.reshape(flat).astype(jnp.bfloat16)
    grad_values = grad_values.reshape(flat).astype(jnp.bfloat16)
    query_weight_part = product_left(whole, grad_queries)
    key_weight_part = product_left(whole, grad_keys)
    value_weight_part = product_left(whole, grad_values)
    query_bias_part = column_sum(grad_queries)
    value_bias_part = column_sum(grad_values)
    grad_whole = (
        product_right(grad_queries, query_weight)
        + product_right(grad_keys, key_weight)
        + product_right(grad_values, value_weight)
    )
    input_grad = (
        lax.psum_scatter(
            grad_whole.astype(jnp.bfloat16), "tensor", scatter_dimension=0, tiled=True
        ).astype(jnp.float32)
        + grad_first
    )
    (
        query_weight_grad,
        query_bias_grad,
        key_weight_grad,
        value_weight_grad,
        value_bias_grad,
        output_weight_grad,
        inner_weight_grad,
        inner_bias_grad,
        down_weight_grad,
    ) = (
        lax.psum(query_weight_part.astype(jnp.bfloat16), "dp").astype(jnp.float32),
        lax.psum(query_bias_part.astype(jnp.bfloat16), "dp").astype(jnp.float32),
        lax.psum(key_weight_part.astype(jnp.bfloat16), "dp").astype(jnp.float32),
        lax.psum(value_weight_part.astype(jnp.bfloat16), "dp").astype(jnp.float32),
        lax.psum(value_bias_part.astype(jnp.bfloat16), "dp").astype(jnp.float32),
        lax.psum(output_weight_part.astype(jnp.bfloat16), "dp").astype(jnp.float32),
        lax.psum(inner_weight_part.astype(jnp.bfloat16), "dp").astype(jnp.float32),
        lax.psum(inner_bias_part.astype(jnp.bfloat16), "dp").astype(jnp.float32),
        lax.psum(down_weight_part.astype(jnp.bfloat16), "dp").astype(jnp.float32),
    )
    (
        output_bias_grad,
        first_gain_grad,
        first_shift_grad,
        down_bias_grad,
        second_gain_grad,
        second_shift_grad,
    ) = lax.psum(
        (
            output_bias_part,
            first_gain_part,
            first_shift_part,
            down_bias_part,
            second_gain_part,
            second_shift_part,
        ),
        ("dp", "tensor"),
    )
    return (
        output.astype(jnp.bfloat16),
        input_grad,
        query_weight_grad,
        query_bias_grad,
        key_weight_grad,
        value_weight_grad,
        value_bias_grad,
        output_weight_grad,
        output_bias_grad,
        first_gain_grad,
        first_shift_grad,
        inner_weight_grad,
        inner_bias_grad,
        down_weight_grad,
        down_bias_grad,
        second_gain_grad,
        second_shift_grad,
    )


class Comm:
    NSTAGE = 10
    def __init__(self, K, g, small, out, sout, bufs, stride=1):
        self.stride = stride
        self.K = K; self.CH = ROWS // K; self.SB = self.CH // 3
        self.g, self.small, self.out_hbm, self.sout = g, small, out, sout
        (self.core_buf, self.acc, self.r1, self.r2, self.r3, self.r4, self.out, self.sm, self.csem, self.rsem, self.asem, self.smsem, self.fsem) = bufs
        dp = lax.axis_index("dp"); t = lax.axis_index("tensor")
        self.t = t
        x = lax.rem(dp, 2); y = lax.rem(dp // 2, 2); p = lax.rem(dp // 4, 2); q = dp // 8
        self.bits = (x, y, p, q)
        self.parts = tuple(dp + w * (1 - 2 * b) for w, b in ((1, x), (2, y), (4, p), (8, q)))
        self.dp = dp
    def barrier(self):
        b = pltpu.get_barrier_semaphore()
        pl.semaphore_signal(b, inc=1, device_id=(self.dp, 1 - self.t), device_id_type=MESH)
        for n in self.parts:
            pl.semaphore_signal(b, inc=1, device_id=(n, self.t), device_id_type=MESH)
        pl.semaphore_wait(b, 5)
    def rc(self, src, dst, s, r, n):
        return pltpu.make_async_remote_copy(src_ref=src, dst_ref=dst, send_sem=s, recv_sem=r, device_id=(n, self.t), device_id_type=MESH)
    def core_copy(self, k):
        return pltpu.make_async_remote_copy(src_ref=self.g.at[1 - self.t, pl.ds(k * self.CH, self.CH)], dst_ref=self.core_buf.at[k],
            send_sem=self.csem.at[0, k], recv_sem=self.csem.at[1, k], device_id=(self.dp, 1 - self.t), device_id_type=MESH)
    def own_copy(self, k):
        sl = pl.ds(k * self.CH, self.CH)
        return pltpu.make_async_copy(self.g.at[self.t, sl], self.acc.at[sl], self.csem.at[2, k])
    def order(self, k, r):
        B, N = self.bits, self.parts
        X, Y, Pp, Qq = ((B[i], N[i]) for i in range(4))
        if r == 0: return X, Y, Pp, Qq
        if r == 1: return Y, X, Pp, Qq
        if isinstance(k, int):
            return (Pp, X, Y, Qq) if k % 2 == 0 else (Pp, Y, X, Qq)
        even = lax.rem(k, 2) == 0
        U = (jnp.where(even, B[0], B[1]), jnp.where(even, N[0], N[1]))
        V = (jnp.where(even, B[1], B[0]), jnp.where(even, N[1], N[0]))
        return Pp, U, V, Qq
    def region(self, k, r, depth, keep):
        o = self.order(k, r)
        rows, cols = self.SB, 512
        r0, c0 = k * self.CH + r * self.SB, 0
        for i in range(depth):
            b = o[i][0]
            if i == depth - 1 and not keep: b = 1 - b
            if i < 2:
                rows //= 2; r0 = r0 + b * rows
            else:
                cols //= 2; c0 = c0 + b * cols
        if depth > 2: c0 = pl.multiple_of(c0, 128)
        return pl.ds(pl.multiple_of(r0, 16), rows), pl.ds(c0, cols)
    def rs(self, k, r, i):
        n = self.order(k, r)[i][1]
        buf = (self.r1, self.r2, self.r3, self.r4)[i]
        return self.rc(self.acc.at[self.region(k, r, i + 1, False)], buf.at[k, r], self.rsem.at[0, i, k, r], self.rsem.at[1, i, k, r], n)
    def ag(self, k, r, i):
        n = self.order(k, r)[i][1]
        sl = self.region(k, r, i + 1, True)
        return self.rc(self.out.at[sl], self.out.at[sl], self.asem.at[0, i, k, r], self.asem.at[1, i, k, r], n)
    def small_copy(self, i):
        dev = (self.dp, 1 - self.t) if i == 0 else (self.parts[i - 1], self.t)
        src = self.small if i == 0 else self.sm.at[1, i - 1]
        return pltpu.make_async_remote_copy(src_ref=src, dst_ref=self.sm.at[0, i], send_sem=self.smsem.at[0, i], recv_sem=self.smsem.at[1, i], device_id=dev, device_id_type=MESH)
    def stage(self, s, k):
        if s == 0:
            self.core_copy(k).start()
            self.own_copy(k).start()
        elif s == 1:
            self.core_copy(k).wait_recv()
            sl = pl.ds(pl.multiple_of(k * self.CH, 16), self.CH)
            self.own_copy(k).wait()
            self.acc[sl] = (self.acc[sl].astype(f32) + self.core_buf[k].astype(f32)).astype(bf16)
            for r in range(3): self.rs(k, r, 0).start()
            self.core_copy(k).wait_send()
        elif s <= 5:
            i = s - 2
            buf = (self.r1, self.r2, self.r3, self.r4)[i]
            for r in range(3):
                self.rs(k, r, i).wait_recv()
                sl = self.region(k, r, i + 1, True)
                v = (self.acc[sl].astype(f32) + buf[k, r].astype(f32)).astype(bf16)
                if i < 3:
                    self.acc[sl] = v
                    self.rs(k, r, i + 1).start()
                else:
                    self.out[sl] = v
                    self.ag(k, r, 3).start()
            for r in range(3): self.rs(k, r, i).wait_send()
        else:
            i = 9 - s
            for r in range(3):
                self.ag(k, r, i).wait_recv()
                if i > 0: self.ag(k, r, i - 1).start()
            if i == 0: self.final_copy(k).start()
            for r in range(3): self.ag(k, r, i).wait_send()
    def final_copy(self, k):
        sl = pl.ds(k * self.CH, self.CH)
        return pltpu.make_async_copy(self.out.at[sl], self.out_hbm.at[sl], self.fsem.at[k])
    def small_stage(self, i):
        if i > 0:
            self.small_copy(i - 1).wait_recv()
            own = self.small[...] if i == 1 else self.sm[1, i - 2]
            v = own + self.sm[0, i - 1]
            if i < 5: self.sm[1, i - 1] = v
            else: self.sout[...] = v
        if i < 5: self.small_copy(i).start()
    def iteration_static(self, it):
        if it == 0:
            for k in range(self.K): self.stage(0, k)
        for s in reversed(range(1, self.NSTAGE)):
            k = it - (s - 1) * self.stride
            if 0 <= k < self.K: self.stage(s, k)
        for i in range(6):
            if it == i * self.stride + 1: self.small_stage(i)
    @property
    def iterations(self): return self.K + (self.NSTAGE - 2) * self.stride
    def finish(self):
        def body(k, c):
            self.final_copy(k).wait()
            return c
        lax.fori_loop(0, self.K, body, 0)
        for i in range(5): self.small_copy(i).wait_send()
    @staticmethod
    def scratch(K, S):
        SB = ROWS // K // 3
        D = pltpu.SemaphoreType.DMA
        return [pltpu.VMEM((K, 3 * SB, 512), bf16), pltpu.VMEM((ROWS, 512), bf16),
            pltpu.VMEM((K, 3, SB // 2, 512), bf16), pltpu.VMEM((K, 3, SB // 4, 512), bf16),
            pltpu.VMEM((K, 3, SB // 4, 256), bf16), pltpu.VMEM((K, 3, SB // 4, 128), bf16),
            pltpu.VMEM((ROWS, 512), bf16), pltpu.VMEM((2, 5, S, 512), f32),
            D((3, K)), D((2, 4, K, 3)), D((2, 4, K, 3)), D((2, 5)), D((K,))]


def gather_kernel(
    x_ref, wq_ref, wk_ref, wv_ref, bq_ref, bv_ref, bi_ref, bo_ref, g1_ref, s1_ref, bd_ref, g2_ref, s2_ref, wo_ref, wi_ref, wd_ref,
    q_ref, k_ref, v_ref, vec_ref, wqkv_out, wo_out, wi_out, wd_out, bias_out,
    wqkv, wo, wi, wd, bias, near, sent, came,
):
    step = pl.program_id(0)
    dp, t = lax.axis_index("dp"), lax.axis_index("tensor")

    def pair(i, src, dst):
        return pltpu.make_async_remote_copy(
            src_ref=src, dst_ref=dst, send_sem=sent.at[i], recv_sem=came.at[i],
            device_id=(dp, 1 - t), device_id_type=MESH,
        )

    first = [
        pair(0, wq_ref, wqkv.at[t, 0]), pair(1, wk_ref, wqkv.at[t, 1]), pair(2, wv_ref, wqkv.at[t, 2]),
        pair(3, bias.at[t], bias.at[t]),
    ]
    later = [pair(4, wo.at[t], wo.at[t]), pair(5, wi.at[t], wi.at[t]), pair(6, wd.at[t], wd.at[t])]
    own = [pltpu.make_async_copy(a, b.at[t], near.at[i]) for i, (a, b) in enumerate(((wo_ref, wo), (wi_ref, wi), (wd_ref, wd)))]
    keep = [pltpu.make_async_copy(wqkv, wqkv_out, near.at[3]), pltpu.make_async_copy(bias, bias_out, near.at[4])]
    keep_later = [pltpu.make_async_copy(a, b, near.at[5 + i]) for i, (a, b) in enumerate(((wo, wo_out), (wi, wi_out), (wd, wd_out)))]

    @pl.when(step == 0)
    def _():
        barrier = pltpu.get_barrier_semaphore()
        pl.semaphore_signal(barrier, inc=1, device_id=(dp, 1 - t), device_id_type=MESH)
        bias[t, 0:1] = bq_ref[...].astype(f32).reshape(1, 256)
        bias[t, 1:2] = bv_ref[...].astype(f32).reshape(1, 256)
        for i in range(4):
            bias[t, 2 + i : 3 + i] = bi_ref[pl.ds(256 * i, 256)].astype(f32).reshape(1, 256)
        bias[t, 6:8] = jnp.zeros((2, 256), f32)
        for copy in own:
            copy.start()
        for i, ref in enumerate((bo_ref, g1_ref, s1_ref, bd_ref, g2_ref, s2_ref)):
            vec_ref[i : i + 1] = ref[...].astype(f32).reshape(1, 512)
        vec_ref[6:8] = jnp.zeros((2, 512), f32)
        pl.semaphore_wait(barrier, 1)
        for copy in first:
            copy.start()
        for j, ref in enumerate((wq_ref, wk_ref, wv_ref)):
            wqkv[t, j] = ref[...]
        for copy in first:
            copy.wait_recv()
        for copy in keep:
            copy.start()
        for mine, copy in zip(own, later):
            mine.wait()
            copy.start()

    x = x_ref[...]
    for h in range(2):
        cols = slice(256 * h, 256 * h + 256)
        q_ref[:, cols] = ((product(x, wqkv[h, 0]) + bias[h, 0:1]).astype(bf16).astype(f32) * SCALE).astype(bf16)
        k_ref[:, cols] = product(x, wqkv[h, 1]).astype(bf16)
        v_ref[:, cols] = (product(x, wqkv[h, 2]) + bias[h, 1:2]).astype(bf16)

    @pl.when(step == pl.num_programs(0) // 2)
    def _():
        for copy, out in zip(later, keep_later):
            copy.wait_recv()
            out.start()

    @pl.when(step == pl.num_programs(0) - 1)
    def _():
        for copy in first:
            copy.wait_send()
        for copy in later:
            copy.wait_send()
        for copy in keep + keep_later:
            copy.wait()


def gather(states, wq, wk, wv, bq, bv, bi, vectors, wo, wi, wd):
    rows = states.shape[0]
    block = rows // 4
    whole = lambda a: pl.BlockSpec(a.shape, lambda i: (0,) * a.ndim)
    tile = pl.BlockSpec((block, 512), lambda i: (i, 0))
    hbm, vm = pl.BlockSpec(memory_space=pl.ANY), pl.BlockSpec(memory_space=pltpu.VMEM)
    D = pltpu.SemaphoreType.DMA
    S = jax.ShapeDtypeStruct
    return pl.pallas_call(
        gather_kernel,
        grid=(rows // block,),
        in_specs=[tile, whole(wq), whole(wk), whole(wv)] + [vm] * 9 + [hbm, hbm, hbm],
        out_specs=[tile, tile, tile, vm, hbm, hbm, hbm, hbm, hbm],
        out_shape=[S((rows, 512), bf16)] * 3 + [
            S((8, 512), f32),
            S((2, 3, 512, 256), bf16), S((2, 256, 512), bf16), S((2, 512, 1024), bf16), S((2, 1024, 512), bf16), S((2, 8, 256), f32),
        ],
        scratch_shapes=[
            pltpu.VMEM((2, 3, 512, 256), bf16), pltpu.VMEM((2, 256, 512), bf16), pltpu.VMEM((2, 512, 1024), bf16),
            pltpu.VMEM((2, 1024, 512), bf16), pltpu.VMEM((2, 8, 256), f32), D((8,)), D((7,)), D((7,)),
        ],
        compiler_params=pltpu.CompilerParams(collective_id=1, has_side_effects=True, vmem_limit_bytes=60 << 20),
        name="gather",
    )(states, wq, wk, wv, bq, bv, bi, *vectors, wo, wi, wd)


def normal_cdf(h):
    return 0.5 + 0.5 * lax.erf(h * 0.7071067811865476)


def inverse(a):
    return pltpu.reciprocal(a, approx=True)


def row_mean(a):
    return jnp.sum(a, axis=-1, keepdims=True) * (1.0 / 512)


WINDOW = 32
UNROLL = 4
FRONT = 8


def live_kernel(
    len_ref, start_ref, end_ref,
    x_hbm, cot_hbm, q_hbm, k_hbm, v_hbm, wqkv_hbm, wo_hbm, wi_hbm, wd_hbm, bias_ref, vec_ref,
    g_out, dk_out, dv_out, dx_out, small_out,
    x_all, cot_all, q_all, k_all, v_all, wq, wo, wi, wd, context, inputs, upstream, first, dv_all, acc_k, acc_v,
    acc_d, acc_i, acc_o, gelu_grad, act, stage, apart, win_chain, win_pos, win_dst, chain_win, in_sems, w_sems, out_sems, dx_sems,
):
    chains = len_ref.shape[0] // 2
    t = lax.axis_index("tensor")
    W, R, U = WINDOW, FFN_BLOCK, UNROLL
    rows_all = chains * SEQ
    dk_all = cot_all
    spread = gelu_grad

    def chain_loads(c):
        rows = pl.ds(c * SEQ, SEQ)
        return [
            pltpu.make_async_copy(a.at[rows], b.at[rows], in_sems.at[i, c])
            for i, (a, b) in enumerate(((q_hbm, q_all), (k_hbm, k_all), (v_hbm, v_all), (cot_hbm, cot_all), (x_hbm, x_all)))
        ]

    loads = [
        pltpu.make_async_copy(a, b, w_sems.at[i])
        for i, (a, b) in enumerate((
            (wo_hbm, wo), (wi_hbm, wi), (wd_hbm, wd), (wqkv_hbm.at[0, 0], wq.at[0]), (wqkv_hbm.at[1, 0], wq.at[1]),
        ))
    ]

    def start_loads(c, carry):
        for copy in chain_loads(c):
            copy.start()
        return carry

    lax.fori_loop(0, chains, start_loads, 0)
    for copy in loads:
        copy.start()

    def list_chain(c, carry):
        at, offset = carry
        start = start_ref[t * chains + c]
        end = jnp.minimum(end_ref[t * chains + c], len_ref[t * chains + c])
        r16 = (start // 16) * 16
        r8 = (start // 8) * 8
        count = jnp.maximum((end - r16 + W - 1) // W, 1)
        chain_win[c] = at

        def put(i, carry):
            win_chain[at + i] = c
            win_pos[at + i] = r16 + W * i
            win_dst[at + i] = offset + r16 - r8 + W * i
            return carry

        lax.fori_loop(0, count, put, 0)
        return at + count, offset + jnp.maximum(((end + 7) // 8) * 8 - r8, 0)

    n_win, n_end = lax.fori_loop(0, chains, list_chain, (0, FRONT))
    chain_win[chains] = n_win
    trash = context.shape[0] - W
    for extra in range(U - 1):
        win_chain[n_win + extra] = chains - 1
        win_pos[n_win + extra] = SEQ
        win_dst[n_win + extra] = trash
    n = n_end - FRONT

    acc_d[...] = jnp.zeros_like(acc_d)
    acc_i[...] = jnp.zeros_like(acc_i)
    acc_o[...] = jnp.zeros_like(acc_o)
    acc_k[...] = jnp.zeros_like(acc_k)
    acc_v[...] = jnp.zeros_like(acc_v)
    small_out[...] = jnp.zeros_like(small_out)
    for ref in (context, upstream, first):
        ref[pl.ds(trash, W)] = jnp.zeros((W, 512), f32)
    for ref in (x_all, cot_all, q_all):
        ref[pl.ds(rows_all, W)] = jnp.zeros((W, 512), bf16)

    lane_head = lax.broadcasted_iota(jnp.int32, (W, 256), 1) // HEAD_DIM
    own = lax.broadcasted_iota(jnp.int32, (4 * W, 256), 1) // HEAD_DIM == lax.broadcasted_iota(jnp.int32, (4 * W, 256), 0) // W
    apart[...] = jnp.where(own, 1.0, 0.0).astype(bf16)
    key_row = lax.broadcasted_iota(jnp.int32, (SEQ, 4 * W), 0)
    row_id = lax.broadcasted_iota(jnp.int32, (W, 512), 0)

    def heads_apart(rows):
        return jnp.concatenate([rows] * 4, axis=0) * apart[...]

    def heads_together(full):
        out = full[3 * W :]
        for h in (2, 1, 0):
            out = jnp.where(lane_head == h, full[h * W : (h + 1) * W], out)
        return out

    def window(i):
        c = win_chain[i]
        pos = win_pos[i]
        start = start_ref[t * chains + c]
        length = len_ref[t * chains + c]
        end = jnp.minimum(end_ref[t * chains + c], length)
        src = pl.ds(pl.multiple_of(c * SEQ + pos, 16), W)
        dst = pl.multiple_of(win_dst[i], 8)
        keys = pl.ds(pl.multiple_of(c * SEQ, 32), SEQ)
        live = (row_id + pos >= start) & (row_id + pos < end)
        whole = pos + 8 > start
        return c, pos, length, src, dst, keys, live, whole

    def put_rows(ref, dst, whole, rows):
        head = pl.ds(dst, 8)
        ref[head] = jnp.where(whole, rows[:8], ref[head])
        ref[pl.ds(pl.multiple_of(dst + 8, 8), W - 8)] = rows[8:]

    def softmax(scores, length):
        scores = jnp.where(key_row < length, scores, -1e9)
        e = jnp.exp(scores - jnp.max(scores, axis=0, keepdims=True))
        return e * inverse(jnp.sum(e, axis=0, keepdims=True))

    def forward(i, waited):
        last = win_chain[U * i + U - 1]

        def wait_chain(c, carry):
            for copy in chain_loads(c):
                copy.wait()
            return carry

        lax.fori_loop(waited, last + 1, wait_chain, 0)
        wins = [window(U * i + u) for u in range(U)]
        streams = [(w, slice(256 * g, 256 * g + 256)) for w in wins for g in range(2)]
        qs = [heads_apart(q_all[w[3], cols]) for w, cols in streams]
        scores = [product_right(k_all[w[5], cols], q) for (w, cols), q in zip(streams, qs)]
        probs = [softmax(s, w[2]).astype(bf16) for (w, _), s in zip(streams, scores)]
        outs = [product_left(p, v_all[w[5], cols]) for (w, cols), p in zip(streams, probs)]
        outs = [heads_together(o) for o in outs]
        for u, (c, pos, length, src, dst, keys, live, whole) in enumerate(wins):
            put_rows(context, dst, whole, jnp.concatenate(outs[2 * u : 2 * u + 2], axis=1))
            put_rows(inputs, dst, whole, x_all[src].astype(f32))
            put_rows(upstream, dst, whole, jnp.where(live, cot_all[src].astype(f32), 0.0))
        return last + 1

    steps = (n_win + U - 1) // U
    waited = lax.fori_loop(0, steps, forward, 0)

    tail = pl.ds(pl.multiple_of(n_end, 8), R)
    for ref in (context, inputs, upstream):
        ref[tail] = jnp.zeros((R, 512), f32)
    for copy in loads:
        copy.wait()
    vec = vec_ref[...]
    bo, g1, s1, bd, g2, s2 = (vec[i : i + 1] for i in range(6))
    blocks = (n + R - 1) // R

    def feed_forward(R, start):
        rows = pl.ds(pl.multiple_of(FRONT + start, 8), R)
        ctx = context[rows].astype(bf16)
        attended = product(ctx[:, :256], wo[0]) + product(ctx[:, 256:], wo[1]) + bo
        s = inputs[rows] + attended
        center = s - row_mean(s)
        rstd1 = lax.rsqrt(row_mean(center * center) + EPSILON)
        hat1 = center * rstd1
        normed = hat1 * g1 + s1
        low = normed.astype(bf16)
        branch = jnp.zeros((R, 512), f32) + bd
        place = [(j // 2, 512 * (j % 2)) for j in range(4)]

        def up_part(j):
            h, o = place[j]
            bi = jnp.concatenate([bias_ref[h, 2 + o // 256 : 3 + o // 256], bias_ref[h, 3 + o // 256 : 4 + o // 256]], axis=1)
            return product(low, wi[h, :, o : o + 512]) + bi

        ahead = up_part(0)
        for j in range(4):
            h, o = place[j]
            hid, ahead = ahead, up_part(j + 1) if j < 3 else None
            cdf = normal_cdf(hid)
            a = (hid * cdf).astype(bf16)
            gelu_grad[j, 0:R] = cdf + hid * (0.3989422804014327 * jnp.exp(-0.5 * hid * hid))
            act[j, 0:R] = a
            branch = branch + product(a, wd[h, o : o + 512])
        s = normed + branch
        center = s - row_mean(s)
        rstd2 = lax.rsqrt(row_mean(center * center) + EPSILON)
        hat2 = center * rstd2
        up = upstream[rows]
        gy = up * g2
        grad = rstd2 * (gy - row_mean(gy) - hat2 * row_mean(gy * hat2))
        gb = grad.astype(bf16)
        gn = grad
        back_part = lambda j: product_right(gb, wd[place[j][0], place[j][1] : place[j][1] + 512])
        ahead = back_part(0)
        for j in range(4):
            h, o = place[j]
            ga, ahead = ahead, back_part(j + 1) if j < 3 else None
            acc_d[h, o : o + 512] += product_left(act[j, 0:R], gb)
            gh = (ga * gelu_grad[j, 0:R]).astype(bf16)
            gn = gn + product_right(gh, wi[h, :, o : o + 512])
            acc_i[j] += product_left(low, gh)
            small_out[8 + j : 9 + j] += jnp.sum(gh.astype(f32), axis=0, keepdims=True)
        small_out[1:2] += jnp.sum(gn * hat1, axis=0, keepdims=True)
        small_out[2:3] += jnp.sum(gn, axis=0, keepdims=True)
        small_out[3:4] += jnp.sum(gb.astype(f32), axis=0, keepdims=True)
        small_out[4:5] += jnp.sum(up * hat2, axis=0, keepdims=True)
        small_out[5:6] += jnp.sum(up, axis=0, keepdims=True)
        gy = gn * g1
        grad = rstd1 * (gy - row_mean(gy) - hat1 * row_mean(gy * hat1))
        first[rows] = grad
        ga = grad.astype(bf16)
        small_out[0:1] += jnp.sum(ga.astype(f32), axis=0, keepdims=True)
        acc_o[...] += product_left(ctx, ga)
        upstream[rows] = jnp.concatenate([product_right(ga, wo[0]), product_right(ga, wo[1])], axis=1)

    def whole_block(b, carry):
        feed_forward(R, b * R)
        return carry

    wholes = (n + R // 2 - 1) // R
    lax.fori_loop(0, wholes, whole_block, 0)

    @pl.when(wholes < blocks)
    def _half_block():
        feed_forward(R // 2, wholes * R)

    def out_copy(h, part):
        rows = pl.ds(0, 2048) if part == 0 else pl.ds(2048, 1024)
        return pltpu.make_async_copy(stage.at[h, rows], g_out.at[h, rows], out_sems.at[2 * part + h])

    for h in range(2):
        stage[h, 0:1024] = acc_d[h].astype(bf16)
        stage[h, 1024:1536] = acc_i[2 * h].astype(bf16)
        stage[h, 1536:2048] = acc_i[2 * h + 1].astype(bf16)
        out_copy(h, 0).start()
        stage[h, 2560:2816, 256:512] = acc_o[256 * h : 256 * h + 256, 0:256].astype(bf16)
        stage[h, 2816:3072, 256:512] = acc_o[256 * h : 256 * h + 256, 256:512].astype(bf16)

    def backward(i, carry):
        wins = [window(U * i + u) for u in range(U)]
        streams = [(w, slice(256 * g, 256 * g + 256)) for w in wins for g in range(2)]
        gcs = [jnp.where(w[6], upstream[pl.ds(w[4], W)], 0.0).astype(bf16) for w in wins]
        qs = [heads_apart(q_all[w[3], cols]) for w, cols in streams]
        gs = [heads_apart(gcs[s // 2][:, cols]) for s, (_, cols) in enumerate(streams)]
        scores = [product_right(k_all[w[5], cols], q) for (w, cols), q in zip(streams, qs)]
        gps = [product_right(v_all[w[5], cols], g) for (w, cols), g in zip(streams, gs)]
        probs = [softmax(s, w[2]) for (w, _), s in zip(streams, scores)]
        dss = [(p * (gp - jnp.sum(p * gp, axis=0, keepdims=True))).astype(bf16) for p, gp in zip(probs, gps)]
        dvs = [product(p.astype(bf16), g) for p, g in zip(probs, gs)]
        dks = [product(ds, q) for ds, q in zip(dss, qs)]
        dqs = [product_left(ds, k_all[w[5], cols]) for (w, cols), ds in zip(streams, dss)]
        for u, w in enumerate(wins):
            same = jnp.where((i + u > 0) & (win_chain[jnp.maximum(U * i + u - 1, 0)] == w[0]), 1.0, 0.0)
            dk = acc_k[...] * same + jnp.concatenate(dks[2 * u : 2 * u + 2], axis=1)
            dv = acc_v[...] * same + jnp.concatenate(dvs[2 * u : 2 * u + 2], axis=1)
            acc_k[...] = dk
            acc_v[...] = dv
            dk_all[w[5]] = dk.astype(bf16)
            dv_all[w[5]] = dv.astype(bf16)
        outs = [heads_together(dq) * SCALE for dq in dqs]
        for u, w in enumerate(wins):
            put_rows(context, w[4], w[7], jnp.concatenate(outs[2 * u : 2 * u + 2], axis=1))
        return carry

    lax.fori_loop(0, steps, backward, 0)
    keep = [
        pltpu.make_async_copy(dk_all.at[pl.ds(0, rows_all)], dk_out, out_sems.at[4]),
        pltpu.make_async_copy(dv_all, dv_out, out_sems.at[5]),
    ]
    for copy in keep:
        copy.start()
    context[tail] = jnp.zeros((R, 512), f32)
    acc_o[...] = jnp.zeros_like(acc_o)

    def query_weight(b, carry):
        rows = pl.ds(pl.multiple_of(FRONT + b * R, 8), R)
        dq = context[rows].astype(bf16)
        acc_o[...] += product_left(inputs[rows].astype(bf16), dq)
        small_out[6:7] += jnp.sum(dq.astype(f32), axis=0, keepdims=True)
        first[rows] = first[rows] + (product_right(dq[:, :256], wq[0]) + product_right(dq[:, 256:], wq[1]))
        return carry

    lax.fori_loop(0, blocks, query_weight, 0)
    def chain_out(c):
        return pltpu.make_async_copy(spread.at[c % 4, pl.ds(0, SEQ)], dx_out.at[pl.ds(c * SEQ, SEQ)], dx_sems.at[c % 4])

    def scatter(c, carry):
        slot = c % 4

        @pl.when(c >= 4)
        def _():
            chain_out(c - 4).wait()

        spread[slot, 0 : SEQ + W] = jnp.zeros((SEQ + W, 512), f32)

        def put(j, carry):
            _, pos, _, _, dst, _, live, _ = window(j)
            spread[slot, pl.ds(pl.multiple_of(pos, 16), W)] = jnp.where(live, first[pl.ds(dst, W)], 0.0)
            return carry

        lax.fori_loop(chain_win[c], chain_win[c + 1], put, 0)
        chain_out(c).start()
        return carry

    lax.fori_loop(0, chains, scatter, 0)
    small_out[7:8] = jnp.sum(dv_all[...].astype(f32), axis=0, keepdims=True)
    part = 4 * SEQ if chains % 4 == 0 else rows_all // 2

    def key_value_weight(b, carry):
        rows = pl.ds(pl.multiple_of(b * part, 32), part)
        x = x_all[rows]
        dk = product_left(x, dk_all[rows])
        dv = product_left(x, dv_all[rows])
        keep = jnp.where(b > 0, 1.0, 0.0)
        acc_d[0, 0:512] = acc_d[0, 0:512] * keep + dk
        acc_d[1, 0:512] = acc_d[1, 0:512] * keep + dv
        return carry

    lax.fori_loop(0, rows_all // part, key_value_weight, 0)
    dk, dv = acc_d[0, 0:512], acc_d[1, 0:512]
    for h in range(2):
        cols = slice(256 * h, 256 * h + 256)
        stage[h, 2048:2560, 0:256] = acc_o[:, cols].astype(bf16)
        stage[h, 2048:2560, 256:512] = dk[:, cols].astype(bf16)
        stage[h, 2560:3072, 0:256] = dv[:, cols].astype(bf16)
        out_copy(h, 1).start()

    for slot in range(4):
        chain_out(chains - 4 + slot).wait()
    for copy in keep:
        copy.wait()
    for h in range(2):
        out_copy(h, 0).wait()
        out_copy(h, 1).wait()


def live_rows(lengths, starts, ends, states, cotangent, q, k, v, wqkv, wo, wi, wd, bias, vec):
    rows = states.shape[0]
    chains = rows // SEQ
    R, W = FFN_BLOCK, WINDOW
    C = -(-(FRONT + rows + R + W) // 8) * 8
    windows = SEQ // WINDOW * chains + UNROLL
    hbm, vm, sm = (pl.BlockSpec(memory_space=s) for s in (pl.ANY, pltpu.VMEM, pltpu.SMEM))
    S, V, D, M = jax.ShapeDtypeStruct, pltpu.VMEM, pltpu.SemaphoreType.DMA, pltpu.SMEM
    return pl.pallas_call(
        live_kernel,
        in_specs=[sm] * 3 + [hbm] * 9 + [vm, vm],
        out_specs=[hbm] * 4 + [vm],
        scratch_shapes=[
            V((rows + W, 512), bf16), V((rows + W, 512), bf16), V((rows + W, 512), bf16), V((rows, 512), bf16), V((rows, 512), bf16),
            V((2, 512, 256), bf16), V((2, 256, 512), bf16), V((2, 512, 1024), bf16), V((2, 1024, 512), bf16),
            V((C, 512), f32), V((C, 512), f32), V((C, 512), f32), V((C, 512), f32),
            V((rows, 512), bf16), V((SEQ, 512), f32), V((SEQ, 512), f32),
            V((2, 1024, 512), f32), V((4, 512, 512), f32), V((512, 512), f32),
            V((4, R, 512), f32), V((4, R, 512), bf16), V((2, 3072, 512), bf16), V((4 * W, 256), bf16),
            M((windows,), jnp.int32), M((windows,), jnp.int32), M((windows,), jnp.int32), M((chains + 1,), jnp.int32),
            D((5, chains)), D((5,)), D((6,)), D((4,)),
        ],
        out_shape=[S((2, ROWS, 512), bf16), S((rows, 512), bf16), S((rows, 512), bf16), S((rows, 512), f32), S((16, 512), f32)],
        compiler_params=pltpu.CompilerParams(vmem_limit_bytes=62 << 20),
        name="live_rows",
    )(lengths, starts, ends, states, cotangent, q, k, v, wqkv, wo, wi, wd, bias, vec)


def rest_kernel(
    STEPS, SLOTS, K, STRIDE,
    g, small, x_ref, q_ref, k_ref, v_ref, len_ref, dk_ref, dv_ref, gf_ref, wqkv_hbm, wo_hbm, wi_hbm, wd_hbm, bias_ref, vec_ref,
    out, sout, y_ref, dx_ref, wqkv, wo, wi, wd, w_sems, *bufs,
):
    step = pl.program_id(0)
    comm = Comm(K, g, small, out, sout, bufs, STRIDE)
    slots = SLOTS
    loads = [
        pltpu.make_async_copy(a, b, w_sems.at[i])
        for i, (a, b) in enumerate(((wo_hbm, wo), (wi_hbm, wi), (wd_hbm, wd), (wqkv_hbm, wqkv)))
    ]

    spots = [(at, i) for at in range(STEPS) for i in range(slots)]

    def slot(i):
        for at in range(STEPS):
            mine = [it for it in range(comm.iterations) if spots[it * len(spots) // comm.iterations] == (at, i)]
            if mine:

                @pl.when(step == at)
                def _(mine=mine):
                    for it in mine:
                        comm.iteration_static(it)

    @pl.when(step == 0)
    def _():
        for copy in loads:
            copy.start()
        comm.barrier()

    vec = vec_ref[...]
    bo, g1, s1, bd, g2, s2 = (vec[i : i + 1] for i in range(6))
    low_lane = lax.broadcasted_iota(jnp.int32, (SEQ, 128), 1) < HEAD_DIM
    key_row = lax.broadcasted_iota(jnp.int32, (SEQ, SEQ), 0)
    ctx = []
    for c in range(2):
        rows = slice(c * SEQ, c * SEQ + SEQ)
        length = len_ref[comm.t * (2 * pl.num_programs(0)) + 2 * step + c]
        slot(c)
        parts = []
        for half in range(2):
            streams = [(slice(128 * pair, 128 * pair + 128), h) for pair in (2 * half, 2 * half + 1) for h in range(2)]
            keys = [jnp.where(low_lane == (h == 0), k_ref[rows, cols], jnp.zeros((), bf16)) for cols, h in streams]
            scores = [product_right(key, q_ref[rows, cols]) for (cols, _), key in zip(streams, keys)]
            scores = [jnp.where(key_row < length, s, -1e9) for s in scores]
            exps = [jnp.exp(s - jnp.max(s, axis=0, keepdims=True)) for s in scores]
            probs = [(e * inverse(jnp.sum(e, axis=0, keepdims=True))).astype(bf16) for e in exps]
            outs = [product_left(p, v_ref[rows, cols]) for (cols, _), p in zip(streams, probs)]
            parts += [jnp.where(low_lane, outs[0], outs[1]), jnp.where(low_lane, outs[2], outs[3])]
        ctx.append(jnp.concatenate(parts, axis=1).astype(bf16))
    ctx = jnp.concatenate(ctx, axis=0)
    slot(2)

    @pl.when(step == 0)
    def _():
        for copy in loads:
            copy.wait()

    s = x_ref[...].astype(f32) + (product(ctx[:, :256], wo[0]) + product(ctx[:, 256:], wo[1]) + bo)
    center = s - row_mean(s)
    normed = center * lax.rsqrt(row_mean(center * center) + EPSILON) * g1 + s1
    low = normed.astype(bf16)
    branch = bd

    def up_part(j):
        h, o = j // 2, 512 * (j % 2)
        bi = jnp.concatenate([bias_ref[h, 2 + o // 256 : 3 + o // 256], bias_ref[h, 3 + o // 256 : 4 + o // 256]], axis=1)
        return product(low, wi[h, :, o : o + 512]) + bi

    ahead = up_part(0)
    for j in range(4):
        hid, ahead = ahead, up_part(j + 1) if j < 3 else None
        branch = branch + product((hid * normal_cdf(hid)).astype(bf16), wd[j // 2, 512 * (j % 2) : 512 * (j % 2) + 512])
        if j == 1:
            slot(3)
    s = normed + branch
    center = s - row_mean(s)
    y_ref[...] = (center * lax.rsqrt(row_mean(center * center) + EPSILON) * g2 + s2).astype(bf16)
    slot(4)
    dx = gf_ref[...]
    for h in range(2):
        cols = slice(256 * h, 256 * h + 256)
        for j, ref in ((1, dk_ref), (2, dv_ref)):
            dx = dx + product_right(ref[:, cols], wqkv[h, j])
    dx_ref[...] = dx

    @pl.when(step == pl.num_programs(0) - 1)
    def _():
        comm.finish()


def rest(g, small, states, q, k, v, lens, dk, dv, gf, wqkv, wo, wi, wd, bias, vec):
    rows = states.shape[0]
    block = 2 * SEQ
    K, STRIDE, SLOTS = 8, 2, 4
    tile = pl.BlockSpec((block, 512), lambda i: (i, 0))
    vm, hbm = pl.BlockSpec(memory_space=pltpu.VMEM), pl.BlockSpec(memory_space=pl.ANY)
    S = jax.ShapeDtypeStruct
    return pl.pallas_call(
        functools.partial(rest_kernel, rows // block, SLOTS, K, STRIDE),
        grid=(rows // block,),
        in_specs=[hbm, vm, tile, tile, tile, tile, pl.BlockSpec(memory_space=pltpu.SMEM), tile, tile, tile,
                  hbm, hbm, hbm, hbm, vm, vm],
        out_specs=[hbm, vm, tile, tile],
        out_shape=[S((ROWS, 512), bf16), S(small.shape, f32), S((rows, 512), bf16), S((rows, 512), f32)],
        scratch_shapes=[
            pltpu.VMEM(wqkv.shape, bf16), pltpu.VMEM(wo.shape, bf16), pltpu.VMEM(wi.shape, bf16), pltpu.VMEM(wd.shape, bf16),
            pltpu.SemaphoreType.DMA((4,)),
        ] + Comm.scratch(K, small.shape[0]),
        compiler_params=pltpu.CompilerParams(collective_id=0, has_side_effects=True, vmem_limit_bytes=61 << 20),
        name="rest",
    )(g, small, states, q, k, v, lens, dk, dv, gf, wqkv, wo, wi, wd, bias, vec)


def finish_kernel(
    sums_hbm, small_ref, y_in, dx_in,
    y_ref, dx_ref, dq_ref, dk_ref, dv_ref, do_ref, di_ref, dd_ref, bq_ref, bv_ref, bo_ref, g1_ref, s1_ref, bi_ref, bd_ref, g2_ref, s2_ref,
    sums_ref, dd, di, dqkvo, sems, in_sems,
):
    step = pl.program_id(0)
    t = lax.axis_index("tensor")
    y_ref[...] = y_in[...]
    dx_ref[...] = dx_in[...]
    w = [
        (2, pltpu.make_async_copy(dd, dd_ref, sems.at[0])), (4, pltpu.make_async_copy(di, di_ref, sems.at[1])),
        (5, pltpu.make_async_copy(dqkvo.at[0], dq_ref, sems.at[2])), (5, pltpu.make_async_copy(dqkvo.at[1], dk_ref, sems.at[3])),
        (6, pltpu.make_async_copy(dqkvo.at[2], dv_ref, sems.at[4])),
    ]

    loads = [
        pltpu.make_async_copy(sums_hbm.at[pl.ds(1024 * i, 1024)], sums_ref.at[pl.ds(1024 * i, 1024)], in_sems.at[i]) for i in range(3)
    ]

    def part(rows):
        return sums_ref[rows].astype(f32)

    @pl.when(step == 0)
    def _():
        for copy in loads:
            copy.start()
        pick = lambda i: jnp.where(t == 0, small_ref[i : i + 1, 0:256], small_ref[i : i + 1, 256:512])
        bq_ref[...] = pick(6)
        bv_ref[...] = pick(7)
        bi_ref[...] = jnp.where(
            t == 0, jnp.concatenate([small_ref[8:9], small_ref[9:10]], axis=1), jnp.concatenate([small_ref[10:11], small_ref[11:12]], axis=1)
        )
        for i, ref in enumerate((bo_ref, g1_ref, s1_ref, bd_ref, g2_ref, s2_ref)):
            ref[...] = small_ref[i : i + 1]

    @pl.when(step == 1)
    def _():
        loads[0].wait()
        dd[...] = part(slice(0, 1024))
        pltpu.make_async_copy(dd, dd_ref, sems.at[0]).start()

    @pl.when(step == 2)
    def _():
        loads[1].wait()
        di[:, 0:512] = part(slice(1024, 1536))
        di[:, 512:1024] = part(slice(1536, 2048))
        pltpu.make_async_copy(di, di_ref, sems.at[1]).start()

    @pl.when(step == 3)
    def _():
        loads[2].wait()
        both = part(slice(2048, 2560))
        dqkvo[0], dqkvo[1] = both[:, :256], both[:, 256:]
        dqkvo[2] = part(slice(2560, 3072))[:, :256]
        do_ref[:, 0:256] = sums_ref[2560:2816, 256:512].astype(f32)
        do_ref[:, 256:512] = sums_ref[2816:3072, 256:512].astype(f32)
        for i, ref in enumerate((dq_ref, dk_ref, dv_ref)):
            pltpu.make_async_copy(dqkvo.at[i], ref, sems.at[2 + i]).start()

    @pl.when(step == pl.num_programs(0) - 1)
    def _():
        for _, copy in w:
            copy.wait()


def finish(sums, small, y, dx):
    rows = y.shape[0]
    block = 2 * SEQ
    tile = pl.BlockSpec((block, 512), lambda i: (i, 0))
    vm, hbm = pl.BlockSpec(memory_space=pltpu.VMEM), pl.BlockSpec(memory_space=pl.ANY)
    S, V = jax.ShapeDtypeStruct, pltpu.VMEM
    line = lambda n: S((1, n), f32)
    return pl.pallas_call(
        finish_kernel,
        grid=(rows // block,),
        in_specs=[hbm, vm, tile, tile],
        out_specs=[tile, tile, hbm, hbm, hbm, vm, hbm, hbm] + [vm] * 9,
        out_shape=[
            S((rows, 512), bf16), S((rows, 512), f32), S((512, 256), f32), S((512, 256), f32), S((512, 256), f32), S((256, 512), f32),
            S((512, 1024), f32), S((1024, 512), f32), line(256), line(256), line(512), line(512), line(512), line(1024), line(512), line(512), line(512),
        ],
        scratch_shapes=[V((3072, 512), bf16), V((1024, 512), f32), V((512, 1024), f32), V((3, 512, 256), f32), pltpu.SemaphoreType.DMA((5,)), pltpu.SemaphoreType.DMA((3,))],
        compiler_params=pltpu.CompilerParams(vmem_limit_bytes=60 << 20),
        name="finish",
    )(sums, small, y, dx)


def whole_chains(
    states, cotangent, lengths, span_starts, span_ends, query_weight, query_bias, key_weight, value_weight, value_bias,
    output_weight, output_bias, first_gain, first_shift, inner_weight, inner_bias, down_weight, down_bias, second_gain, second_shift,
):
    q, k, v, vec, wqkv, wo, wi, wd, bias = gather(
        states, query_weight, key_weight, value_weight, query_bias, value_bias, inner_bias,
        (output_bias, first_gain, first_shift, down_bias, second_gain, second_shift), output_weight, inner_weight, down_weight,
    )
    g, dk, dv, gf, small = live_rows(lengths, span_starts, span_ends, states, cotangent, q, k, v, wqkv, wo, wi, wd, bias, vec)
    summed, small, output, input_grad = rest(g, small, states, q, k, v, lengths, dk, dv, gf, wqkv, wo, wi, wd, bias, vec)
    (
        output, input_grad, query, key, value, out, inner, down, query_b, value_b, out_b, gain1, shift1, inner_b, down_b, gain2, shift2,
    ) = finish(summed, small, output, input_grad)
    flat = lambda a: a.reshape(-1)
    return (
        output, input_grad, query, flat(query_b), key, value, flat(value_b), out, flat(out_b), flat(gain1), flat(shift1),
        inner, flat(inner_b), down, flat(down_b), flat(gain2), flat(shift2),
    )


def local(*arguments):
    rows, hidden = arguments[0].shape[0], arguments[14].shape[1]
    if rows % SEQ == 0 and lax.axis_size("dp") == 16 and lax.axis_size("tensor") == 2:
        return whole_chains(*arguments)
    return general(*arguments)


def solution(mesh):
    placed = (
        P(("dp", "tensor"), None),
        P(("dp", "tensor"), None),
        P("dp"),
        P("dp"),
        P("dp"),
        P(None, "tensor"),
        P("tensor"),
        P(None, "tensor"),
        P(None, "tensor"),
        P("tensor"),
        P("tensor", None),
        P(),
        P(),
        P(),
        P(None, "tensor"),
        P("tensor"),
        P("tensor", None),
        P(),
        P(),
        P(),
    )
    return jax.shard_map(
        local,
        mesh=mesh,
        in_specs=placed,
        out_specs=(
            P(("dp", "tensor"), None),
            P(("dp", "tensor"), None),
            P(None, "tensor"),
            P("tensor"),
            P(None, "tensor"),
            P(None, "tensor"),
            P("tensor"),
            P("tensor", None),
            P(),
            P(),
            P(),
            P(None, "tensor"),
            P("tensor"),
            P("tensor", None),
            P(),
            P(),
            P(),
        ),
        check_vma=False,
    )
```
